32 devices in a mesh: gx: 8 (over z, x), gy: 4 (over y, core).
Axes of the slice: x: 2, y: 2, z: 4, core: 2. Of those that a mesh axis runs over, the one named last changes fastest.
Arguments:
- hidden_in: bfloat16 [2048, 16384], P('gy', 'gx'), may hold values from -200 to 200
- norm_gain: float32 [16384], P('gx'), may hold values from 0.1 to 1.9
- w_query: bfloat16 [16384, 8192], P('gx', 'gy'), may hold values from -24 to 24
- w_key: bfloat16 [16384, 1024], P('gx'), may hold values from -1 to 1
- w_value: bfloat16 [16384, 1024], P('gx'), may hold values from -0.046875 to 0.046875
- w_out: bfloat16 [8192, 16384], P('gy', 'gx'), may hold values from -0.06591797 to 0.06591797
- seg_lengths: int32 [8], replicated, may hold values from 1 to 512, 2048 in all
Outputs:
- update: bfloat16 [2048, 16384], P('gy', 'gx')
The draws below stay inside these ranges and needn't reach their ends.
Inputs may be any that keep to these rules, and one draw needn't show every extreme that they name: `seg_lengths`: the 8 lengths sum to 2048 and the longest is exactly 512.
All inputs are finite; a program needn't handle non-finite values.
Results may differ from the reference program's by a relative error of at most 0.04.
Values may be sent and summed in bfloat16 or wider, within the bound.
No kernel may reach another device: no remote copies, remote signals or barrier semaphores. Data moves between devices by JAX's collectives and lax.ppermute only.
A program may use at most 128 MiB of HBM per device.

```python
import math
import jax
import jax.numpy as jnp
import numpy as np
from jax import lax

D = 16384
H = 64
KVH = 8
HD = 128
TOKENS = 2048
SEGS = 8
SEG_MOST = 512
N_GX = 8
N_GY = 4


def shared_keys(key):
    return jnp.clip(jax.random.normal(key, (D, KVH * HD), jnp.float32), -6.0, 6.0) * D ** (-0.5)


def draw_w_key(key, part):
    shared = shared_keys(key)
    return shared.astype(jnp.bfloat16)


def draw_w_query(key, part):
    key = jax.random.fold_in(key, 23)
    first_key = jax.random.fold_in(key, 0)
    base = jnp.clip(jax.random.normal(first_key, (D, H * HD), jnp.float32), -6.0, 6.0) * D ** (-0.5)
    return base.astype(jnp.bfloat16)


def draw_hidden_in(key, part):
    key = jax.random.fold_in(key, 5)
    col_key, row_key, noise_key = jax.random.split(key, 3)
    column = jnp.arange(D, dtype=jnp.float32) / D
    col_scale = jnp.exp(math.log(10.0) * 0.5 * (column + jax.random.uniform(col_key, (D,), jnp.float32)))
    row_scale = jnp.exp(math.log(10.0) * jax.random.uniform(row_key, (TOKENS, 1), jnp.float32))
    noise = jnp.clip(jax.random.normal(noise_key, (TOKENS, D), jnp.float32), -6.0, 6.0)
    return (0.3 * noise * col_scale[None, :] * row_scale).astype(jnp.bfloat16)


def spiked(array, rng, source, target, shards_of, factor):
    def block_of(dim):
        return (jnp.arange(array.shape[dim]) // (array.shape[dim] // shards_of)).reshape((-1,) + (1,) * (array.ndim - 1 - dim))

    one_side = jax.random.permutation(rng, shards_of)[block_of(target)]
    second = (block_of(target) + shards_of // 2) % shards_of
    return jnp.where((block_of(source) == one_side) | (block_of(source) == second), factor * array, array)


def block_scale(key, dims, pieces, least, high):
    factor_of, own = 1.0, jax.random.fold_in(key, 6)
    for dim, parts in pieces:
        heights = jnp.exp(jax.random.uniform(jax.random.fold_in(own, dim), (parts,), jnp.float32, least / len(pieces), high / len(pieces)))
        factor_of = factor_of * jnp.repeat(heights, dims[dim] // parts).reshape([-1 if axis == dim else 1 for axis in range(len(dims))])
    return factor_of


def split_up(number_of, total, limit, slope):
    loads = [(1 << 20) // math.isqrt(grade ** slope) + 1 for grade in range(2, number_of + 1)]
    surplus, given = total - limit - (number_of - 1), [1] * (number_of - 1)
    while surplus > 0:
        movable = [i for i in range(number_of - 1) if given[i] < limit]
        mass, budget = sum([loads[i] for i in movable]), surplus
        for i in movable:
            extra = min(limit - given[i], max(1, budget * loads[i] // mass), surplus)
            given[i] = given[i] + extra
            surplus = surplus - extra
    return np.array([limit] + given)


def ragged_sizes(rng, count, total, bound, slope):
    if count == 2:
        one = jax.random.randint(rng, (), max(1, total - bound), min(bound, total - 1) + 1)
        return jnp.stack([one, total - one])
    tallies = jnp.asarray(split_up(count, total, bound, slope), jnp.int32)
    twos = (count - 1) // 2
    giver, sink = tallies[1:1 + 2 * twos:2], tallies[2:2 + 2 * twos:2]
    room = jnp.minimum(giver - 1, bound - sink)
    moved = jax.random.randint(jax.random.fold_in(rng, 1), (twos,), 0, 1 << 20) % (room + 1)
    tallies = tallies.at[1:1 + 2 * twos:2].set(giver - moved).at[2:2 + 2 * twos:2].set(sink + moved)
    return tallies[jax.random.permutation(jax.random.fold_in(rng, 2), count)]


def gaussian(stream_key, shape, width, reach, shards=(), held_as=jnp.bfloat16):
    result = jax.random.normal(stream_key, shape, jnp.float32) * width
    if len(shards) > 0:
        result = block_scale(stream_key, shape, shards, -0.22, 0.18) * result
    return jnp.clip(result, min=-reach, max=reach).astype(held_as)


def noise_with(stream_key, shape, width, limit, cuts, heavy, kind=jnp.bfloat16):
    result = width * jax.random.normal(stream_key, shape, jnp.float32)
    if cuts:
        result = result * block_scale(stream_key, shape, cuts, -0.22, 0.18)
    return jnp.clip(spiked(result, jax.random.fold_in(stream_key, 3), *heavy), -limit, limit).astype(kind)


def setup_inputs(seed: int = 0) -> dict:
    splits = jax.random.split(jax.random.key(seed), 8)
    return {
        "hidden_in": draw_hidden_in(jax.random.fold_in(splits[7], 71), 0),
        "norm_gain": jnp.clip(1.0 + 0.18 * jax.random.normal(splits[1], (D,), jnp.float32), 0.1, 1.9),
        "w_query": draw_w_query(jax.random.fold_in(splits[7], 71), 0),
        "w_key": draw_w_key(jax.random.fold_in(splits[7], 71), 0),
        "w_value": gaussian(splits[4], (D, KVH * HD), D ** -0.5, 0.046875, ((0, 8),)),
        "w_out": noise_with(splits[5], (H * HD, D), ((H * HD) ** -0.5), 0.06591797, ((0, 4), (1, 8)), (0, 1, 8, 2.0)),
        "seg_lengths": ragged_sizes(splits[6], SEGS, TOKENS, SEG_MOST, 2).astype(jnp.int32),
    }


ROPE_BASE = 500000.0
EPS = 1e-05

def rotate(values, position, head_size):
    half = head_size // 2
    exponent = jnp.arange(half, dtype=jnp.float32) * (2.0 / head_size)
    frequency = ROPE_BASE ** (-exponent)
    angle = position[:, None, None] * frequency[None, None, :]
    cosine = jnp.cos(angle)
    sine = jnp.sin(angle)
    first = values[..., :half]
    second = values[..., half:]
    return jnp.concatenate([first * cosine - second * sine, second * cosine + first * sine], axis=-1)

def segment_table(seg_lengths, tokens):
    ends = jnp.cumsum(seg_lengths).astype(jnp.int32)
    starts = (ends - seg_lengths).astype(jnp.int32)
    index = jnp.arange(tokens, dtype=jnp.int32)
    member = ((index[:, None] >= starts[None, :]) & (index[:, None] < ends[None, :])).astype(jnp.int32)
    seg_id = lax.optimization_barrier(jnp.sum(member * jnp.arange(seg_lengths.shape[0], dtype=jnp.int32)[None, :], axis=1)).astype(jnp.int32)
    first_index = lax.optimization_barrier(jnp.sum(member * starts[None, :], axis=1)).astype(jnp.int32)
    return (seg_id, (index - first_index).astype(jnp.int32))

def block_sum(left, right, blocks):
    total_rows = left.shape[0]
    block_width = left.shape[1] // blocks
    left_blocks = left.reshape(total_rows, blocks, block_width).transpose(1, 0, 2)
    right_blocks = right.reshape(blocks, block_width, right.shape[1])

    def add_block(total, pair):
        product = jnp.dot(pair[0], pair[1], preferred_element_type=jnp.float32)
        rounded = lax.optimization_barrier(product.astype(jnp.bfloat16))
        return (total + rounded.astype(jnp.float32), None)
    start_total = jnp.zeros((total_rows, right.shape[1]), jnp.float32)
    total, _ = lax.scan(add_block, start_total, (left_blocks, right_blocks))
    return total

def reference(hidden_in, norm_gain, w_query, w_key, w_value, w_out, seg_lengths):
    widened = hidden_in.astype(jnp.float32)
    squares = lax.optimization_barrier(jnp.sum(widened * widened, axis=1))
    scale = lax.rsqrt(squares / D + EPS)
    normed = (widened * scale[:, None] * norm_gain.astype(jnp.float32)[None, :]).astype(jnp.bfloat16)
    query_sum = block_sum(normed, w_query, N_GX)
    key_raw = block_sum(normed, w_key, N_GX).astype(jnp.bfloat16)
    value_raw = block_sum(normed, w_value, N_GX).astype(jnp.bfloat16)
    seg_id, position = segment_table(seg_lengths, TOKENS)
    position_f = position.astype(jnp.float32)
    queries = rotate(query_sum.reshape(TOKENS, H, HD), position_f, HD).astype(jnp.bfloat16)
    keys = rotate(key_raw.astype(jnp.float32).reshape(TOKENS, KVH, HD), position_f, HD).astype(jnp.bfloat16)
    group = H // KVH
    query_groups = queries.reshape(TOKENS, KVH, group, HD).transpose(1, 2, 0, 3)
    key_groups = keys.transpose(1, 0, 2)
    value_groups = value_raw.reshape(TOKENS, KVH, HD).transpose(1, 0, 2)
    index = jnp.arange(TOKENS, dtype=jnp.int32)
    allowed = (seg_id[:, None] == seg_id[None, :]) & (index[None, :] <= index[:, None])

    def one_group(operands):
        query_part, key_part, value_part = operands
        scores = jnp.einsum('gtd,sd->gts', query_part.astype(jnp.float32), key_part.astype(jnp.float32)) * HD ** (-0.5)
        scores = jnp.where(allowed[None], scores, -jnp.inf)
        largest = lax.optimization_barrier(jnp.max(scores, axis=-1, keepdims=True))
        expo = jnp.exp(scores - largest)
        denominator = lax.optimization_barrier(jnp.sum(expo, axis=-1, keepdims=True))
        weights = expo.astype(jnp.bfloat16)
        summed = jnp.einsum('gts,sd->gtd', weights.astype(jnp.float32), value_part.astype(jnp.float32))
        return (summed / denominator).astype(jnp.bfloat16)
    attended = lax.map(one_group, (query_groups, key_groups, value_groups))
    attended = attended.transpose(2, 0, 1, 3).reshape(TOKENS, H * HD)
    return block_sum(attended, w_out, N_GY).astype(jnp.bfloat16)
```

```python
import functools
import math

import jax
import jax.numpy as jnp
from jax import lax
from jax.experimental import pallas as pl
from jax.experimental.pallas import tpu as pltpu
from jax.sharding import PartitionSpec as P

H = 64
KVH = 8
HD = 128


ROPE_BASE = 500000.0
EPS = 1e-05
SEG_MOST = 512


def rotate(values, position, head_size):
    half = head_size // 2
    exponent = jnp.arange(half, dtype=jnp.float32) * (2.0 / head_size)
    frequency = ROPE_BASE ** (-exponent)
    angle = position[:, None, None] * frequency[None, None, :]
    cosine = jnp.cos(angle)
    sine = jnp.sin(angle)
    first = values[..., :half]
    second = values[..., half:]
    return jnp.concatenate(
        [first * cosine - second * sine, second * cosine + first * sine], axis=-1
    )


def segment_table(seg_lengths, tokens):
    ends = jnp.cumsum(seg_lengths)
    starts = ends - seg_lengths
    index = jnp.arange(tokens, dtype=jnp.int32)
    member = ((index[:, None] >= starts[None, :]) & (index[:, None] < ends[None, :])).astype(
        jnp.int32
    )
    seg_id = jnp.sum(member * jnp.arange(seg_lengths.shape[0], dtype=jnp.int32)[None, :], axis=1)
    first_index = jnp.sum(member * starts[None, :], axis=1)
    return (seg_id, index - first_index)


def normalize(block, gain, squares, model_width):
    widened = block.astype(jnp.float32)
    scale = lax.rsqrt(squares / model_width + EPS)
    return (widened * scale[:, None] * gain[None, :]).astype(jnp.bfloat16)


def shards_any(hidden_in, norm_gain, w_query, w_key, w_value, w_out, seg_lengths):
    rows_own, width = hidden_in.shape
    model_width = width * lax.axis_size("gx")
    tokens = rows_own * lax.axis_size("gy")
    query_rows = tokens // lax.axis_size("gx")
    widened = hidden_in.astype(jnp.float32)
    squares = lax.psum(jnp.sum(widened * widened, axis=1), "gx")
    source = normalize(hidden_in, norm_gain, squares, model_width)
    gathered = lax.all_gather(source, "gy", axis=0, tiled=True)
    query_cols = w_query.shape[1]
    heads_local = query_cols // HD
    group = H // KVH
    kv_local = max(1, heads_local // group)
    pair_cols = kv_local * HD
    first_head = lax.axis_index("gy") * heads_local // group
    key_own = lax.dynamic_slice_in_dim(w_key, first_head * HD, pair_cols, 1)
    value_own = lax.dynamic_slice_in_dim(w_value, first_head * HD, pair_cols, 1)
    seg_id, position = segment_table(seg_lengths, tokens)
    here = lax.axis_index("gx") * query_rows
    query_seg = lax.dynamic_slice_in_dim(seg_id, here, query_rows)
    query_pos = lax.dynamic_slice_in_dim(position, here, query_rows)
    query_index = here + jnp.arange(query_rows, dtype=jnp.int32)
    query_sum = lax.psum_scatter(
        jnp.dot(gathered, w_query, preferred_element_type=jnp.float32).astype(jnp.bfloat16),
        "gx",
        scatter_dimension=0,
        tiled=True,
    ).astype(jnp.float32)
    pair_part = jnp.concatenate(
        [
            jnp.dot(gathered, key_own, preferred_element_type=jnp.float32),
            jnp.dot(gathered, value_own, preferred_element_type=jnp.float32),
        ],
        axis=1,
    )
    pair_sum = lax.psum(pair_part.astype(jnp.bfloat16), "gx").astype(jnp.float32)
    key_raw = pair_sum[:, :pair_cols].astype(jnp.bfloat16)
    value_raw = pair_sum[:, pair_cols:].astype(jnp.bfloat16)
    group_local = heads_local // kv_local
    queries = rotate(
        query_sum.reshape(query_rows, heads_local, HD), query_pos.astype(jnp.float32), HD
    ).astype(jnp.bfloat16)
    queries = queries.reshape(query_rows, kv_local, group_local, HD)
    key_count = key_raw.shape[0]
    keys = rotate(
        key_raw.astype(jnp.float32).reshape(key_count, kv_local, HD),
        position.astype(jnp.float32),
        HD,
    )
    keys = keys.astype(jnp.bfloat16).reshape(key_count, pair_cols)
    score_scale = 1.0 / math.sqrt(HD)
    running = jnp.full((kv_local, group_local, query_rows), -1e30, jnp.float32)
    count = keys.shape[0]
    key_index = jnp.arange(count, dtype=jnp.int32)
    allowed = (query_seg[:, None] == seg_id[None, :]) & (key_index[None, :] <= query_index[:, None])
    key_heads = keys.reshape(count, kv_local, HD)
    value_heads = value_raw.reshape(count, kv_local, HD)
    scores = (
        jnp.einsum("rkgd,nkd->kgrn", queries, key_heads, preferred_element_type=jnp.float32)
        * score_scale
    )
    scores = jnp.where(allowed[None, None], scores, -1e30)
    newest = jnp.maximum(running, jnp.max(scores, axis=-1))
    weights = jnp.where(allowed[None, None], jnp.exp(scores - newest[..., None]), 0.0)
    denominator = jnp.sum(weights, axis=-1)
    added = jnp.einsum(
        "kgrn,nkd->rkgd",
        weights.astype(jnp.bfloat16),
        value_heads,
        preferred_element_type=jnp.float32,
    )
    accum = added
    running, denominator, accum = (newest, denominator, accum)
    attended = (
        (accum / denominator.transpose(2, 0, 1)[..., None])
        .reshape(query_rows, query_cols)
        .astype(jnp.bfloat16)
    )
    partial_out = jnp.dot(
        lax.all_gather(attended, "gx", axis=0, tiled=True),
        w_out,
        preferred_element_type=jnp.float32,
    )
    return lax.psum_scatter(partial_out.astype(jnp.bfloat16), "gy", scatter_dimension=0, tiled=True)


def swap(value, axis, bit):
    return lax.ppermute(value, axis, [(i, i ^ bit) for i in range(lax.axis_size(axis))])


def columns(array, start, size):
    return lax.dynamic_slice_in_dim(array, start, size, 1)


def prepare_kernel(own_ref, pair_ref, cos_ref, sin_ref, scale_ref, key_ref, value_ref):
    blocks = 4
    rows = pair_ref.shape[0] // blocks
    own = own_ref[0]
    key_ref[:SEG_MOST, :] = jnp.zeros((SEG_MOST, HD), jnp.bfloat16)
    value_ref[:SEG_MOST, :] = jnp.zeros((SEG_MOST, HD), jnp.bfloat16)
    for block in range(blocks):
        start = pl.multiple_of((block ^ own) * rows, rows)
        here = pl.ds(block * rows, rows)
        there = pl.ds(SEG_MOST + block * rows, rows)
        key = pair_ref[pl.ds(start, rows), :HD].astype(jnp.float32)
        value = pair_ref[pl.ds(start, rows), HD:].astype(jnp.float32)
        key = key * cos_ref[here, :] + pltpu.roll(key, HD // 2, 1) * sin_ref[here, :]
        key_ref[there, :] = key.astype(jnp.bfloat16)
        value_ref[there, :] = (value * scale_ref[here, :]).astype(jnp.bfloat16)


def prepare(own, pair, cosine, sine, scale):
    tokens = pair.shape[0]
    padded = jax.ShapeDtypeStruct((SEG_MOST + tokens, HD), jnp.bfloat16)
    vmem = pl.BlockSpec(memory_space=pltpu.VMEM)
    return pl.pallas_call(
        prepare_kernel,
        out_shape=[padded, padded],
        in_specs=[pl.BlockSpec(memory_space=pltpu.SMEM)] + [vmem] * 4,
        out_specs=[vmem, vmem],
        compiler_params=pltpu.CompilerParams(vmem_limit_bytes=32 * 2**20),
        cost_estimate=pl.CostEstimate(
            flops=8 * tokens * HD, bytes_accessed=20 * tokens * HD, transcendentals=0
        ),
    )(own, pair, cosine, sine, scale)


def attend_kernel(first, half, own_ref, len_ref, query_ref, key_ref, value_ref, cos_ref, sin_ref, out_ref):
    rows = query_ref.shape[0] // 2
    block_rows = cos_ref.shape[0] // 4
    window = SEG_MOST + rows
    own = own_ref[0]
    for piece in range(2):
        start = pl.multiple_of((own ^ (first + piece)) * block_rows + half * rows, rows)
        here = pl.ds(start, rows)
        key = key_ref[pl.ds(start, window), :]
        value = value_ref[pl.ds(start, window), :]
        query_at = start + lax.broadcasted_iota(jnp.int32, (rows, 1), 0)
        key_at = start - SEG_MOST + lax.broadcasted_iota(jnp.int32, (rows, window), 1)
        begin = jnp.zeros((rows, 1), jnp.int32)
        total = len_ref[0]
        for i in range(1, len_ref.shape[0]):
            begin = jnp.where(query_at >= total, total, begin)
            total = total + len_ref[i]
        allowed = (key_at >= begin) & (key_at <= query_at)
        for head in range(2):
            at = pl.ds(head * HD, HD)
            query = query_ref[pl.ds(piece * rows, rows), at].astype(jnp.float32)
            query = query * cos_ref[here, :] + pltpu.roll(query, HD // 2, 1) * sin_ref[here, :]
            scores = lax.dot_general(
                query.astype(jnp.bfloat16),
                key,
                (((1,), (1,)), ((), ())),
                preferred_element_type=jnp.float32,
            )
            scores = jnp.where(allowed, scores * (1.0 / math.sqrt(HD)), -1e30)
            weights = jnp.exp(scores - jnp.max(scores, axis=1, keepdims=True))
            weights = jnp.where(allowed, weights, 0.0)
            denominator = jnp.sum(weights, axis=1, keepdims=True)
            added = jnp.dot(weights.astype(jnp.bfloat16), value, preferred_element_type=jnp.float32)
            out_ref[pl.ds(piece * rows, rows), at] = (added / denominator).astype(jnp.bfloat16)


def attend(first, half, own, seg_lengths, query, key, value, cosine, sine):
    rows = query.shape[0]
    vmem = pl.BlockSpec(memory_space=pltpu.VMEM)
    smem = pl.BlockSpec(memory_space=pltpu.SMEM)
    scores = 2 * rows * (SEG_MOST + rows // 2)
    return pl.pallas_call(
        functools.partial(attend_kernel, first, half),
        out_shape=jax.ShapeDtypeStruct(query.shape, jnp.bfloat16),
        in_specs=[smem, smem] + [vmem] * 5,
        out_specs=vmem,
        compiler_params=pltpu.CompilerParams(vmem_limit_bytes=32 * 2**20),
        cost_estimate=pl.CostEstimate(
            flops=4 * scores * HD, bytes_accessed=4 * 2**20, transcendentals=scores
        ),
    )(own, seg_lengths, query, key, value, cosine, sine)


def shards_8x4(hidden_in, norm_gain, w_query, w_key, w_value, w_out, seg_lengths):
    f32, bf16 = jnp.float32, jnp.bfloat16
    rows, width = hidden_in.shape
    model_width = width * lax.axis_size("gx")
    tokens = rows * lax.axis_size("gy")
    cols = w_query.shape[1]
    half_rows, half_cols, piece = rows // 2, cols // 2, cols // 8
    gx, gy = lax.axis_index("gx"), lax.axis_index("gy")
    x_at, z_low, z_high = gx & 1, (gx >> 1) & 1, gx >> 2
    rank = x_at * 4 + z_low * 2 + z_high
    own = gy.astype(jnp.int32)[None]

    widened = hidden_in.astype(f32)
    source = (widened * norm_gain[None, :]).astype(bf16)
    squares = jnp.sum(widened * widened, axis=1)
    squares = lax.dynamic_update_slice_in_dim(jnp.zeros((tokens,), f32), squares, gy * rows, 0)

    parts = {}
    for h in range(2):
        parts[0, h] = source[h * half_rows : (h + 1) * half_rows]
        parts[1, h] = swap(parts[0, h], "gy", 1)
        parts[2, h] = swap(parts[0, h], "gy", 2)
        parts[3, h] = swap(parts[2, h], "gy", 1)

    key_part = jnp.dot(source, w_key, preferred_element_type=f32).astype(bf16)
    value_part = jnp.dot(source, w_value, preferred_element_type=f32).astype(bf16)

    def pair_heads(side):
        picked = []
        for r in range(4):
            head = (gy ^ r) * 2 + side
            picked += [columns(key_part, head * HD, HD), columns(value_part, head * HD, HD)]
        return jnp.concatenate(picked, axis=1)

    pair = pair_heads(x_at).astype(f32) + swap(pair_heads(1 - x_at), "gx", 1).astype(f32)
    pair = pair.astype(bf16)
    b = [pair[:, 2 * HD * r : 2 * HD * (r + 1)] for r in range(4)]
    got = swap(jnp.concatenate([b[1], b[3]], axis=0), "gy", 1)
    got_1, got_3 = got[:rows], got[rows:]
    far = swap(jnp.concatenate([b[2], got_3], axis=0), "gy", 2)
    pair = jnp.concatenate([b[0], got_1, far], axis=0)
    pair = lax.psum(pair, "gx", axis_index_groups=[[0, 2, 4, 6], [1, 3, 5, 7]])

    squares = lax.psum(squares, ("gx", "gy"))
    scale = lax.rsqrt(squares / model_width + EPS)[:, None]
    _, position = segment_table(seg_lengths, tokens)
    lane = jnp.arange(HD, dtype=jnp.int32)
    exponent = (lane % (HD // 2)).astype(f32) * (2.0 / HD)
    angle = position.astype(f32)[:, None] * (ROPE_BASE ** (-exponent))[None, :]
    cosine = jnp.cos(angle) * scale
    sine = jnp.where(lane < HD // 2, -1.0, 1.0)[None, :] * jnp.sin(angle) * scale
    key, value = prepare(own, pair, cosine, sine, jnp.broadcast_to(scale, (tokens, HD)))

    query_blocks = [columns(w_query, (rank ^ r) * piece, piece) for r in range(8)]
    w_near = jnp.concatenate(query_blocks[0:2], axis=1)
    w_low = jnp.concatenate(query_blocks[2:4], axis=1)
    w_cross = jnp.concatenate(query_blocks[4:8], axis=1)
    w_rows = jnp.concatenate(
        [lax.dynamic_slice_in_dim(w_out, (rank ^ r) * piece, piece, 0) for r in range(8)], axis=0
    )

    attended = {}
    for first in (0, 2):
        for h in range(2):
            chunk = jnp.concatenate([parts[first, h], parts[first + 1, h]], axis=0)
            cross = swap(jnp.dot(chunk, w_cross, preferred_element_type=f32).astype(bf16), "gx", 1)
            low = jnp.dot(chunk, w_low, preferred_element_type=f32) + cross[:, half_cols // 2 :].astype(f32)
            near = jnp.dot(chunk, w_near, preferred_element_type=f32) + cross[:, : half_cols // 2].astype(f32)
            got = swap(low.astype(bf16), "gx", 2)
            high = near[:, piece:] + got[:, piece:].astype(f32)
            near = near[:, :piece] + got[:, :piece].astype(f32)
            query = (near + swap(high.astype(bf16), "gx", 4).astype(f32)).astype(bf16)
            attended[first, h] = attend(first, h, own, seg_lengths, query, key, value, cosine, sine)

    kept, crossed = {}, {}
    for first, h in ((0, 0), (2, 0), (2, 1), (0, 1)):
        a = attended[first, h]
        a = jnp.concatenate([a, swap(a, "gx", 4)], axis=1)
        a = jnp.concatenate([a, swap(a, "gx", 2)], axis=1)
        a = jnp.concatenate([a, swap(a, "gx", 1)], axis=1)
        given = jnp.dot(a[half_rows:], w_rows, preferred_element_type=f32).astype(bf16)
        mine = jnp.dot(a[:half_rows], w_rows, preferred_element_type=f32)
        mine = mine + swap(given, "gy", 1).astype(f32)
        if first:
            crossed[h] = swap(mine.astype(bf16), "gy", 2)
        else:
            kept[h] = mine
    return jnp.concatenate(
        [(kept[h] + crossed[h].astype(f32)).astype(bf16) for h in range(2)], axis=0
    )


def shards(hidden_in, norm_gain, w_query, w_key, w_value, w_out, seg_lengths):
    split = (lax.axis_size("gx"), lax.axis_size("gy"))
    body = shards_8x4 if split == (8, 4) else shards_any
    return body(hidden_in, norm_gain, w_query, w_key, w_value, w_out, seg_lengths)


def solution(mesh):
    in_specs = (
        P("gy", "gx"),
        P("gx"),
        P("gx", "gy"),
        P("gx", None),
        P("gx", None),
        P("gy", "gx"),
        P(),
    )
    out_specs = P("gy", "gx")
    return jax.shard_map(shards, mesh=mesh, in_specs=in_specs, out_specs=out_specs, check_vma=False)
```

```python
import functools
import math

import jax
import jax.numpy as jnp
from jax import lax
from jax.experimental import pallas as pl
from jax.experimental.pallas import tpu as pltpu
from jax.sharding import PartitionSpec as P

H = 64
KVH = 8
HD = 128


ROPE_BASE = 500000.0
EPS = 1e-05
SEG_MOST = 512


def rotate(values, position, head_size):
    half = head_size // 2
    exponent = jnp.arange(half, dtype=jnp.float32) * (2.0 / head_size)
    frequency = ROPE_BASE ** (-exponent)
    angle = position[:, None, None] * frequency[None, None, :]
    cosine = jnp.cos(angle)
    sine = jnp.sin(angle)
    first = values[..., :half]
    second = values[..., half:]
    return jnp.concatenate(
        [first * cosine - second * sine, second * cosine + first * sine], axis=-1
    )


def segment_table(seg_lengths, tokens):
    ends = jnp.cumsum(seg_lengths)
    starts = ends - seg_lengths
    index = jnp.arange(tokens, dtype=jnp.int32)
    member = ((index[:, None] >= starts[None, :]) & (index[:, None] < ends[None, :])).astype(
        jnp.int32
    )
    seg_id = jnp.sum(member * jnp.arange(seg_lengths.shape[0], dtype=jnp.int32)[None, :], axis=1)
    first_index = jnp.sum(member * starts[None, :], axis=1)
    return (seg_id, index - first_index)


def normalize(block, gain, squares, model_width):
    widened = block.astype(jnp.float32)
    scale = lax.rsqrt(squares / model_width + EPS)
    return (widened * scale[:, None] * gain[None, :]).astype(jnp.bfloat16)


def shards_any(hidden_in, norm_gain, w_query, w_key, w_value, w_out, seg_lengths):
    rows_own, width = hidden_in.shape
    model_width = width * lax.axis_size("gx")
    tokens = rows_own * lax.axis_size("gy")
    query_rows = tokens // lax.axis_size("gx")
    widened = hidden_in.astype(jnp.float32)
    squares = lax.psum(jnp.sum(widened * widened, axis=1), "gx")
    source = normalize(hidden_in, norm_gain, squares, model_width)
    gathered = lax.all_gather(source, "gy", axis=0, tiled=True)
    query_cols = w_query.shape[1]
    heads_local = query_cols // HD
    group = H // KVH
    kv_local = max(1, heads_local // group)
    pair_cols = kv_local * HD
    first_head = lax.axis_index("gy") * heads_local // group
    key_own = lax.dynamic_slice_in_dim(w_key, first_head * HD, pair_cols, 1)
    value_own = lax.dynamic_slice_in_dim(w_value, first_head * HD, pair_cols, 1)
    seg_id, position = segment_table(seg_lengths, tokens)
    here = lax.axis_index("gx") * query_rows
    query_seg = lax.dynamic_slice_in_dim(seg_id, here, query_rows)
    query_pos = lax.dynamic_slice_in_dim(position, here, query_rows)
    query_index = here + jnp.arange(query_rows, dtype=jnp.int32)
    query_sum = lax.psum_scatter(
        jnp.dot(gathered, w_query, preferred_element_type=jnp.float32).astype(jnp.bfloat16),
        "gx",
        scatter_dimension=0,
        tiled=True,
    ).astype(jnp.float32)
    pair_part = jnp.concatenate(
        [
            jnp.dot(gathered, key_own, preferred_element_type=jnp.float32),
            jnp.dot(gathered, value_own, preferred_element_type=jnp.float32),
        ],
        axis=1,
    )
    pair_sum = lax.psum(pair_part.astype(jnp.bfloat16), "gx").astype(jnp.float32)
    key_raw = pair_sum[:, :pair_cols].astype(jnp.bfloat16)
    value_raw = pair_sum[:, pair_cols:].astype(jnp.bfloat16)
    group_local = heads_local // kv_local
    queries = rotate(
        query_sum.reshape(query_rows, heads_local, HD), query_pos.astype(jnp.float32), HD
    ).astype(jnp.bfloat16)
    queries = queries.reshape(query_rows, kv_local, group_local, HD)
    key_count = key_raw.shape[0]
    keys = rotate(
        key_raw.astype(jnp.float32).reshape(key_count, kv_local, HD),
        position.astype(jnp.float32),
        HD,
    )
    keys = keys.astype(jnp.bfloat16).reshape(key_count, pair_cols)
    score_scale = 1.0 / math.sqrt(HD)
    running = jnp.full((kv_local, group_local, query_rows), -1e30, jnp.float32)
    count = keys.shape[0]
    key_index = jnp.arange(count, dtype=jnp.int32)
    allowed = (query_seg[:, None] == seg_id[None, :]) & (key_index[None, :] <= query_index[:, None])
    key_heads = keys.reshape(count, kv_local, HD)
    value_heads = value_raw.reshape(count, kv_local, HD)
    scores = (
        jnp.einsum("rkgd,nkd->kgrn", queries, key_heads, preferred_element_type=jnp.float32)
        * score_scale
    )
    scores = jnp.where(allowed[None, None], scores, -1e30)
    newest = jnp.maximum(running, jnp.max(scores, axis=-1))
    weights = jnp.where(allowed[None, None], jnp.exp(scores - newest[..., None]), 0.0)
    denominator = jnp.sum(weights, axis=-1)
    added = jnp.einsum(
        "kgrn,nkd->rkgd",
        weights.astype(jnp.bfloat16),
        value_heads,
        preferred_element_type=jnp.float32,
    )
    accum = added
    running, denominator, accum = (newest, denominator, accum)
    attended = (
        (accum / denominator.transpose(2, 0, 1)[..., None])
        .reshape(query_rows, query_cols)
        .astype(jnp.bfloat16)
    )
    partial_out = jnp.dot(
        lax.all_gather(attended, "gx", axis=0, tiled=True),
        w_out,
        preferred_element_type=jnp.float32,
    )
    return lax.psum_scatter(partial_out.astype(jnp.bfloat16), "gy", scatter_dimension=0, tiled=True)


SCOPE = 32 * 2**20
SMALL = pl.CostEstimate(flops=0, bytes_accessed=0, transcendentals=0)


def swap(value, axis, bit):
    return lax.ppermute(value, axis, [(i, i ^ bit) for i in range(lax.axis_size(axis))])


def columns(array, start, size):
    return lax.dynamic_slice_in_dim(array, start, size, 1)


def after(value, *others):
    hbm = pl.BlockSpec(memory_space=pl.ANY)
    return pl.pallas_call(
        lambda *refs: None,
        out_shape=jax.ShapeDtypeStruct(value.shape, value.dtype),
        in_specs=[hbm] * (1 + len(others)),
        out_specs=hbm,
        input_output_aliases={0: 0},
        cost_estimate=SMALL,
    )(value, *others)


def prepare_kernel(own_ref, pair_ref, cos_ref, sin_ref, scale_ref, key_ref, value_ref):
    blocks = 4
    rows = pair_ref.shape[0] // blocks
    own = own_ref[0]
    key_ref[:SEG_MOST, :] = jnp.zeros((SEG_MOST, HD), jnp.bfloat16)
    value_ref[:SEG_MOST, :] = jnp.zeros((SEG_MOST, HD), jnp.bfloat16)
    for block in range(blocks):
        start = pl.multiple_of((block ^ own) * rows, rows)
        here = pl.ds(block * rows, rows)
        there = pl.ds(SEG_MOST + block * rows, rows)
        key = pair_ref[pl.ds(start, rows), :HD].astype(jnp.float32)
        value = pair_ref[pl.ds(start, rows), HD:].astype(jnp.float32)
        key = key * cos_ref[here, :] + pltpu.roll(key, HD // 2, 1) * sin_ref[here, :]
        key_ref[there, :] = key.astype(jnp.bfloat16)
        value_ref[there, :] = (value * scale_ref[here, :]).astype(jnp.bfloat16)


def prepare(own, pair, cosine, sine, scale):
    tokens = pair.shape[0]
    padded = jax.ShapeDtypeStruct((SEG_MOST + tokens, HD), jnp.bfloat16)
    vmem = pl.BlockSpec(memory_space=pltpu.VMEM)
    return pl.pallas_call(
        prepare_kernel,
        out_shape=[padded, padded],
        in_specs=[pl.BlockSpec(memory_space=pltpu.SMEM)] + [vmem] * 4,
        out_specs=[vmem, vmem],
        compiler_params=pltpu.CompilerParams(vmem_limit_bytes=SCOPE),
        cost_estimate=SMALL,
    )(own, pair, cosine, sine, scale)


def attend_kernel(first, half, own_ref, len_ref, query_ref, key_ref, value_ref, cos_ref, sin_ref, out_ref):
    rows = query_ref.shape[0] // 2
    block_rows = cos_ref.shape[0] // 4
    window = SEG_MOST + rows
    own = own_ref[0]
    for piece in range(2):
        start = pl.multiple_of((own ^ (first + piece)) * block_rows + half * rows, rows)
        here = pl.ds(start, rows)
        key = key_ref[pl.ds(start, window), :]
        value = value_ref[pl.ds(start, window), :]
        query_at = start + lax.broadcasted_iota(jnp.int32, (rows, 1), 0)
        key_at = start - SEG_MOST + lax.broadcasted_iota(jnp.int32, (rows, window), 1)
        begin = jnp.zeros((rows, 1), jnp.int32)
        total = len_ref[0]
        for i in range(1, len_ref.shape[0]):
            begin = jnp.where(query_at >= total, total, begin)
            total = total + len_ref[i]
        allowed = (key_at >= begin) & (key_at <= query_at)
        for head in range(2):
            at = pl.ds(head * HD, HD)
            query = query_ref[pl.ds(piece * rows, rows), at].astype(jnp.float32)
            query = query * cos_ref[here, :] + pltpu.roll(query, HD // 2, 1) * sin_ref[here, :]
            scores = lax.dot_general(
                query.astype(jnp.bfloat16),
                key,
                (((1,), (1,)), ((), ())),
                preferred_element_type=jnp.float32,
            )
            scores = jnp.where(allowed, scores * (1.0 / math.sqrt(HD)), -1e30)
            weights = jnp.exp(scores - jnp.max(scores, axis=1, keepdims=True))
            weights = jnp.where(allowed, weights, 0.0)
            denominator = jnp.sum(weights, axis=1, keepdims=True)
            added = jnp.dot(weights.astype(jnp.bfloat16), value, preferred_element_type=jnp.float32)
            out_ref[pl.ds(piece * rows, rows), at] = (added / denominator).astype(jnp.bfloat16)


def attend(first, half, own, seg_lengths, query, key, value, cosine, sine):
    rows = query.shape[0]
    vmem = pl.BlockSpec(memory_space=pltpu.VMEM)
    smem = pl.BlockSpec(memory_space=pltpu.SMEM)
    return pl.pallas_call(
        functools.partial(attend_kernel, first, half),
        out_shape=jax.ShapeDtypeStruct(query.shape, jnp.bfloat16),
        in_specs=[smem, smem] + [vmem] * 5,
        out_specs=vmem,
        compiler_params=pltpu.CompilerParams(vmem_limit_bytes=SCOPE),
        cost_estimate=pl.CostEstimate(
            flops=2**31, bytes_accessed=2**20, transcendentals=0
        ),
    )(own, seg_lengths, query, key, value, cosine, sine)


def copy_kernel(place_ref, weight_ref, out_ref):
    del place_ref
    out_ref[...] = weight_ref[...]


def reorder(place, weight):
    blocks = place.shape[0]
    shape = (weight.shape[0] // blocks, weight.shape[1])
    return pl.pallas_call(
        copy_kernel,
        out_shape=jax.ShapeDtypeStruct(weight.shape, jnp.bfloat16),
        grid_spec=pltpu.PrefetchScalarGridSpec(
            num_scalar_prefetch=1,
            grid=(blocks,),
            in_specs=[pl.BlockSpec(shape, lambda j, place: (place[j], 0))],
            out_specs=pl.BlockSpec(shape, lambda j, place: (j, 0)),
        ),
        compiler_params=pltpu.CompilerParams(vmem_limit_bytes=SCOPE),
        cost_estimate=pl.CostEstimate(
            flops=0, bytes_accessed=4 * weight.size, transcendentals=0
        ),
    )(place, weight)


def scale_rows(gain_ref, source_refs, scaled):
    @pl.when(pl.program_id(0) == 0)
    def _():
        at = 0
        for ref in source_refs:
            widened = ref[...].astype(jnp.float32) * gain_ref[...]
            scaled[pl.ds(at, ref.shape[0]), :] = widened.astype(jnp.bfloat16)
            at += ref.shape[0]


def pairs_kernel(place_ref, gain_ref, source_ref, key_ref, value_ref, given_ref, kept_ref, scaled):
    scale_rows(gain_ref, [source_ref], scaled)
    second = place_ref[place_ref.shape[0] - 1] == 1
    for i, ref in enumerate((key_ref, value_ref)):
        product = jnp.dot(scaled[...], ref[...], preferred_element_type=jnp.float32)
        product = product.astype(jnp.bfloat16)
        low, high = product[:, :HD], product[:, HD:]
        kept_ref[:, pl.ds(i * HD, HD)] = jnp.where(second, high, low)
        given_ref[:, pl.ds(i * HD, HD)] = jnp.where(second, low, high)


def pairs(place, gain, source, w_key, w_value):
    rows, depth = source.shape
    out = jax.ShapeDtypeStruct((rows, 8 * HD), jnp.bfloat16)
    picked = pl.BlockSpec((depth, 2 * HD), lambda j, place: (0, place[j]))
    made = pl.BlockSpec((rows, 2 * HD), lambda j, place: (0, j))
    return pl.pallas_call(
        pairs_kernel,
        out_shape=[out, out],
        grid_spec=pltpu.PrefetchScalarGridSpec(
            num_scalar_prefetch=1,
            grid=(4,),
            in_specs=[
                pl.BlockSpec((1, depth), lambda j, place: (0, 0)),
                pl.BlockSpec((rows, depth), lambda j, place: (0, 0)),
                picked,
                picked,
            ],
            out_specs=[made, made],
            scratch_shapes=[pltpu.VMEM((rows, depth), jnp.bfloat16)],
        ),
        compiler_params=pltpu.CompilerParams(vmem_limit_bytes=SCOPE),
        cost_estimate=pl.CostEstimate(
            flops=4 * rows * depth * 8 * HD, bytes_accessed=4 * depth * 8 * HD, transcendentals=0
        ),
    )(place, gain[None, :], source, w_key, w_value)


def project_kernel(pieces, place_ref, gain_ref, *refs):
    weight_ref, out_refs, scaled = refs[pieces], refs[pieces + 1 : -1], refs[-1]
    scale_rows(gain_ref, refs[:pieces], scaled)
    product = jnp.dot(scaled[...], weight_ref[...], preferred_element_type=jnp.float32)
    rows = product.shape[0] // len(out_refs)
    for i, ref in enumerate(out_refs):
        ref[...] = product[i * rows : (i + 1) * rows, :].astype(jnp.bfloat16)


def project(place, gain, pieces, weight, size, outs):
    piece_rows, depth = pieces[0].shape
    rows, width = len(pieces) * piece_rows, size * place.shape[0]
    out = jax.ShapeDtypeStruct((rows // outs, width), jnp.bfloat16)
    return pl.pallas_call(
        functools.partial(project_kernel, len(pieces)),
        out_shape=[out] * outs,
        grid_spec=pltpu.PrefetchScalarGridSpec(
            num_scalar_prefetch=1,
            grid=(place.shape[0],),
            in_specs=[pl.BlockSpec((1, depth), lambda j, place: (0, 0))]
            + [pl.BlockSpec((piece_rows, depth), lambda j, place: (0, 0))] * len(pieces)
            + [pl.BlockSpec((depth, size), lambda j, place: (0, place[j]))],
            out_specs=[pl.BlockSpec((rows // outs, size), lambda j, place: (0, j))] * outs,
            scratch_shapes=[pltpu.VMEM((rows, depth), jnp.bfloat16)],
        ),
        compiler_params=pltpu.CompilerParams(vmem_limit_bytes=SCOPE),
        cost_estimate=pl.CostEstimate(
            flops=2 * rows * depth * width,
            bytes_accessed=2 * (rows * depth + (depth + rows) * width),
            transcendentals=0,
        ),
    )(place, gain[None, :], *pieces, weight)


def shards_8x4(hidden_in, norm_gain, w_query, w_key, w_value, w_out, seg_lengths):
    f32, bf16 = jnp.float32, jnp.bfloat16
    rows, width = hidden_in.shape
    model_width = width * lax.axis_size("gx")
    tokens = rows * lax.axis_size("gy")
    cols = w_query.shape[1]
    half_rows, piece, pair_cols = rows // 2, cols // 8, 2 * HD
    gx, gy = lax.axis_index("gx"), lax.axis_index("gy")
    x_at, z_low, z_high = gx & 1, (gx >> 1) & 1, gx >> 2
    rank = (x_at * 4 + z_low * 2 + z_high).astype(jnp.int32)
    z_at = z_low * 2 + z_high
    own = gy.astype(jnp.int32)[None]
    order = jnp.arange(4, dtype=jnp.int32)

    widened = hidden_in.astype(f32)
    squares = jnp.sum(widened * widened, axis=1)
    squares = lax.dynamic_update_slice_in_dim(jnp.zeros((tokens,), f32), squares, gy * rows, 0)
    squares = squares.reshape(tokens // HD, HD)
    squares = squares_x = squares + swap(squares, "gx", 1)
    for axis, bit in (("gy", 1), ("gx", 2), ("gx", 4)):
        squares = squares + swap(squares, axis, bit)

    parts = {}
    for h in range(2):
        parts[0, h] = hidden_in[h * half_rows : (h + 1) * half_rows]
        parts[1, h] = swap(parts[0, h], "gy", 1)

    for h in range(2):
        parts[2, h] = swap(parts[0, h], "gy", 2)
        parts[3, h] = swap(parts[2, h], "gy", 1)


    x_served = []

    def swap_x(value):
        if x_served:
            value = after(value, x_served[-1])
        x_served.append(swap(value, "gx", 1))
        return x_served[-1]

    def pieces(first):
        return [parts[first + i, h] for h in range(2) for i in range(2)]

    place = jnp.concatenate([gy ^ order, x_at[None]]).astype(jnp.int32)
    given, kept_pair = pairs(place, norm_gain, hidden_in, w_key, w_value)
    near_place = after(rank ^ (order + 4), given)
    crossed_in, keeps = {}, {}
    outs = project(near_place, norm_gain, pieces(0), w_query, piece, 2)
    (keeps[0],) = project(after(rank ^ order, outs[0]), norm_gain, pieces(0), w_query, piece, 1)
    given = swap_x(after(given, squares_x))
    crossed_in[0, 0], crossed_in[0, 1] = swap_x(outs[0]), swap_x(outs[1])
    pair = given.astype(f32) + after(kept_pair, keeps[0]).astype(f32)
    pair = pair.astype(bf16)
    given = columns(pair, (1 - z_low) * 2 * pair_cols, 2 * pair_cols)
    pair = columns(pair, z_low * 2 * pair_cols, 2 * pair_cols).astype(f32)
    pair = (pair + swap(given, "gx", 2).astype(f32)).astype(bf16)
    outs = project(after(rank ^ (order + 4), pair), norm_gain, pieces(2), w_query, piece, 2)
    (keeps[2],) = project(after(rank ^ order, outs[0]), norm_gain, pieces(2), w_query, piece, 1)
    crossed_in[2, 0], crossed_in[2, 1] = swap_x(outs[0]), swap_x(outs[1])
    given = columns(pair, (1 - z_high) * pair_cols, pair_cols)
    pair = columns(pair, z_high * pair_cols, pair_cols).astype(f32)
    pair = (pair + swap(given, "gx", 4).astype(f32)).astype(bf16)
    across = []
    for i in range(8):
        for j in range(4):
            across.append((i * 4 + j, i * 4 + (j ^ ((i >> 1) & 1) * 2 ^ (i >> 2))))
    squares = after(squares, pair)
    pair = lax.ppermute(pair, ("gx", "gy"), across)
    squares = squares + swap(squares, "gy", 2)
    pair = jnp.concatenate([pair, swap(pair, "gx", 4)], axis=0)
    pair = jnp.concatenate([pair, swap(pair, "gx", 2)], axis=0)

    scale = lax.rsqrt(squares.reshape(tokens) / model_width + EPS)[:, None]
    _, position = segment_table(seg_lengths, tokens)
    lane = jnp.arange(HD, dtype=jnp.int32)
    exponent = (lane % (HD // 2)).astype(f32) * (2.0 / HD)
    angle = position.astype(f32)[:, None] * (ROPE_BASE ** (-exponent))[None, :]
    cosine = jnp.cos(angle) * scale
    sine = jnp.where(lane < HD // 2, -1.0, 1.0)[None, :] * jnp.sin(angle) * scale
    key, value = prepare(own ^ z_at, pair, cosine, sine, jnp.broadcast_to(scale, (tokens, HD)))

    attended, last = {}, None
    for first, h in ((0, 0), (0, 1), (2, 0), (2, 1)):
        cross = crossed_in[first, h]
        keep = keeps[first][h * rows : (h + 1) * rows]
        low = (keep[:, 2 * piece :].astype(f32) + cross[:, 2 * piece :].astype(f32)).astype(bf16)
        if last is not None:
            low = after(low, last, keeps[2])
        last = got = swap(low, "gx", 2)
        near = keep[:, : 2 * piece].astype(f32) + cross[:, : 2 * piece].astype(f32)
        high = near[:, piece:] + got[:, piece:].astype(f32)
        near = near[:, :piece] + got[:, :piece].astype(f32)
        got = swap(high.astype(bf16), "gx", 4)
        query = (near + got.astype(f32)).astype(bf16)
        attended[first, h] = attend(first, h, own, seg_lengths, query, key, value, cosine, sine)
    attended[0, 1] = after(attended[0, 1], got)

    w_rows = reorder(after(rank ^ jnp.arange(8, dtype=jnp.int32), crossed_in[2, 0]), w_out)
    kept, crossed = {}, {}
    for first, h in ((0, 0), (2, 0), (2, 1), (0, 1)):
        a = attended[first, h]
        a = jnp.concatenate([a, swap(a, "gx", 4)], axis=1)
        a = jnp.concatenate([a, swap(a, "gx", 2)], axis=1)
        got = swap_x(a)
        a = jnp.concatenate([a, got], axis=1)
        given = jnp.dot(a[half_rows:], w_rows, preferred_element_type=f32).astype(bf16)
        mine = jnp.dot(a[:half_rows], w_rows, preferred_element_type=f32)
        mine = mine + swap(given, "gy", 1).astype(f32)
        if first:
            crossed[h] = swap(mine.astype(bf16), "gy", 2)
        else:
            kept[h] = mine
    return jnp.concatenate(
        [(kept[h] + crossed[h].astype(f32)).astype(bf16) for h in range(2)], axis=0
    )


def shards(hidden_in, norm_gain, w_query, w_key, w_value, w_out, seg_lengths):
    split = (lax.axis_size("gx"), lax.axis_size("gy"))
    body = shards_8x4 if split == (8, 4) else shards_any
    return body(hidden_in, norm_gain, w_query, w_key, w_value, w_out, seg_lengths)


def solution(mesh):
    in_specs = (
        P("gy", "gx"),
        P("gx"),
        P("gx", "gy"),
        P("gx", None),
        P("gx", None),
        P("gy", "gx"),
        P(),
    )
    out_specs = P("gy", "gx")
    return jax.shard_map(shards, mesh=mesh, in_specs=in_specs, out_specs=out_specs, check_vma=False)
```

```python
import functools
import math

import jax
import jax.numpy as jnp
from jax import lax
from jax.experimental import pallas as pl
from jax.experimental.pallas import tpu as pltpu
from jax.sharding import PartitionSpec as P

H = 64
KVH = 8
HD = 128


ROPE_BASE = 500000.0
EPS = 1e-05
SEG_MOST = 512


def rotate(values, position, head_size):
    half = head_size // 2
    exponent = jnp.arange(half, dtype=jnp.float32) * (2.0 / head_size)
    frequency = ROPE_BASE ** (-exponent)
    angle = position[:, None, None] * frequency[None, None, :]
    cosine = jnp.cos(angle)
    sine = jnp.sin(angle)
    first = values[..., :half]
    second = values[..., half:]
    return jnp.concatenate(
        [first * cosine - second * sine, second * cosine + first * sine], axis=-1
    )


def segment_table(seg_lengths, tokens):
    ends = jnp.cumsum(seg_lengths)
    starts = ends - seg_lengths
    index = jnp.arange(tokens, dtype=jnp.int32)
    member = ((index[:, None] >= starts[None, :]) & (index[:, None] < ends[None, :])).astype(
        jnp.int32
    )
    seg_id = jnp.sum(member * jnp.arange(seg_lengths.shape[0], dtype=jnp.int32)[None, :], axis=1)
    first_index = jnp.sum(member * starts[None, :], axis=1)
    return (seg_id, index - first_index)


def normalize(block, gain, squares, model_width):
    widened = block.astype(jnp.float32)
    scale = lax.rsqrt(squares / model_width + EPS)
    return (widened * scale[:, None] * gain[None, :]).astype(jnp.bfloat16)


def shards_any(hidden_in, norm_gain, w_query, w_key, w_value, w_out, seg_lengths):
    rows_own, width = hidden_in.shape
    model_width = width * lax.axis_size("gx")
    tokens = rows_own * lax.axis_size("gy")
    query_rows = tokens // lax.axis_size("gx")
    widened = hidden_in.astype(jnp.float32)
    squares = lax.psum(jnp.sum(widened * widened, axis=1), "gx")
    source = normalize(hidden_in, norm_gain, squares, model_width)
    gathered = lax.all_gather(source, "gy", axis=0, tiled=True)
    query_cols = w_query.shape[1]
    heads_local = query_cols // HD
    group = H // KVH
    kv_local = max(1, heads_local // group)
    pair_cols = kv_local * HD
    first_head = lax.axis_index("gy") * heads_local // group
    key_own = lax.dynamic_slice_in_dim(w_key, first_head * HD, pair_cols, 1)
    value_own = lax.dynamic_slice_in_dim(w_value, first_head * HD, pair_cols, 1)
    seg_id, position = segment_table(seg_lengths, tokens)
    here = lax.axis_index("gx") * query_rows
    query_seg = lax.dynamic_slice_in_dim(seg_id, here, query_rows)
    query_pos = lax.dynamic_slice_in_dim(position, here, query_rows)
    query_index = here + jnp.arange(query_rows, dtype=jnp.int32)
    query_sum = lax.psum_scatter(
        jnp.dot(gathered, w_query, preferred_element_type=jnp.float32).astype(jnp.bfloat16),
        "gx",
        scatter_dimension=0,
        tiled=True,
    ).astype(jnp.float32)
    pair_part = jnp.concatenate(
        [
            jnp.dot(gathered, key_own, preferred_element_type=jnp.float32),
            jnp.dot(gathered, value_own, preferred_element_type=jnp.float32),
        ],
        axis=1,
    )
    pair_sum = lax.psum(pair_part.astype(jnp.bfloat16), "gx").astype(jnp.float32)
    key_raw = pair_sum[:, :pair_cols].astype(jnp.bfloat16)
    value_raw = pair_sum[:, pair_cols:].astype(jnp.bfloat16)
    group_local = heads_local // kv_local
    queries = rotate(
        query_sum.reshape(query_rows, heads_local, HD), query_pos.astype(jnp.float32), HD
    ).astype(jnp.bfloat16)
    queries = queries.reshape(query_rows, kv_local, group_local, HD)
    key_count = key_raw.shape[0]
    keys = rotate(
        key_raw.astype(jnp.float32).reshape(key_count, kv_local, HD),
        position.astype(jnp.float32),
        HD,
    )
    keys = keys.astype(jnp.bfloat16).reshape(key_count, pair_cols)
    score_scale = 1.0 / math.sqrt(HD)
    running = jnp.full((kv_local, group_local, query_rows), -1e30, jnp.float32)
    count = keys.shape[0]
    key_index = jnp.arange(count, dtype=jnp.int32)
    allowed = (query_seg[:, None] == seg_id[None, :]) & (key_index[None, :] <= query_index[:, None])
    key_heads = keys.reshape(count, kv_local, HD)
    value_heads = value_raw.reshape(count, kv_local, HD)
    scores = (
        jnp.einsum("rkgd,nkd->kgrn", queries, key_heads, preferred_element_type=jnp.float32)
        * score_scale
    )
    scores = jnp.where(allowed[None, None], scores, -1e30)
    newest = jnp.maximum(running, jnp.max(scores, axis=-1))
    weights = jnp.where(allowed[None, None], jnp.exp(scores - newest[..., None]), 0.0)
    denominator = jnp.sum(weights, axis=-1)
    added = jnp.einsum(
        "kgrn,nkd->rkgd",
        weights.astype(jnp.bfloat16),
        value_heads,
        preferred_element_type=jnp.float32,
    )
    accum = added
    running, denominator, accum = (newest, denominator, accum)
    attended = (
        (accum / denominator.transpose(2, 0, 1)[..., None])
        .reshape(query_rows, query_cols)
        .astype(jnp.bfloat16)
    )
    partial_out = jnp.dot(
        lax.all_gather(attended, "gx", axis=0, tiled=True),
        w_out,
        preferred_element_type=jnp.float32,
    )
    return lax.psum_scatter(partial_out.astype(jnp.bfloat16), "gy", scatter_dimension=0, tiled=True)


SCOPE = 24 * 2**20
EXTRA = 16
SMALL = pl.CostEstimate(flops=0, bytes_accessed=0, transcendentals=0)


def swap(value, axis, bit):
    return lax.ppermute(value, axis, [(i, i ^ bit) for i in range(lax.axis_size(axis))])


def columns(array, start, size):
    return lax.dynamic_slice_in_dim(array, start, size, 1)


def after(value, *others):
    hbm = pl.BlockSpec(memory_space=pl.ANY)
    return pl.pallas_call(
        lambda *refs: None,
        out_shape=jax.ShapeDtypeStruct(value.shape, value.dtype),
        in_specs=[hbm] * (1 + len(others)),
        out_specs=hbm,
        input_output_aliases={0: 0},
        cost_estimate=SMALL,
    )(value, *others)


def merge_kernel(split, at_ref, kept_ref, got_ref, squares_ref, *out_refs):
    rows = kept_ref.shape[0]
    arrived = got_ref[rows:, :HD].astype(jnp.float32)
    squares = squares_ref[...] + arrived[: EXTRA // 2] + arrived[EXTRA // 2 :]
    high = squares.astype(jnp.bfloat16).astype(jnp.float32)
    given_ref = out_refs[0]
    width = given_ref.shape[1]
    given_ref[rows:, :] = jnp.zeros((EXTRA, width), jnp.bfloat16)
    given_ref[rows:, :HD] = jnp.concatenate([high, squares - high], axis=0).astype(jnp.bfloat16)
    side = at_ref[0] if split else 1
    for i in range(1 + split):
        ref, at = out_refs[i], side if i else 1 - side
        at = pl.ds(pl.multiple_of(at * width, width), width) if split else slice(None)
        total = kept_ref[:, at].astype(jnp.float32) + got_ref[:rows, at].astype(jnp.float32)
        ref[:rows, :] = total.astype(jnp.bfloat16)
    if split:
        out_refs[2][...] = squares


def merge(split, side, kept, got, squares):
    rows, width = kept.shape
    vmem = pl.BlockSpec(memory_space=pltpu.VMEM)
    outs = [jax.ShapeDtypeStruct((rows + EXTRA, width // (1 + split)), jnp.bfloat16)]
    if split:
        outs.append(jax.ShapeDtypeStruct((rows, width // 2), jnp.bfloat16))
        outs.append(jax.ShapeDtypeStruct(squares.shape, jnp.float32))
    return pl.pallas_call(
        functools.partial(merge_kernel, split),
        out_shape=outs,
        in_specs=[pl.BlockSpec(memory_space=pltpu.SMEM)] + [vmem] * 3,
        out_specs=[vmem] * len(outs),
        compiler_params=pltpu.CompilerParams(vmem_limit_bytes=SCOPE),
        cost_estimate=SMALL,
    )(side, kept, got, squares)


def prepare_kernel(model_width, own_ref, pair_ref, cos_ref, sin_ref, key_ref, value_ref, scale_ref):
    blocks = 4
    held = pair_ref.shape[0] // blocks
    rows = held - EXTRA
    own = own_ref[0]
    key_ref[:SEG_MOST, :] = jnp.zeros((SEG_MOST, HD), jnp.bfloat16)
    value_ref[:SEG_MOST, :] = jnp.zeros((SEG_MOST, HD), jnp.bfloat16)
    for block in range(blocks):
        start = pl.multiple_of((block ^ own) * held, EXTRA)
        squares = pair_ref[pl.ds(pl.multiple_of(start + rows, EXTRA), EXTRA), :HD]
        squares = squares.astype(jnp.float32)
        squares = squares[: EXTRA // 2] + squares[EXTRA // 2 :]
        inverse = lax.rsqrt(squares / model_width + EPS)
        for i in range(rows // HD):
            here = pl.ds(block * rows + i * HD, HD)
            scale_ref[here, :] = jnp.transpose(jnp.broadcast_to(inverse[i : i + 1, :], (HD, HD)))
        here = pl.ds(block * rows, rows)
        there = pl.ds(SEG_MOST + block * rows, rows)
        key = pair_ref[pl.ds(start, rows), :HD].astype(jnp.float32)
        value = pair_ref[pl.ds(start, rows), HD:].astype(jnp.float32)
        key = key * cos_ref[here, :] + pltpu.roll(key, HD // 2, 1) * sin_ref[here, :]
        key_ref[there, :] = (key * scale_ref[here, :]).astype(jnp.bfloat16)
        value_ref[there, :] = (value * scale_ref[here, :]).astype(jnp.bfloat16)


def prepare(model_width, own, pair, cosine, sine):
    tokens = cosine.shape[0]
    padded = jax.ShapeDtypeStruct((SEG_MOST + tokens, HD), jnp.bfloat16)
    vmem = pl.BlockSpec(memory_space=pltpu.VMEM)
    return pl.pallas_call(
        functools.partial(prepare_kernel, model_width),
        out_shape=[padded, padded, jax.ShapeDtypeStruct((tokens, HD), jnp.float32)],
        in_specs=[pl.BlockSpec(memory_space=pltpu.SMEM)] + [vmem] * 3,
        out_specs=[vmem] * 3,
        compiler_params=pltpu.CompilerParams(vmem_limit_bytes=SCOPE),
        cost_estimate=SMALL,
    )(own, pair, cosine, sine)


def attend_kernel(first, half, own_ref, len_ref, query_ref, key_ref, value_ref, cos_ref, sin_ref, scale_ref, out_ref):
    rows = query_ref.shape[0] // 2
    block_rows = cos_ref.shape[0] // 4
    window = SEG_MOST + rows
    own = own_ref[0]
    for piece in range(2):
        start = pl.multiple_of((own ^ (first + piece)) * block_rows + half * rows, rows)
        here = pl.ds(start, rows)
        key = key_ref[pl.ds(start, window), :]
        value = value_ref[pl.ds(start, window), :]
        query_at = start + lax.broadcasted_iota(jnp.int32, (rows, 1), 0)
        key_at = start - SEG_MOST + lax.broadcasted_iota(jnp.int32, (rows, window), 1)
        begin = jnp.zeros((rows, 1), jnp.int32)
        total = len_ref[0]
        for i in range(1, len_ref.shape[0]):
            begin = jnp.where(query_at >= total, total, begin)
            total = total + len_ref[i]
        allowed = (key_at >= begin) & (key_at <= query_at)
        for head in range(2):
            at = pl.ds(head * HD, HD)
            query = query_ref[pl.ds(piece * rows, rows), at].astype(jnp.float32)
            query = query * cos_ref[here, :] + pltpu.roll(query, HD // 2, 1) * sin_ref[here, :]
            query = query * scale_ref[here, :]
            scores = lax.dot_general(
                query.astype(jnp.bfloat16),
                key,
                (((1,), (1,)), ((), ())),
                preferred_element_type=jnp.float32,
            )
            scores = jnp.where(allowed, scores * (1.0 / math.sqrt(HD)), -1e30)
            weights = jnp.exp(scores - jnp.max(scores, axis=1, keepdims=True))
            weights = jnp.where(allowed, weights, 0.0)
            denominator = jnp.sum(weights, axis=1, keepdims=True)
            added = jnp.dot(weights.astype(jnp.bfloat16), value, preferred_element_type=jnp.float32)
            out_ref[pl.ds(piece * rows, rows), at] = (added / denominator).astype(jnp.bfloat16)


def attend(first, half, own, seg_lengths, query, key, value, cosine, sine, scale):
    rows = query.shape[0]
    vmem = pl.BlockSpec(memory_space=pltpu.VMEM)
    smem = pl.BlockSpec(memory_space=pltpu.SMEM)
    return pl.pallas_call(
        functools.partial(attend_kernel, first, half),
        out_shape=jax.ShapeDtypeStruct(query.shape, jnp.bfloat16),
        in_specs=[smem, smem] + [vmem] * 6,
        out_specs=vmem,
        compiler_params=pltpu.CompilerParams(vmem_limit_bytes=SCOPE),
        cost_estimate=pl.CostEstimate(
            flops=2**31, bytes_accessed=2**20, transcendentals=0
        ),
    )(own, seg_lengths, query, key, value, cosine, sine, scale)


def copy_kernel(place_ref, weight_ref, out_ref):
    del place_ref
    out_ref[...] = weight_ref[...]


def reorder(place, weight):
    blocks = place.shape[0]
    shape = (weight.shape[0] // blocks, weight.shape[1])
    return pl.pallas_call(
        copy_kernel,
        out_shape=jax.ShapeDtypeStruct(weight.shape, jnp.bfloat16),
        grid_spec=pltpu.PrefetchScalarGridSpec(
            num_scalar_prefetch=1,
            grid=(blocks,),
            in_specs=[pl.BlockSpec(shape, lambda j, place: (place[j], 0))],
            out_specs=pl.BlockSpec(shape, lambda j, place: (j, 0)),
        ),
        compiler_params=pltpu.CompilerParams(vmem_limit_bytes=SCOPE),
        cost_estimate=pl.CostEstimate(
            flops=0, bytes_accessed=4 * weight.size, transcendentals=0
        ),
    )(place, weight)


def scale_rows(gain_ref, source_refs, scaled):
    @pl.when(pl.program_id(0) == 0)
    def _():
        at = 0
        for ref in source_refs:
            widened = ref[...].astype(jnp.float32) * gain_ref[...]
            scaled[pl.ds(at, ref.shape[0]), :] = widened.astype(jnp.bfloat16)
            at += ref.shape[0]


def pairs_kernel(place_ref, gain_ref, source_ref, extra_ref, key_ref, value_ref, given_ref, kept_ref, scaled):
    scale_rows(gain_ref, [source_ref], scaled)
    second = place_ref[place_ref.shape[0] - 1] == 1
    for i, ref in enumerate((key_ref, value_ref)):
        product = jnp.dot(scaled[...], ref[...], preferred_element_type=jnp.float32)
        product = product.astype(jnp.bfloat16)
        low, high = product[:, :HD], product[:, HD:]
        rows = low.shape[0]
        kept_ref[:, pl.ds(i * HD, HD)] = jnp.where(second, high, low)
        given_ref[:rows, pl.ds(i * HD, HD)] = jnp.where(second, low, high)
    given_ref[rows:, :] = jnp.zeros((EXTRA, 2 * HD), jnp.bfloat16)
    given_ref[rows:, :HD] = extra_ref[...]


def pairs(place, gain, source, extra, w_key, w_value):
    rows, depth = source.shape
    out = jax.ShapeDtypeStruct((rows, 8 * HD), jnp.bfloat16)
    picked = pl.BlockSpec((depth, 2 * HD), lambda j, place: (0, place[j]))
    given = jax.ShapeDtypeStruct((rows + EXTRA, 8 * HD), jnp.bfloat16)
    return pl.pallas_call(
        pairs_kernel,
        out_shape=[given, out],
        grid_spec=pltpu.PrefetchScalarGridSpec(
            num_scalar_prefetch=1,
            grid=(4,),
            in_specs=[
                pl.BlockSpec((1, depth), lambda j, place: (0, 0)),
                pl.BlockSpec((rows, depth), lambda j, place: (0, 0)),
                pl.BlockSpec((EXTRA, HD), lambda j, place: (0, 0)),
                picked,
                picked,
            ],
            out_specs=[
                pl.BlockSpec((rows + EXTRA, 2 * HD), lambda j, place: (0, j)),
                pl.BlockSpec((rows, 2 * HD), lambda j, place: (0, j)),
            ],
            scratch_shapes=[pltpu.VMEM((rows, depth), jnp.bfloat16)],
        ),
        compiler_params=pltpu.CompilerParams(vmem_limit_bytes=SCOPE),
        cost_estimate=pl.CostEstimate(
            flops=4 * rows * depth * 8 * HD, bytes_accessed=4 * depth * 8 * HD, transcendentals=0
        ),
    )(place, gain[None, :], source, extra, w_key, w_value)


def project_kernel(pieces, place_ref, gain_ref, *refs):
    weight_ref, out_ref, scaled = refs[pieces:]
    scale_rows(gain_ref, refs[:pieces], scaled)
    product = jnp.dot(scaled[...], weight_ref[...], preferred_element_type=jnp.float32)
    out_ref[...] = product.astype(jnp.bfloat16)


def project(place, gain, pieces, weight, size):
    piece_rows, depth = pieces[0].shape
    rows, width = len(pieces) * piece_rows, size * place.shape[0]
    return pl.pallas_call(
        functools.partial(project_kernel, len(pieces)),
        out_shape=jax.ShapeDtypeStruct((rows, width), jnp.bfloat16),
        grid_spec=pltpu.PrefetchScalarGridSpec(
            num_scalar_prefetch=1,
            grid=(place.shape[0],),
            in_specs=[pl.BlockSpec((1, depth), lambda j, place: (0, 0))]
            + [pl.BlockSpec((piece_rows, depth), lambda j, place: (0, 0))] * len(pieces)
            + [pl.BlockSpec((depth, size), lambda j, place: (0, place[j]))],
            out_specs=pl.BlockSpec((rows, size), lambda j, place: (0, j)),
            scratch_shapes=[pltpu.VMEM((rows, depth), jnp.bfloat16)],
        ),
        compiler_params=pltpu.CompilerParams(vmem_limit_bytes=SCOPE),
        cost_estimate=pl.CostEstimate(
            flops=2 * rows * depth * width,
            bytes_accessed=2 * (rows * depth + (depth + rows) * width),
            transcendentals=0,
        ),
    )(place, gain[None, :], *pieces, weight)


def shards_8x4(hidden_in, norm_gain, w_query, w_key, w_value, w_out, seg_lengths):
    f32, bf16 = jnp.float32, jnp.bfloat16
    rows, width = hidden_in.shape
    model_width = width * lax.axis_size("gx")
    tokens = rows * lax.axis_size("gy")
    cols = w_query.shape[1]
    half_rows, piece, pair_cols = rows // 2, cols // 8, 2 * HD
    gx, gy = lax.axis_index("gx"), lax.axis_index("gy")
    x_at, z_low, z_high = [b.astype(jnp.int32) for b in (gx & 1, (gx >> 1) & 1, gx >> 2)]
    rank = (x_at * 4 + z_low * 2 + z_high).astype(jnp.int32)
    z_at = z_low * 2 + z_high
    own = gy.astype(jnp.int32)[None]
    order = jnp.arange(4, dtype=jnp.int32)

    widened = hidden_in.astype(f32)
    squares = jnp.sum(widened * widened, axis=1).reshape(rows // HD, HD)
    squares = jnp.pad(squares, ((0, EXTRA // 2 - rows // HD), (0, 0)))
    high = lax.reduce_precision(squares, 8, 7)
    extra = jnp.concatenate([high, squares - high], axis=0).astype(bf16)

    parts = {}
    for h in range(2):
        parts[0, h] = hidden_in[h * half_rows : (h + 1) * half_rows]
        parts[1, h] = swap(parts[0, h], "gy", 1)
    parts[2, 0] = swap(parts[0, 0], "gy", 2)

    x_served = []

    def swap_x(value):
        if x_served:
            value = after(value, x_served[-1])
        x_served.append(swap(value, "gx", 1))
        return x_served[-1]

    def project_half(h, blocks, *others):
        picked = [parts[i, h] for i in range(4)]
        return project(after(rank ^ blocks, *others), norm_gain, picked, w_query, piece)

    place = jnp.concatenate([gy ^ order, x_at[None]]).astype(jnp.int32)
    given, kept_pair = pairs(place, norm_gain, hidden_in, extra, w_key, w_value)
    parts[2, 0] = after(parts[2, 0], given)
    parts[3, 0] = swap(parts[2, 0], "gy", 1)
    parts[2, 1] = swap(parts[0, 1], "gy", 2)
    cross = project_half(0, order + 4, given)
    given = swap_x(given)
    crossed_in, keeps = {0: swap_x(cross)}, {}
    given, pair, squares = merge(True, z_low[None], after(kept_pair, cross), given, squares)
    parts[2, 1] = after(parts[2, 1], given)
    parts[3, 1] = swap(parts[2, 1], "gy", 1)
    keeps[0] = project_half(0, order, given)
    pair = after(pair, keeps[0])
    given, pair, squares = merge(True, z_high[None], pair, swap(given, "gx", 2), squares)
    cross = project_half(1, order + 4, given)
    (pair,) = merge(False, z_high[None], after(pair, cross), swap(given, "gx", 4), squares)
    across = []
    for i in range(8):
        for j in range(4):
            across.append((i * 4 + j, i * 4 + (j ^ ((i >> 1) & 1) * 2 ^ (i >> 2))))
    pair = lax.ppermute(pair, ("gx", "gy"), across)
    pair = jnp.concatenate([pair, swap(pair, "gx", 4)], axis=0)
    keeps[1] = project_half(1, order, cross, pair)
    pair = jnp.concatenate([pair, swap(pair, "gx", 2)], axis=0)
    crossed_in = {(0, 0): crossed_in[0][:rows], (2, 0): crossed_in[0][rows:]}
    crossed_in[2, 1] = swap_x(cross[rows:])
    crossed_in[0, 1] = swap_x(cross[:rows])

    _, position = segment_table(seg_lengths, tokens)
    lane = jnp.arange(HD, dtype=jnp.int32)
    exponent = (lane % (HD // 2)).astype(f32) * (2.0 / HD)
    angle = position.astype(f32)[:, None] * (ROPE_BASE ** (-exponent))[None, :]
    cosine = jnp.cos(angle)
    sine = jnp.where(lane < HD // 2, -1.0, 1.0)[None, :] * jnp.sin(angle)
    key, value, scale = prepare(model_width, own ^ z_at, pair, cosine, sine)

    served, halved, attended, gathered = [], {}, {}, {}

    def queries(first, h, *others):
        at = slice(first // 2 * rows, (first // 2 + 1) * rows)
        keep, cross = keeps[h][at], crossed_in[first, h]
        low = (keep[:, 2 * piece :].astype(f32) + cross[:, 2 * piece :].astype(f32)).astype(bf16)
        if served:
            low = after(low, served[-1], *others)
        got = swap(low, "gx", 2)
        served.append(got)
        near = keep[:, : 2 * piece].astype(f32) + cross[:, : 2 * piece].astype(f32)
        high = near[:, piece:] + got[:, piece:].astype(f32)
        near = near[:, :piece] + got[:, :piece].astype(f32)
        halved[first, h] = near, swap(high.astype(bf16), "gx", 4)

    def attend_chunk(first, h, *others):
        near, got = halved[first, h]
        query = (near + got.astype(f32)).astype(bf16)
        if others:
            query = after(query, *others)
        attended[first, h] = attend(first, h, own, seg_lengths, query, key, value, cosine, sine, scale)

    def gather_z(first, h):
        a = attended[first, h]
        a = jnp.concatenate([a, swap(a, "gx", 4)], axis=1)
        gathered[first, h] = jnp.concatenate([a, swap(a, "gx", 2)], axis=1)

    queries(0, 0)
    queries(2, 0)
    attend_chunk(0, 0)
    gather_z(0, 0)
    attend_chunk(2, 0)
    queries(2, 1)
    x_served[-1] = crossed_in[0, 1] = after(crossed_in[0, 1], attended[0, 0], attended[2, 0])
    queries(0, 1, gathered[0, 0])
    gather_z(2, 0)
    crossed_out = {(0, 0): swap_x(gathered[0, 0])}
    attend_chunk(2, 1, crossed_out[0, 0])
    attend_chunk(0, 1)
    gather_z(2, 1)
    gather_z(0, 1)

    w_rows = reorder(after(rank ^ jnp.arange(8, dtype=jnp.int32), crossed_in[0, 1]), w_out)
    kept, crossed, crossed_given = {}, {}, {}
    for first, h in ((0, 0), (2, 0), (2, 1), (0, 1)):
        a = gathered[first, h]
        if (first, h) == (0, 1):
            a = after(a, crossed_given[0])
        got = crossed_out[first, h] if (first, h) in crossed_out else swap_x(a)
        a = jnp.concatenate([a, got], axis=1)
        given = jnp.dot(a[half_rows:], w_rows, preferred_element_type=f32).astype(bf16)
        a = a[:half_rows]
        if h == 1:
            a = after(a, crossed[1 - first // 2])
        mine = jnp.dot(a, w_rows, preferred_element_type=f32)
        mine = mine + swap(given, "gy", 1).astype(f32)
        if first:
            crossed_given[h] = mine.astype(bf16)
            crossed[h] = swap(crossed_given[h], "gy", 2)
        else:
            kept[h] = mine
    return jnp.concatenate(
        [(kept[h] + crossed[h].astype(f32)).astype(bf16) for h in range(2)], axis=0
    )


def shards(hidden_in, norm_gain, w_query, w_key, w_value, w_out, seg_lengths):
    split = (lax.axis_size("gx"), lax.axis_size("gy"))
    body = shards_8x4 if split == (8, 4) else shards_any
    return body(hidden_in, norm_gain, w_query, w_key, w_value, w_out, seg_lengths)


def solution(mesh):
    in_specs = (
        P("gy", "gx"),
        P("gx"),
        P("gx", "gy"),
        P("gx", None),
        P("gx", None),
        P("gy", "gx"),
        P(),
    )
    out_specs = P("gy", "gx")
    return jax.shard_map(shards, mesh=mesh, in_specs=in_specs, out_specs=out_specs, check_vma=False)
```

```python
import functools
import math

import jax
import jax.numpy as jnp
from jax import lax
from jax.experimental import pallas as pl
from jax.experimental.pallas import tpu as pltpu
from jax.sharding import PartitionSpec as P

H = 64
KVH = 8
HD = 128


ROPE_BASE = 500000.0
EPS = 1e-05
SEG_MOST = 512


def rotate(values, position, head_size):
    half = head_size // 2
    exponent = jnp.arange(half, dtype=jnp.float32) * (2.0 / head_size)
    frequency = ROPE_BASE ** (-exponent)
    angle = position[:, None, None] * frequency[None, None, :]
    cosine = jnp.cos(angle)
    sine = jnp.sin(angle)
    first = values[..., :half]
    second = values[..., half:]
    return jnp.concatenate(
        [first * cosine - second * sine, second * cosine + first * sine], axis=-1
    )


def segment_table(seg_lengths, tokens):
    ends = jnp.cumsum(seg_lengths)
    starts = ends - seg_lengths
    index = jnp.arange(tokens, dtype=jnp.int32)
    member = ((index[:, None] >= starts[None, :]) & (index[:, None] < ends[None, :])).astype(
        jnp.int32
    )
    seg_id = jnp.sum(member * jnp.arange(seg_lengths.shape[0], dtype=jnp.int32)[None, :], axis=1)
    first_index = jnp.sum(member * starts[None, :], axis=1)
    return (seg_id, index - first_index)


def normalize(block, gain, squares, model_width):
    widened = block.astype(jnp.float32)
    scale = lax.rsqrt(squares / model_width + EPS)
    return (widened * scale[:, None] * gain[None, :]).astype(jnp.bfloat16)


def shards_any(hidden_in, norm_gain, w_query, w_key, w_value, w_out, seg_lengths):
    rows_own, width = hidden_in.shape
    model_width = width * lax.axis_size("gx")
    tokens = rows_own * lax.axis_size("gy")
    query_rows = tokens // lax.axis_size("gx")
    widened = hidden_in.astype(jnp.float32)
    squares = lax.psum(jnp.sum(widened * widened, axis=1), "gx")
    source = normalize(hidden_in, norm_gain, squares, model_width)
    gathered = lax.all_gather(source, "gy", axis=0, tiled=True)
    query_cols = w_query.shape[1]
    heads_local = query_cols // HD
    group = H // KVH
    kv_local = max(1, heads_local // group)
    pair_cols = kv_local * HD
    first_head = lax.axis_index("gy") * heads_local // group
    key_own = lax.dynamic_slice_in_dim(w_key, first_head * HD, pair_cols, 1)
    value_own = lax.dynamic_slice_in_dim(w_value, first_head * HD, pair_cols, 1)
    seg_id, position = segment_table(seg_lengths, tokens)
    here = lax.axis_index("gx") * query_rows
    query_seg = lax.dynamic_slice_in_dim(seg_id, here, query_rows)
    query_pos = lax.dynamic_slice_in_dim(position, here, query_rows)
    query_index = here + jnp.arange(query_rows, dtype=jnp.int32)
    query_sum = lax.psum_scatter(
        jnp.dot(gathered, w_query, preferred_element_type=jnp.float32).astype(jnp.bfloat16),
        "gx",
        scatter_dimension=0,
        tiled=True,
    ).astype(jnp.float32)
    pair_part = jnp.concatenate(
        [
            jnp.dot(gathered, key_own, preferred_element_type=jnp.float32),
            jnp.dot(gathered, value_own, preferred_element_type=jnp.float32),
        ],
        axis=1,
    )
    pair_sum = lax.psum(pair_part.astype(jnp.bfloat16), "gx").astype(jnp.float32)
    key_raw = pair_sum[:, :pair_cols].astype(jnp.bfloat16)
    value_raw = pair_sum[:, pair_cols:].astype(jnp.bfloat16)
    group_local = heads_local // kv_local
    queries = rotate(
        query_sum.reshape(query_rows, heads_local, HD), query_pos.astype(jnp.float32), HD
    ).astype(jnp.bfloat16)
    queries = queries.reshape(query_rows, kv_local, group_local, HD)
    key_count = key_raw.shape[0]
    keys = rotate(
        key_raw.astype(jnp.float32).reshape(key_count, kv_local, HD),
        position.astype(jnp.float32),
        HD,
    )
    keys = keys.astype(jnp.bfloat16).reshape(key_count, pair_cols)
    score_scale = 1.0 / math.sqrt(HD)
    running = jnp.full((kv_local, group_local, query_rows), -1e30, jnp.float32)
    count = keys.shape[0]
    key_index = jnp.arange(count, dtype=jnp.int32)
    allowed = (query_seg[:, None] == seg_id[None, :]) & (key_index[None, :] <= query_index[:, None])
    key_heads = keys.reshape(count, kv_local, HD)
    value_heads = value_raw.reshape(count, kv_local, HD)
    scores = (
        jnp.einsum("rkgd,nkd->kgrn", queries, key_heads, preferred_element_type=jnp.float32)
        * score_scale
    )
    scores = jnp.where(allowed[None, None], scores, -1e30)
    newest = jnp.maximum(running, jnp.max(scores, axis=-1))
    weights = jnp.where(allowed[None, None], jnp.exp(scores - newest[..., None]), 0.0)
    denominator = jnp.sum(weights, axis=-1)
    added = jnp.einsum(
        "kgrn,nkd->rkgd",
        weights.astype(jnp.bfloat16),
        value_heads,
        preferred_element_type=jnp.float32,
    )
    accum = added
    running, denominator, accum = (newest, denominator, accum)
    attended = (
        (accum / denominator.transpose(2, 0, 1)[..., None])
        .reshape(query_rows, query_cols)
        .astype(jnp.bfloat16)
    )
    partial_out = jnp.dot(
        lax.all_gather(attended, "gx", axis=0, tiled=True),
        w_out,
        preferred_element_type=jnp.float32,
    )
    return lax.psum_scatter(partial_out.astype(jnp.bfloat16), "gy", scatter_dimension=0, tiled=True)


SCOPE = 24 * 2**20
EXTRA = 16
SMALL = pl.CostEstimate(flops=0, bytes_accessed=0, transcendentals=0)


def swap(value, axis, bit):
    return lax.ppermute(value, axis, [(i, i ^ bit) for i in range(lax.axis_size(axis))])


def columns(array, start, size):
    return lax.dynamic_slice_in_dim(array, start, size, 1)


def after(value, *others):
    hbm = pl.BlockSpec(memory_space=pl.ANY)
    return pl.pallas_call(
        lambda *refs: None,
        out_shape=jax.ShapeDtypeStruct(value.shape, value.dtype),
        in_specs=[hbm] * (1 + len(others)),
        out_specs=hbm,
        input_output_aliases={0: 0},
        cost_estimate=SMALL,
    )(value, *others)


def merge_kernel(split, at_ref, kept_ref, got_ref, squares_ref, *out_refs):
    rows = kept_ref.shape[0]
    arrived = got_ref[rows:, :HD].astype(jnp.float32)
    squares = squares_ref[...] + arrived[: EXTRA // 2] + arrived[EXTRA // 2 :]
    high = squares.astype(jnp.bfloat16).astype(jnp.float32)
    given_ref = out_refs[0]
    width = given_ref.shape[1]
    given_ref[rows:, :] = jnp.zeros((EXTRA, width), jnp.bfloat16)
    given_ref[rows:, :HD] = jnp.concatenate([high, squares - high], axis=0).astype(jnp.bfloat16)
    side = at_ref[0] if split else 1
    for i in range(1 + split):
        ref, at = out_refs[i], side if i else 1 - side
        at = pl.ds(pl.multiple_of(at * width, width), width) if split else slice(None)
        total = kept_ref[:, at].astype(jnp.float32) + got_ref[:rows, at].astype(jnp.float32)
        ref[:rows, :] = total.astype(jnp.bfloat16)
    if split:
        out_refs[2][...] = squares


def merge(split, side, kept, got, squares):
    rows, width = kept.shape
    vmem = pl.BlockSpec(memory_space=pltpu.VMEM)
    outs = [jax.ShapeDtypeStruct((rows + EXTRA, width // (1 + split)), jnp.bfloat16)]
    if split:
        outs.append(jax.ShapeDtypeStruct((rows, width // 2), jnp.bfloat16))
        outs.append(jax.ShapeDtypeStruct(squares.shape, jnp.float32))
    return pl.pallas_call(
        functools.partial(merge_kernel, split),
        out_shape=outs,
        in_specs=[pl.BlockSpec(memory_space=pltpu.SMEM)] + [vmem] * 3,
        out_specs=[vmem] * len(outs),
        compiler_params=pltpu.CompilerParams(vmem_limit_bytes=SCOPE),
        cost_estimate=SMALL,
    )(side, kept, got, squares)


def prepare_kernel(model_width, own_ref, pair_ref, cos_ref, sin_ref, key_ref, value_ref, scale_ref):
    blocks = 4
    held = pair_ref.shape[0] // blocks
    rows = held - EXTRA
    own = own_ref[0]
    key_ref[:SEG_MOST, :] = jnp.zeros((SEG_MOST, HD), jnp.bfloat16)
    value_ref[:SEG_MOST, :] = jnp.zeros((SEG_MOST, HD), jnp.bfloat16)
    for block in range(blocks):
        start = pl.multiple_of((block ^ own) * held, EXTRA)
        squares = pair_ref[pl.ds(pl.multiple_of(start + rows, EXTRA), EXTRA), :HD]
        squares = squares.astype(jnp.float32)
        squares = squares[: EXTRA // 2] + squares[EXTRA // 2 :]
        inverse = lax.rsqrt(squares / model_width + EPS)
        for i in range(rows // HD):
            here = pl.ds(block * rows + i * HD, HD)
            scale_ref[here, :] = jnp.transpose(jnp.broadcast_to(inverse[i : i + 1, :], (HD, HD)))
        here = pl.ds(block * rows, rows)
        there = pl.ds(SEG_MOST + block * rows, rows)
        key = pair_ref[pl.ds(start, rows), :HD].astype(jnp.float32)
        value = pair_ref[pl.ds(start, rows), HD:].astype(jnp.float32)
        key = key * cos_ref[here, :] + pltpu.roll(key, HD // 2, 1) * sin_ref[here, :]
        key_ref[there, :] = (key * scale_ref[here, :]).astype(jnp.bfloat16)
        value_ref[there, :] = (value * scale_ref[here, :]).astype(jnp.bfloat16)


def prepare(model_width, own, pair, cosine, sine):
    tokens = cosine.shape[0]
    padded = jax.ShapeDtypeStruct((SEG_MOST + tokens, HD), jnp.bfloat16)
    vmem = pl.BlockSpec(memory_space=pltpu.VMEM)
    return pl.pallas_call(
        functools.partial(prepare_kernel, model_width),
        out_shape=[padded, padded, jax.ShapeDtypeStruct((tokens, HD), jnp.float32)],
        in_specs=[pl.BlockSpec(memory_space=pltpu.SMEM)] + [vmem] * 3,
        out_specs=[vmem] * 3,
        compiler_params=pltpu.CompilerParams(vmem_limit_bytes=SCOPE),
        cost_estimate=SMALL,
    )(own, pair, cosine, sine)


def attend_kernel(first, half, own_ref, len_ref, query_ref, key_ref, value_ref, cos_ref, sin_ref, scale_ref, out_ref):
    rows = query_ref.shape[0] // 2
    block_rows = cos_ref.shape[0] // 4
    window = SEG_MOST + rows
    own = own_ref[0]
    for piece in range(2):
        start = pl.multiple_of((own ^ (first + piece)) * block_rows + half * rows, rows)
        here = pl.ds(start, rows)
        key = key_ref[pl.ds(start, window), :]
        value = value_ref[pl.ds(start, window), :]
        query_at = start + lax.broadcasted_iota(jnp.int32, (rows, 1), 0)
        key_at = start - SEG_MOST + lax.broadcasted_iota(jnp.int32, (rows, window), 1)
        begin = jnp.zeros((rows, 1), jnp.int32)
        total = len_ref[0]
        for i in range(1, len_ref.shape[0]):
            begin = jnp.where(query_at >= total, total, begin)
            total = total + len_ref[i]
        allowed = (key_at >= begin) & (key_at <= query_at)
        for head in range(2):
            at = pl.ds(head * HD, HD)
            query = query_ref[pl.ds(piece * rows, rows), at].astype(jnp.float32)
            query = query * cos_ref[here, :] + pltpu.roll(query, HD // 2, 1) * sin_ref[here, :]
            query = query * scale_ref[here, :]
            scores = lax.dot_general(
                query.astype(jnp.bfloat16),
                key,
                (((1,), (1,)), ((), ())),
                preferred_element_type=jnp.float32,
            )
            scores = jnp.where(allowed, scores * (1.0 / math.sqrt(HD)), -1e30)
            weights = jnp.exp(scores - jnp.max(scores, axis=1, keepdims=True))
            weights = jnp.where(allowed, weights, 0.0)
            denominator = jnp.sum(weights, axis=1, keepdims=True)
            added = jnp.dot(weights.astype(jnp.bfloat16), value, preferred_element_type=jnp.float32)
            out_ref[pl.ds(piece * rows, rows), at] = (added / denominator).astype(jnp.bfloat16)


def attend(first, half, own, seg_lengths, query, key, value, cosine, sine, scale):
    rows = query.shape[0]
    vmem = pl.BlockSpec(memory_space=pltpu.VMEM)
    smem = pl.BlockSpec(memory_space=pltpu.SMEM)
    return pl.pallas_call(
        functools.partial(attend_kernel, first, half),
        out_shape=jax.ShapeDtypeStruct(query.shape, jnp.bfloat16),
        in_specs=[smem, smem] + [vmem] * 6,
        out_specs=vmem,
        compiler_params=pltpu.CompilerParams(vmem_limit_bytes=SCOPE),
        cost_estimate=pl.CostEstimate(
            flops=2**31, bytes_accessed=2**20, transcendentals=0
        ),
    )(own, seg_lengths, query, key, value, cosine, sine, scale)


def copy_kernel(place_ref, weight_ref, out_ref):
    del place_ref
    out_ref[...] = weight_ref[...]


def reorder(place, weight):
    blocks = place.shape[0]
    shape = (weight.shape[0] // blocks, weight.shape[1])
    return pl.pallas_call(
        copy_kernel,
        out_shape=jax.ShapeDtypeStruct(weight.shape, jnp.bfloat16),
        grid_spec=pltpu.PrefetchScalarGridSpec(
            num_scalar_prefetch=1,
            grid=(blocks,),
            in_specs=[pl.BlockSpec(shape, lambda j, place: (place[j], 0))],
            out_specs=pl.BlockSpec(shape, lambda j, place: (j, 0)),
        ),
        compiler_params=pltpu.CompilerParams(vmem_limit_bytes=SCOPE),
        cost_estimate=pl.CostEstimate(
            flops=0, bytes_accessed=4 * weight.size, transcendentals=0
        ),
    )(place, weight)


def scale_rows(gain_ref, source_refs, scaled):
    @pl.when(pl.program_id(0) == 0)
    def _():
        at = 0
        for ref in source_refs:
            widened = ref[...].astype(jnp.float32) * gain_ref[...]
            scaled[pl.ds(at, ref.shape[0]), :] = widened.astype(jnp.bfloat16)
            at += ref.shape[0]


def pairs_kernel(place_ref, gain_ref, source_ref, extra_ref, key_ref, value_ref, given_ref, kept_ref, scaled):
    scale_rows(gain_ref, [source_ref], scaled)
    second = place_ref[place_ref.shape[0] - 1] == 1
    for i, ref in enumerate((key_ref, value_ref)):
        product = jnp.dot(scaled[...], ref[...], preferred_element_type=jnp.float32)
        product = product.astype(jnp.bfloat16)
        low, high = product[:, :HD], product[:, HD:]
        rows = low.shape[0]
        kept_ref[:, pl.ds(i * HD, HD)] = jnp.where(second, high, low)
        given_ref[:rows, pl.ds(i * HD, HD)] = jnp.where(second, low, high)
    given_ref[rows:, :] = jnp.zeros((EXTRA, 2 * HD), jnp.bfloat16)
    given_ref[rows:, :HD] = extra_ref[...]


def pairs(place, gain, source, extra, w_key, w_value):
    rows, depth = source.shape
    out = jax.ShapeDtypeStruct((rows, 8 * HD), jnp.bfloat16)
    picked = pl.BlockSpec((depth, 2 * HD), lambda j, place: (0, place[j]))
    given = jax.ShapeDtypeStruct((rows + EXTRA, 8 * HD), jnp.bfloat16)
    return pl.pallas_call(
        pairs_kernel,
        out_shape=[given, out],
        grid_spec=pltpu.PrefetchScalarGridSpec(
            num_scalar_prefetch=1,
            grid=(4,),
            in_specs=[
                pl.BlockSpec((1, depth), lambda j, place: (0, 0)),
                pl.BlockSpec((rows, depth), lambda j, place: (0, 0)),
                pl.BlockSpec((EXTRA, HD), lambda j, place: (0, 0)),
                picked,
                picked,
            ],
            out_specs=[
                pl.BlockSpec((rows + EXTRA, 2 * HD), lambda j, place: (0, j)),
                pl.BlockSpec((rows, 2 * HD), lambda j, place: (0, j)),
            ],
            scratch_shapes=[pltpu.VMEM((rows, depth), jnp.bfloat16)],
        ),
        compiler_params=pltpu.CompilerParams(vmem_limit_bytes=SCOPE),
        cost_estimate=pl.CostEstimate(
            flops=4 * rows * depth * 8 * HD, bytes_accessed=4 * depth * 8 * HD, transcendentals=0
        ),
    )(place, gain[None, :], source, extra, w_key, w_value)


def project_kernel(pieces, place_ref, gain_ref, *refs):
    weight_ref, out_ref, scaled = refs[pieces:]
    scale_rows(gain_ref, refs[:pieces], scaled)
    product = jnp.dot(scaled[...], weight_ref[...], preferred_element_type=jnp.float32)
    out_ref[...] = product.astype(jnp.bfloat16)


def project(place, gain, pieces, weight, size):
    piece_rows, depth = pieces[0].shape
    rows, width = len(pieces) * piece_rows, size * place.shape[0]
    return pl.pallas_call(
        functools.partial(project_kernel, len(pieces)),
        out_shape=jax.ShapeDtypeStruct((rows, width), jnp.bfloat16),
        grid_spec=pltpu.PrefetchScalarGridSpec(
            num_scalar_prefetch=1,
            grid=(place.shape[0],),
            in_specs=[pl.BlockSpec((1, depth), lambda j, place: (0, 0))]
            + [pl.BlockSpec((piece_rows, depth), lambda j, place: (0, 0))] * len(pieces)
            + [pl.BlockSpec((depth, size), lambda j, place: (0, place[j]))],
            out_specs=pl.BlockSpec((rows, size), lambda j, place: (0, j)),
            scratch_shapes=[pltpu.VMEM((rows, depth), jnp.bfloat16)],
        ),
        compiler_params=pltpu.CompilerParams(vmem_limit_bytes=SCOPE),
        cost_estimate=pl.CostEstimate(
            flops=2 * rows * depth * width,
            bytes_accessed=2 * (rows * depth + (depth + rows) * width),
            transcendentals=0,
        ),
    )(place, gain[None, :], *pieces, weight)


def shards_8x4(hidden_in, norm_gain, w_query, w_key, w_value, w_out, seg_lengths):
    f32, bf16 = jnp.float32, jnp.bfloat16
    rows, width = hidden_in.shape
    model_width = width * lax.axis_size("gx")
    tokens = rows * lax.axis_size("gy")
    cols = w_query.shape[1]
    half_rows, piece, pair_cols = rows // 2, cols // 8, 2 * HD
    gx, gy = lax.axis_index("gx"), lax.axis_index("gy")
    x_at, z_low, z_high = [b.astype(jnp.int32) for b in (gx & 1, (gx >> 1) & 1, gx >> 2)]
    rank = (x_at * 4 + z_low * 2 + z_high).astype(jnp.int32)
    z_at = z_low * 2 + z_high
    own = gy.astype(jnp.int32)[None]
    order = jnp.arange(4, dtype=jnp.int32)

    widened = hidden_in.astype(f32)
    squares = jnp.sum(widened * widened, axis=1).reshape(rows // HD, HD)
    squares = jnp.pad(squares, ((0, EXTRA // 2 - rows // HD), (0, 0)))
    high = lax.reduce_precision(squares, 8, 7)
    extra = jnp.concatenate([high, squares - high], axis=0).astype(bf16)

    parts = {}
    for h in range(2):
        parts[0, h] = hidden_in[h * half_rows : (h + 1) * half_rows]
        parts[1, h] = swap(parts[0, h], "gy", 1)
    parts[2, 0] = swap(parts[0, 0], "gy", 2)

    x_served = []

    def swap_x(value, *others):
        if x_served:
            value = after(value, x_served[-1], *others)
        x_served.append(swap(value, "gx", 1))
        return x_served[-1]

    def project_half(h, blocks, *others):
        picked = [parts[i, h] for i in range(4)]
        return project(after(rank ^ blocks, *others), norm_gain, picked, w_query, piece)

    place = jnp.concatenate([gy ^ order, x_at[None]]).astype(jnp.int32)
    given, kept_pair = pairs(place, norm_gain, hidden_in, extra, w_key, w_value)
    parts[2, 0] = after(parts[2, 0], given)
    parts[3, 0] = swap(parts[2, 0], "gy", 1)
    parts[2, 1] = swap(parts[0, 1], "gy", 2)
    cross = project_half(0, order + 4, given)
    given = swap_x(given)
    crossed_in, keeps = {}, {}
    crossed_in[0, 0] = swap_x(cross[:rows])
    next_cross = cross[rows:]
    given, pair, squares = merge(True, z_low[None], after(kept_pair, cross), given, squares)
    parts[2, 1] = after(parts[2, 1], given)
    parts[3, 1] = swap(parts[2, 1], "gy", 1)
    keeps[0] = project_half(0, order, given)
    crossed_in[2, 0] = swap_x(next_cross, keeps[0])
    pair = after(pair, keeps[0])
    given, pair, squares = merge(True, z_high[None], pair, swap(given, "gx", 2), squares)
    cross = project_half(1, order + 4, given)
    (pair,) = merge(False, z_high[None], after(pair, cross), swap(given, "gx", 4), squares)
    across = []
    for i in range(8):
        for j in range(4):
            across.append((i * 4 + j, i * 4 + (j ^ ((i >> 1) & 1) * 2 ^ (i >> 2))))
    pair = lax.ppermute(pair, ("gx", "gy"), across)
    pair = jnp.concatenate([pair, swap(pair, "gx", 4)], axis=0)
    keeps[1] = project_half(1, order, cross, pair)
    pair = jnp.concatenate([pair, swap(pair, "gx", 2)], axis=0)
    crossed_in[2, 1] = swap_x(cross[rows:])
    crossed_in[0, 1] = swap_x(cross[:rows])

    _, position = segment_table(seg_lengths, tokens)
    lane = jnp.arange(HD, dtype=jnp.int32)
    exponent = (lane % (HD // 2)).astype(f32) * (2.0 / HD)
    angle = position.astype(f32)[:, None] * (ROPE_BASE ** (-exponent))[None, :]
    cosine = jnp.cos(angle)
    sine = jnp.where(lane < HD // 2, -1.0, 1.0)[None, :] * jnp.sin(angle)
    key, value, scale = prepare(model_width, own ^ z_at, pair, cosine, sine)

    served, sums, halved, attended, shared, gathered = [], {}, {}, {}, {}, {}

    def halve_near(first, h, *others):
        at = slice(first // 2 * rows, (first // 2 + 1) * rows)
        keep, cross = keeps[h][at], crossed_in[first, h]
        low = (keep[:, 2 * piece :].astype(f32) + cross[:, 2 * piece :].astype(f32)).astype(bf16)
        if served:
            low = after(low, served[-1], *others)
        served.append(swap(low, "gx", 2))
        near = keep[:, : 2 * piece].astype(f32) + cross[:, : 2 * piece].astype(f32)
        sums[first, h] = near, served[-1]

    def halve_far(first, h, *others):
        near, got = sums[first, h]
        if others:
            got = after(got, *others)
        high = near[:, piece:] + got[:, piece:].astype(f32)
        near = near[:, :piece] + got[:, :piece].astype(f32)
        halved[first, h] = near, swap(high.astype(bf16), "gx", 4)

    def attend_chunk(first, h, *others):
        near, got = halved[first, h]
        query = (near + got.astype(f32)).astype(bf16)
        if others:
            query = after(query, *others)
        attended[first, h] = attend(first, h, own, seg_lengths, query, key, value, cosine, sine, scale)

    def gather_z(first, h):
        a = attended[first, h]
        shared[first, h] = swap(a, "gx", 4)
        a = jnp.concatenate([a, shared[first, h]], axis=1)
        gathered[first, h] = jnp.concatenate([a, swap(a, "gx", 2)], axis=1)

    for first in (0, 2):
        halve_near(first, 0)
        halve_far(first, 0)
        attend_chunk(first, 0)
        gather_z(first, 0)
    halve_near(2, 1)
    x_served[-1] = crossed_in[0, 1] = after(crossed_in[0, 1], shared[0, 0], shared[2, 0])
    w_rows = reorder(after(rank ^ jnp.arange(8, dtype=jnp.int32), crossed_in[0, 1]), w_out)
    leaving = after(gathered[0, 0], x_served[-1])
    crossed_out = {(0, 0): swap(leaving, "gx", 1)}
    x_served.append(crossed_out[0, 0])
    halve_far(2, 1, leaving)
    halve_near(0, 1, leaving)
    halve_far(0, 1, w_rows)
    attend_chunk(2, 1, crossed_out[0, 0])
    attend_chunk(0, 1)
    gather_z(2, 1)
    gather_z(0, 1)
    kept, crossed, crossed_given = {}, {}, {}
    for first, h in ((0, 0), (2, 0), (2, 1), (0, 1)):
        if (first, h) in crossed_out:
            a, got = leaving, crossed_out[first, h]
        else:
            others = [crossed_given[0]] if (first, h) == (0, 1) else []
            a = after(gathered[first, h], x_served[-1], *others)
            got = swap(a, "gx", 1)
            x_served.append(got)
        if (first, h) == (0, 1):
            got = after(got, crossed_given[1])
        a = jnp.concatenate([a, got], axis=1)
        given = jnp.dot(a[half_rows:], w_rows, preferred_element_type=f32).astype(bf16)
        a = a[:half_rows]
        if (first, h) == (0, 1):
            a = after(a, crossed[1])
        mine = jnp.dot(a, w_rows, preferred_element_type=f32)
        mine = mine + swap(given, "gy", 1).astype(f32)
        if first:
            crossed_given[h] = mine.astype(bf16)
            crossed[h] = swap(crossed_given[h], "gy", 2)
        else:
            kept[h] = mine
    return jnp.concatenate(
        [(kept[h] + crossed[h].astype(f32)).astype(bf16) for h in range(2)], axis=0
    )


def shards(hidden_in, norm_gain, w_query, w_key, w_value, w_out, seg_lengths):
    split = (lax.axis_size("gx"), lax.axis_size("gy"))
    body = shards_8x4 if split == (8, 4) else shards_any
    return body(hidden_in, norm_gain, w_query, w_key, w_value, w_out, seg_lengths)


def solution(mesh):
    in_specs = (
        P("gy", "gx"),
        P("gx"),
        P("gx", "gy"),
        P("gx", None),
        P("gx", None),
        P("gy", "gx"),
        P(),
    )
    out_specs = P("gy", "gx")
    return jax.shard_map(shards, mesh=mesh, in_specs=in_specs, out_specs=out_specs, check_vma=False)
```

```python
import functools
import math

import jax
import jax.numpy as jnp
from jax import lax
from jax.experimental import pallas as pl
from jax.experimental.pallas import tpu as pltpu
from jax.sharding import PartitionSpec as P

H = 64
KVH = 8
HD = 128


ROPE_BASE = 500000.0
EPS = 1e-05
SEG_MOST = 512


def rotate(values, position, head_size):
    half = head_size // 2
    exponent = jnp.arange(half, dtype=jnp.float32) * (2.0 / head_size)
    frequency = ROPE_BASE ** (-exponent)
    angle = position[:, None, None] * frequency[None, None, :]
    cosine = jnp.cos(angle)
    sine = jnp.sin(angle)
    first = values[..., :half]
    second = values[..., half:]
    return jnp.concatenate(
        [first * cosine - second * sine, second * cosine + first * sine], axis=-1
    )


def segment_table(seg_lengths, tokens):
    ends = jnp.cumsum(seg_lengths)
    starts = ends - seg_lengths
    index = jnp.arange(tokens, dtype=jnp.int32)
    member = ((index[:, None] >= starts[None, :]) & (index[:, None] < ends[None, :])).astype(
        jnp.int32
    )
    seg_id = jnp.sum(member * jnp.arange(seg_lengths.shape[0], dtype=jnp.int32)[None, :], axis=1)
    first_index = jnp.sum(member * starts[None, :], axis=1)
    return (seg_id, index - first_index)


def normalize(block, gain, squares, model_width):
    widened = block.astype(jnp.float32)
    scale = lax.rsqrt(squares / model_width + EPS)
    return (widened * scale[:, None] * gain[None, :]).astype(jnp.bfloat16)


def shards_any(hidden_in, norm_gain, w_query, w_key, w_value, w_out, seg_lengths):
    rows_own, width = hidden_in.shape
    model_width = width * lax.axis_size("gx")
    tokens = rows_own * lax.axis_size("gy")
    query_rows = tokens // lax.axis_size("gx")
    widened = hidden_in.astype(jnp.float32)
    squares = lax.psum(jnp.sum(widened * widened, axis=1), "gx")
    source = normalize(hidden_in, norm_gain, squares, model_width)
    gathered = lax.all_gather(source, "gy", axis=0, tiled=True)
    query_cols = w_query.shape[1]
    heads_local = query_cols // HD
    group = H // KVH
    kv_local = max(1, heads_local // group)
    pair_cols = kv_local * HD
    first_head = lax.axis_index("gy") * heads_local // group
    key_own = lax.dynamic_slice_in_dim(w_key, first_head * HD, pair_cols, 1)
    value_own = lax.dynamic_slice_in_dim(w_value, first_head * HD, pair_cols, 1)
    seg_id, position = segment_table(seg_lengths, tokens)
    here = lax.axis_index("gx") * query_rows
    query_seg = lax.dynamic_slice_in_dim(seg_id, here, query_rows)
    query_pos = lax.dynamic_slice_in_dim(position, here, query_rows)
    query_index = here + jnp.arange(query_rows, dtype=jnp.int32)
    query_sum = lax.psum_scatter(
        jnp.dot(gathered, w_query, preferred_element_type=jnp.float32).astype(jnp.bfloat16),
        "gx",
        scatter_dimension=0,
        tiled=True,
    ).astype(jnp.float32)
    pair_part = jnp.concatenate(
        [
            jnp.dot(gathered, key_own, preferred_element_type=jnp.float32),
            jnp.dot(gathered, value_own, preferred_element_type=jnp.float32),
        ],
        axis=1,
    )
    pair_sum = lax.psum(pair_part.astype(jnp.bfloat16), "gx").astype(jnp.float32)
    key_raw = pair_sum[:, :pair_cols].astype(jnp.bfloat16)
    value_raw = pair_sum[:, pair_cols:].astype(jnp.bfloat16)
    group_local = heads_local // kv_local
    queries = rotate(
        query_sum.reshape(query_rows, heads_local, HD), query_pos.astype(jnp.float32), HD
    ).astype(jnp.bfloat16)
    queries = queries.reshape(query_rows, kv_local, group_local, HD)
    key_count = key_raw.shape[0]
    keys = rotate(
        key_raw.astype(jnp.float32).reshape(key_count, kv_local, HD),
        position.astype(jnp.float32),
        HD,
    )
    keys = keys.astype(jnp.bfloat16).reshape(key_count, pair_cols)
    score_scale = 1.0 / math.sqrt(HD)
    running = jnp.full((kv_local, group_local, query_rows), -1e30, jnp.float32)
    count = keys.shape[0]
    key_index = jnp.arange(count, dtype=jnp.int32)
    allowed = (query_seg[:, None] == seg_id[None, :]) & (key_index[None, :] <= query_index[:, None])
    key_heads = keys.reshape(count, kv_local, HD)
    value_heads = value_raw.reshape(count, kv_local, HD)
    scores = (
        jnp.einsum("rkgd,nkd->kgrn", queries, key_heads, preferred_element_type=jnp.float32)
        * score_scale
    )
    scores = jnp.where(allowed[None, None], scores, -1e30)
    newest = jnp.maximum(running, jnp.max(scores, axis=-1))
    weights = jnp.where(allowed[None, None], jnp.exp(scores - newest[..., None]), 0.0)
    denominator = jnp.sum(weights, axis=-1)
    added = jnp.einsum(
        "kgrn,nkd->rkgd",
        weights.astype(jnp.bfloat16),
        value_heads,
        preferred_element_type=jnp.float32,
    )
    accum = added
    running, denominator, accum = (newest, denominator, accum)
    attended = (
        (accum / denominator.transpose(2, 0, 1)[..., None])
        .reshape(query_rows, query_cols)
        .astype(jnp.bfloat16)
    )
    partial_out = jnp.dot(
        lax.all_gather(attended, "gx", axis=0, tiled=True),
        w_out,
        preferred_element_type=jnp.float32,
    )
    return lax.psum_scatter(partial_out.astype(jnp.bfloat16), "gy", scatter_dimension=0, tiled=True)


SCOPE = 24 * 2**20
EXTRA = 16
SMALL = pl.CostEstimate(flops=0, bytes_accessed=0, transcendentals=0)


def swap(value, axis, bit):
    return lax.ppermute(value, axis, [(i, i ^ bit) for i in range(lax.axis_size(axis))])


def columns(array, start, size):
    return lax.dynamic_slice_in_dim(array, start, size, 1)


def after(value, *others):
    hbm = pl.BlockSpec(memory_space=pl.ANY)
    return pl.pallas_call(
        lambda *refs: None,
        out_shape=jax.ShapeDtypeStruct(value.shape, value.dtype),
        in_specs=[hbm] * (1 + len(others)),
        out_specs=hbm,
        input_output_aliases={0: 0},
        cost_estimate=SMALL,
    )(value, *others)


def merge_kernel(split, at_ref, kept_ref, got_ref, squares_ref, *out_refs):
    rows = kept_ref.shape[0]
    arrived = got_ref[rows:, :HD].astype(jnp.float32)
    squares = squares_ref[...] + arrived[: EXTRA // 2] + arrived[EXTRA // 2 :]
    high = squares.astype(jnp.bfloat16).astype(jnp.float32)
    given_ref = out_refs[0]
    width = given_ref.shape[1]
    given_ref[rows:, :] = jnp.zeros((EXTRA, width), jnp.bfloat16)
    given_ref[rows:, :HD] = jnp.concatenate([high, squares - high], axis=0).astype(jnp.bfloat16)
    side = at_ref[0] if split else 1
    for i in range(1 + split):
        ref, at = out_refs[i], side if i else 1 - side
        at = pl.ds(pl.multiple_of(at * width, width), width) if split else slice(None)
        total = kept_ref[:, at].astype(jnp.float32) + got_ref[:rows, at].astype(jnp.float32)
        ref[:rows, :] = total.astype(jnp.bfloat16)
    if split:
        out_refs[2][...] = squares


def merge(split, side, kept, got, squares):
    rows, width = kept.shape
    vmem = pl.BlockSpec(memory_space=pltpu.VMEM)
    outs = [jax.ShapeDtypeStruct((rows + EXTRA, width // (1 + split)), jnp.bfloat16)]
    if split:
        outs.append(jax.ShapeDtypeStruct((rows, width // 2), jnp.bfloat16))
        outs.append(jax.ShapeDtypeStruct(squares.shape, jnp.float32))
    return pl.pallas_call(
        functools.partial(merge_kernel, split),
        out_shape=outs,
        in_specs=[pl.BlockSpec(memory_space=pltpu.SMEM)] + [vmem] * 3,
        out_specs=[vmem] * len(outs),
        compiler_params=pltpu.CompilerParams(vmem_limit_bytes=SCOPE),
        cost_estimate=SMALL,
    )(side, kept, got, squares)


def prepare_kernel(model_width, own_ref, pair_ref, cos_ref, sin_ref, key_ref, value_ref, scale_ref):
    blocks = 4
    held = pair_ref.shape[0] // blocks
    rows = held - EXTRA
    own = own_ref[0]
    key_ref[:SEG_MOST, :] = jnp.zeros((SEG_MOST, HD), jnp.bfloat16)
    value_ref[:SEG_MOST, :] = jnp.zeros((SEG_MOST, HD), jnp.bfloat16)
    for block in range(blocks):
        start = pl.multiple_of((block ^ own) * held, EXTRA)
        squares = pair_ref[pl.ds(pl.multiple_of(start + rows, EXTRA), EXTRA), :HD]
        squares = squares.astype(jnp.float32)
        squares = squares[: EXTRA // 2] + squares[EXTRA // 2 :]
        inverse = lax.rsqrt(squares / model_width + EPS)
        for i in range(rows // HD):
            here = pl.ds(block * rows + i * HD, HD)
            scale_ref[here, :] = jnp.transpose(jnp.broadcast_to(inverse[i : i + 1, :], (HD, HD)))
        here = pl.ds(block * rows, rows)
        there = pl.ds(SEG_MOST + block * rows, rows)
        key = pair_ref[pl.ds(start, rows), :HD].astype(jnp.float32)
        value = pair_ref[pl.ds(start, rows), HD:].astype(jnp.float32)
        key = key * cos_ref[here, :] + pltpu.roll(key, HD // 2, 1) * sin_ref[here, :]
        key_ref[there, :] = (key * scale_ref[here, :]).astype(jnp.bfloat16)
        value_ref[there, :] = (value * scale_ref[here, :]).astype(jnp.bfloat16)


def prepare(model_width, own, pair, cosine, sine):
    tokens = cosine.shape[0]
    padded = jax.ShapeDtypeStruct((SEG_MOST + tokens, HD), jnp.bfloat16)
    vmem = pl.BlockSpec(memory_space=pltpu.VMEM)
    return pl.pallas_call(
        functools.partial(prepare_kernel, model_width),
        out_shape=[padded, padded, jax.ShapeDtypeStruct((tokens, HD), jnp.float32)],
        in_specs=[pl.BlockSpec(memory_space=pltpu.SMEM)] + [vmem] * 3,
        out_specs=[vmem] * 3,
        compiler_params=pltpu.CompilerParams(vmem_limit_bytes=SCOPE),
        cost_estimate=SMALL,
    )(own, pair, cosine, sine)


def attend_kernel(first, half, own_ref, len_ref, query_ref, key_ref, value_ref, cos_ref, sin_ref, scale_ref, out_ref):
    rows = query_ref.shape[0] // 2
    block_rows = cos_ref.shape[0] // 4
    window = SEG_MOST + rows
    own = own_ref[0]
    for piece in range(2):
        start = pl.multiple_of((own ^ (first + piece)) * block_rows + half * rows, rows)
        here = pl.ds(start, rows)
        key = key_ref[pl.ds(start, window), :]
        value = value_ref[pl.ds(start, window), :]
        query_at = start + lax.broadcasted_iota(jnp.int32, (rows, 1), 0)
        key_at = start - SEG_MOST + lax.broadcasted_iota(jnp.int32, (rows, window), 1)
        begin = jnp.zeros((rows, 1), jnp.int32)
        total = len_ref[0]
        for i in range(1, len_ref.shape[0]):
            begin = jnp.where(query_at >= total, total, begin)
            total = total + len_ref[i]
        allowed = (key_at >= begin) & (key_at <= query_at)
        for head in range(2):
            at = pl.ds(head * HD, HD)
            query = query_ref[pl.ds(piece * rows, rows), at].astype(jnp.float32)
            query = query * cos_ref[here, :] + pltpu.roll(query, HD // 2, 1) * sin_ref[here, :]
            query = query * scale_ref[here, :]
            scores = lax.dot_general(
                query.astype(jnp.bfloat16),
                key,
                (((1,), (1,)), ((), ())),
                preferred_element_type=jnp.float32,
            )
            scores = jnp.where(allowed, scores * (1.0 / math.sqrt(HD)), -1e30)
            weights = jnp.exp(scores - jnp.max(scores, axis=1, keepdims=True))
            weights = jnp.where(allowed, weights, 0.0)
            denominator = jnp.sum(weights, axis=1, keepdims=True)
            added = jnp.dot(weights.astype(jnp.bfloat16), value, preferred_element_type=jnp.float32)
            out_ref[pl.ds(piece * rows, rows), at] = (added / denominator).astype(jnp.bfloat16)


def attend(first, half, own, seg_lengths, query, key, value, cosine, sine, scale):
    rows = query.shape[0]
    vmem = pl.BlockSpec(memory_space=pltpu.VMEM)
    smem = pl.BlockSpec(memory_space=pltpu.SMEM)
    return pl.pallas_call(
        functools.partial(attend_kernel, first, half),
        out_shape=jax.ShapeDtypeStruct(query.shape, jnp.bfloat16),
        in_specs=[smem, smem] + [vmem] * 6,
        out_specs=vmem,
        compiler_params=pltpu.CompilerParams(vmem_limit_bytes=SCOPE),
        cost_estimate=pl.CostEstimate(
            flops=2**31, bytes_accessed=2**20, transcendentals=0
        ),
    )(own, seg_lengths, query, key, value, cosine, sine, scale)


def copy_kernel(place_ref, weight_ref, out_ref):
    del place_ref
    out_ref[...] = weight_ref[...]


def reorder(place, weight):
    blocks = place.shape[0]
    shape = (weight.shape[0] // blocks, weight.shape[1])
    return pl.pallas_call(
        copy_kernel,
        out_shape=jax.ShapeDtypeStruct(weight.shape, jnp.bfloat16),
        grid_spec=pltpu.PrefetchScalarGridSpec(
            num_scalar_prefetch=1,
            grid=(blocks,),
            in_specs=[pl.BlockSpec(shape, lambda j, place: (place[j], 0))],
            out_specs=pl.BlockSpec(shape, lambda j, place: (j, 0)),
        ),
        compiler_params=pltpu.CompilerParams(vmem_limit_bytes=SCOPE),
        cost_estimate=pl.CostEstimate(
            flops=0, bytes_accessed=4 * weight.size, transcendentals=0
        ),
    )(place, weight)


def scale_rows(gain_ref, source_refs, scaled):
    @pl.when(pl.program_id(0) == 0)
    def _():
        at = 0
        for ref in source_refs:
            widened = ref[...].astype(jnp.float32) * gain_ref[...]
            scaled[pl.ds(at, ref.shape[0]), :] = widened.astype(jnp.bfloat16)
            at += ref.shape[0]


def pairs_kernel(place_ref, gain_ref, source_ref, extra_ref, key_ref, value_ref, given_ref, kept_ref, scaled):
    scale_rows(gain_ref, [source_ref], scaled)
    second = place_ref[place_ref.shape[0] - 1] == 1
    for i, ref in enumerate((key_ref, value_ref)):
        product = jnp.dot(scaled[...], ref[...], preferred_element_type=jnp.float32)
        product = product.astype(jnp.bfloat16)
        low, high = product[:, :HD], product[:, HD:]
        rows = low.shape[0]
        kept_ref[:, pl.ds(i * HD, HD)] = jnp.where(second, high, low)
        given_ref[:rows, pl.ds(i * HD, HD)] = jnp.where(second, low, high)
    given_ref[rows:, :] = jnp.zeros((EXTRA, 2 * HD), jnp.bfloat16)
    given_ref[rows:, :HD] = extra_ref[...]


def pairs(place, gain, source, extra, w_key, w_value):
    rows, depth = source.shape
    out = jax.ShapeDtypeStruct((rows, 8 * HD), jnp.bfloat16)
    picked = pl.BlockSpec((depth, 2 * HD), lambda j, place: (0, place[j]))
    given = jax.ShapeDtypeStruct((rows + EXTRA, 8 * HD), jnp.bfloat16)
    return pl.pallas_call(
        pairs_kernel,
        out_shape=[given, out],
        grid_spec=pltpu.PrefetchScalarGridSpec(
            num_scalar_prefetch=1,
            grid=(4,),
            in_specs=[
                pl.BlockSpec((1, depth), lambda j, place: (0, 0)),
                pl.BlockSpec((rows, depth), lambda j, place: (0, 0)),
                pl.BlockSpec((EXTRA, HD), lambda j, place: (0, 0)),
                picked,
                picked,
            ],
            out_specs=[
                pl.BlockSpec((rows + EXTRA, 2 * HD), lambda j, place: (0, j)),
                pl.BlockSpec((rows, 2 * HD), lambda j, place: (0, j)),
            ],
            scratch_shapes=[pltpu.VMEM((rows, depth), jnp.bfloat16)],
        ),
        compiler_params=pltpu.CompilerParams(vmem_limit_bytes=SCOPE),
        cost_estimate=pl.CostEstimate(
            flops=4 * rows * depth * 8 * HD, bytes_accessed=4 * depth * 8 * HD, transcendentals=0
        ),
    )(place, gain[None, :], source, extra, w_key, w_value)


def project_kernel(pieces, place_ref, gain_ref, *refs):
    weight_ref, out_ref, scaled = refs[pieces:]
    scale_rows(gain_ref, refs[:pieces], scaled)
    product = jnp.dot(scaled[...], weight_ref[...], preferred_element_type=jnp.float32)
    out_ref[...] = product.astype(jnp.bfloat16)


def project(place, gain, pieces, weight, size):
    piece_rows, depth = pieces[0].shape
    rows, width = len(pieces) * piece_rows, size * place.shape[0]
    return pl.pallas_call(
        functools.partial(project_kernel, len(pieces)),
        out_shape=jax.ShapeDtypeStruct((rows, width), jnp.bfloat16),
        grid_spec=pltpu.PrefetchScalarGridSpec(
            num_scalar_prefetch=1,
            grid=(place.shape[0],),
            in_specs=[pl.BlockSpec((1, depth), lambda j, place: (0, 0))]
            + [pl.BlockSpec((piece_rows, depth), lambda j, place: (0, 0))] * len(pieces)
            + [pl.BlockSpec((depth, size), lambda j, place: (0, place[j]))],
            out_specs=pl.BlockSpec((rows, size), lambda j, place: (0, j)),
            scratch_shapes=[pltpu.VMEM((rows, depth), jnp.bfloat16)],
        ),
        compiler_params=pltpu.CompilerParams(vmem_limit_bytes=SCOPE),
        cost_estimate=pl.CostEstimate(
            flops=2 * rows * depth * width,
            bytes_accessed=2 * (rows * depth + (depth + rows) * width),
            transcendentals=0,
        ),
    )(place, gain[None, :], *pieces, weight)


def shards_8x4(hidden_in, norm_gain, w_query, w_key, w_value, w_out, seg_lengths):
    f32, bf16 = jnp.float32, jnp.bfloat16
    rows, width = hidden_in.shape
    model_width = width * lax.axis_size("gx")
    tokens = rows * lax.axis_size("gy")
    cols = w_query.shape[1]
    half_rows, piece, pair_cols = rows // 2, cols // 8, 2 * HD
    gx, gy = lax.axis_index("gx"), lax.axis_index("gy")
    x_at, z_low, z_high = [b.astype(jnp.int32) for b in (gx & 1, (gx >> 1) & 1, gx >> 2)]
    rank = (x_at * 4 + z_low * 2 + z_high).astype(jnp.int32)
    z_at = z_low * 2 + z_high
    own = gy.astype(jnp.int32)[None]
    order = jnp.arange(4, dtype=jnp.int32)

    widened = hidden_in.astype(f32)
    squares = jnp.sum(widened * widened, axis=1).reshape(rows // HD, HD)
    squares = jnp.pad(squares, ((0, EXTRA // 2 - rows // HD), (0, 0)))
    high = lax.reduce_precision(squares, 8, 7)
    extra = jnp.concatenate([high, squares - high], axis=0).astype(bf16)

    parts = {}
    for h in range(2):
        parts[0, h] = hidden_in[h * half_rows : (h + 1) * half_rows]
        parts[1, h] = swap(parts[0, h], "gy", 1)
    parts[2, 0] = swap(parts[0, 0], "gy", 2)

    x_served = []

    def swap_x(value):
        if x_served:
            value = after(value, x_served[-1])
        x_served.append(swap(value, "gx", 1))
        return x_served[-1]

    def project_half(h, blocks, *others):
        picked = [parts[i, h] for i in range(4)]
        return project(after(rank ^ blocks, *others), norm_gain, picked, w_query, piece)

    place = jnp.concatenate([gy ^ order, x_at[None]]).astype(jnp.int32)
    given, kept_pair = pairs(place, norm_gain, hidden_in, extra, w_key, w_value)
    parts[2, 0] = after(parts[2, 0], given)
    parts[3, 0] = swap(parts[2, 0], "gy", 1)
    parts[2, 1] = swap(parts[0, 1], "gy", 2)
    cross = project_half(0, order + 4, given)
    given = swap_x(given)
    crossed_in, keeps = {}, {}
    arrived = swap_x(cross)
    crossed_in[0, 0], crossed_in[2, 0] = arrived[:rows], arrived[rows:]
    given, pair, squares = merge(True, z_low[None], after(kept_pair, cross), given, squares)
    parts[2, 1] = after(parts[2, 1], given)
    parts[3, 1] = swap(parts[2, 1], "gy", 1)
    keeps[0] = project_half(0, order, given)
    pair = after(pair, keeps[0])
    given, pair, squares = merge(True, z_high[None], pair, swap(given, "gx", 2), squares)
    cross = project_half(1, order + 4, given)
    (pair,) = merge(False, z_high[None], after(pair, cross), swap(given, "gx", 4), squares)
    across = []
    for i in range(8):
        for j in range(4):
            across.append((i * 4 + j, i * 4 + (j ^ ((i >> 1) & 1) * 2 ^ (i >> 2))))
    pair = lax.ppermute(pair, ("gx", "gy"), across)
    pair = jnp.concatenate([pair, swap(pair, "gx", 4)], axis=0)
    served, sums, halved, attended, shared, wide, gathered = [], {}, {}, {}, {}, {}, {}

    def halve_near(first, h, *others):
        at = slice(first // 2 * rows, (first // 2 + 1) * rows)
        keep, cross = keeps[h][at], crossed_in[first, h]
        low = (keep[:, 2 * piece :].astype(f32) + cross[:, 2 * piece :].astype(f32)).astype(bf16)
        if served:
            low = after(low, served[-1], *others)
        served.append(swap(low, "gx", 2))
        near = keep[:, : 2 * piece].astype(f32) + cross[:, : 2 * piece].astype(f32)
        sums[first, h] = near, served[-1]

    def halve_far(first, h, *others):
        near, got = sums[first, h]
        if others:
            got = after(got, *others)
        high = near[:, piece:] + got[:, piece:].astype(f32)
        near = near[:, :piece] + got[:, :piece].astype(f32)
        halved[first, h] = near, swap(high.astype(bf16), "gx", 4)

    halve_near(0, 0)
    halve_far(0, 0)
    keeps[1] = project_half(1, order, cross, pair, served[-1])
    pair = jnp.concatenate([pair, after(swap(pair, "gx", 2), keeps[1])], axis=0)
    crossed_in[2, 1] = swap_x(cross[rows:])
    crossed_in[0, 1] = swap_x(cross[:rows])

    _, position = segment_table(seg_lengths, tokens)
    lane = jnp.arange(HD, dtype=jnp.int32)
    exponent = (lane % (HD // 2)).astype(f32) * (2.0 / HD)
    angle = position.astype(f32)[:, None] * (ROPE_BASE ** (-exponent))[None, :]
    cosine = jnp.cos(angle)
    sine = jnp.where(lane < HD // 2, -1.0, 1.0)[None, :] * jnp.sin(angle)
    key, value, scale = prepare(model_width, own ^ z_at, pair, cosine, sine)

    def attend_chunk(first, h, *others):
        near, got = halved[first, h]
        query = (near + got.astype(f32)).astype(bf16)
        if others:
            query = after(query, *others)
        attended[first, h] = attend(first, h, own, seg_lengths, query, key, value, cosine, sine, scale)

    def gather_z(first, h, *others):
        a = attended[first, h]
        shared[first, h] = got = swap(a, "gx", 4)
        if others:
            got = after(got, *others)
        a = wide[first, h] = jnp.concatenate([a, got], axis=1)
        gathered[first, h] = jnp.concatenate([a, swap(a, "gx", 2)], axis=1)

    halve_near(2, 0)
    halve_far(2, 0)
    attend_chunk(0, 0)
    eight = jnp.arange(8, dtype=jnp.int32)
    w_rows = reorder(after(rank ^ eight, attended[0, 0]), w_out)
    gather_z(0, 0, w_rows)
    attend_chunk(2, 0)
    gather_z(2, 0)
    halve_near(2, 1)
    x_served[-1] = crossed_in[0, 1] = after(crossed_in[0, 1], attended[0, 0], attended[2, 0])
    leaving = after(gathered[0, 0], x_served[-1], shared[2, 0])
    crossed_out = {(0, 0): swap(leaving, "gx", 1)}
    x_served.append(crossed_out[0, 0])
    halve_far(2, 1, leaving, wide[2, 0])
    halve_near(0, 1, gathered[2, 0])
    halve_far(0, 1)
    attend_chunk(2, 1, crossed_out[0, 0])
    attend_chunk(0, 1)
    gather_z(2, 1)
    gather_z(0, 1)
    kept, crossed, crossed_given = {}, {}, {}
    for first, h in ((0, 0), (2, 0), (2, 1), (0, 1)):
        if (first, h) in crossed_out:
            a, got = leaving, crossed_out[first, h]
        else:
            others = [crossed_given[0]] if (first, h) == (0, 1) else []
            a = after(gathered[first, h], x_served[-1], *others)
            got = swap(a, "gx", 1)
            x_served.append(got)
        if (first, h) == (0, 1):
            got = after(got, crossed_given[1])
        a = jnp.concatenate([a, got], axis=1)
        given = jnp.dot(a[half_rows:], w_rows, preferred_element_type=f32).astype(bf16)
        a = a[:half_rows]
        mine = jnp.dot(a, w_rows, preferred_element_type=f32)
        mine = mine + swap(given, "gy", 1).astype(f32)
        if first:
            crossed_given[h] = mine.astype(bf16)
            crossed[h] = swap(crossed_given[h], "gy", 2)
        else:
            kept[h] = mine
    return jnp.concatenate(
        [(kept[h] + crossed[h].astype(f32)).astype(bf16) for h in range(2)], axis=0
    )


def shards(hidden_in, norm_gain, w_query, w_key, w_value, w_out, seg_lengths):
    split = (lax.axis_size("gx"), lax.axis_size("gy"))
    body = shards_8x4 if split == (8, 4) else shards_any
    return body(hidden_in, norm_gain, w_query, w_key, w_value, w_out, seg_lengths)


def solution(mesh):
    in_specs = (
        P("gy", "gx"),
        P("gx"),
        P("gx", "gy"),
        P("gx", None),
        P("gx", None),
        P("gy", "gx"),
        P(),
    )
    out_specs = P("gy", "gx")
    return jax.shard_map(shards, mesh=mesh, in_specs=in_specs, out_specs=out_specs, check_vma=False)
```

```python
import functools
import math

import jax
import jax.numpy as jnp
from jax import lax
from jax.experimental import pallas as pl
from jax.experimental.pallas import tpu as pltpu
from jax.sharding import PartitionSpec as P

H = 64
KVH = 8
HD = 128


ROPE_BASE = 500000.0
EPS = 1e-05
SEG_MOST = 512


def rotate(values, position, head_size):
    half = head_size // 2
    exponent = jnp.arange(half, dtype=jnp.float32) * (2.0 / head_size)
    frequency = ROPE_BASE ** (-exponent)
    angle = position[:, None, None] * frequency[None, None, :]
    cosine = jnp.cos(angle)
    sine = jnp.sin(angle)
    first = values[..., :half]
    second = values[..., half:]
    return jnp.concatenate(
        [first * cosine - second * sine, second * cosine + first * sine], axis=-1
    )


def segment_table(seg_lengths, tokens):
    ends = jnp.cumsum(seg_lengths)
    starts = ends - seg_lengths
    index = jnp.arange(tokens, dtype=jnp.int32)
    member = ((index[:, None] >= starts[None, :]) & (index[:, None] < ends[None, :])).astype(
        jnp.int32
    )
    seg_id = jnp.sum(member * jnp.arange(seg_lengths.shape[0], dtype=jnp.int32)[None, :], axis=1)
    first_index = jnp.sum(member * starts[None, :], axis=1)
    return (seg_id, index - first_index)


def normalize(block, gain, squares, model_width):
    widened = block.astype(jnp.float32)
    scale = lax.rsqrt(squares / model_width + EPS)
    return (widened * scale[:, None] * gain[None, :]).astype(jnp.bfloat16)


def shards_any(hidden_in, norm_gain, w_query, w_key, w_value, w_out, seg_lengths):
    rows_own, width = hidden_in.shape
    model_width = width * lax.axis_size("gx")
    tokens = rows_own * lax.axis_size("gy")
    query_rows = tokens // lax.axis_size("gx")
    widened = hidden_in.astype(jnp.float32)
    squares = lax.psum(jnp.sum(widened * widened, axis=1), "gx")
    source = normalize(hidden_in, norm_gain, squares, model_width)
    gathered = lax.all_gather(source, "gy", axis=0, tiled=True)
    query_cols = w_query.shape[1]
    heads_local = query_cols // HD
    group = H // KVH
    kv_local = max(1, heads_local // group)
    pair_cols = kv_local * HD
    first_head = lax.axis_index("gy") * heads_local // group
    key_own = lax.dynamic_slice_in_dim(w_key, first_head * HD, pair_cols, 1)
    value_own = lax.dynamic_slice_in_dim(w_value, first_head * HD, pair_cols, 1)
    seg_id, position = segment_table(seg_lengths, tokens)
    here = lax.axis_index("gx") * query_rows
    query_seg = lax.dynamic_slice_in_dim(seg_id, here, query_rows)
    query_pos = lax.dynamic_slice_in_dim(position, here, query_rows)
    query_index = here + jnp.arange(query_rows, dtype=jnp.int32)
    query_sum = lax.psum_scatter(
        jnp.dot(gathered, w_query, preferred_element_type=jnp.float32).astype(jnp.bfloat16),
        "gx",
        scatter_dimension=0,
        tiled=True,
    ).astype(jnp.float32)
    pair_part = jnp.concatenate(
        [
            jnp.dot(gathered, key_own, preferred_element_type=jnp.float32),
            jnp.dot(gathered, value_own, preferred_element_type=jnp.float32),
        ],
        axis=1,
    )
    pair_sum = lax.psum(pair_part.astype(jnp.bfloat16), "gx").astype(jnp.float32)
    key_raw = pair_sum[:, :pair_cols].astype(jnp.bfloat16)
    value_raw = pair_sum[:, pair_cols:].astype(jnp.bfloat16)
    group_local = heads_local // kv_local
    queries = rotate(
        query_sum.reshape(query_rows, heads_local, HD), query_pos.astype(jnp.float32), HD
    ).astype(jnp.bfloat16)
    queries = queries.reshape(query_rows, kv_local, group_local, HD)
    key_count = key_raw.shape[0]
    keys = rotate(
        key_raw.astype(jnp.float32).reshape(key_count, kv_local, HD),
        position.astype(jnp.float32),
        HD,
    )
    keys = keys.astype(jnp.bfloat16).reshape(key_count, pair_cols)
    score_scale = 1.0 / math.sqrt(HD)
    running = jnp.full((kv_local, group_local, query_rows), -1e30, jnp.float32)
    count = keys.shape[0]
    key_index = jnp.arange(count, dtype=jnp.int32)
    allowed = (query_seg[:, None] == seg_id[None, :]) & (key_index[None, :] <= query_index[:, None])
    key_heads = keys.reshape(count, kv_local, HD)
    value_heads = value_raw.reshape(count, kv_local, HD)
    scores = (
        jnp.einsum("rkgd,nkd->kgrn", queries, key_heads, preferred_element_type=jnp.float32)
        * score_scale
    )
    scores = jnp.where(allowed[None, None], scores, -1e30)
    newest = jnp.maximum(running, jnp.max(scores, axis=-1))
    weights = jnp.where(allowed[None, None], jnp.exp(scores - newest[..., None]), 0.0)
    denominator = jnp.sum(weights, axis=-1)
    added = jnp.einsum(
        "kgrn,nkd->rkgd",
        weights.astype(jnp.bfloat16),
        value_heads,
        preferred_element_type=jnp.float32,
    )
    accum = added
    running, denominator, accum = (newest, denominator, accum)
    attended = (
        (accum / denominator.transpose(2, 0, 1)[..., None])
        .reshape(query_rows, query_cols)
        .astype(jnp.bfloat16)
    )
    partial_out = jnp.dot(
        lax.all_gather(attended, "gx", axis=0, tiled=True),
        w_out,
        preferred_element_type=jnp.float32,
    )
    return lax.psum_scatter(partial_out.astype(jnp.bfloat16), "gy", scatter_dimension=0, tiled=True)


SCOPE = 32 * 2**20
SMALL = pl.CostEstimate(flops=0, bytes_accessed=0, transcendentals=0)


def swap(value, axis, bit):
    return lax.ppermute(value, axis, [(i, i ^ bit) for i in range(lax.axis_size(axis))])


def columns(array, start, size):
    return lax.dynamic_slice_in_dim(array, start, size, 1)


def after(value, *others):
    hbm = pl.BlockSpec(memory_space=pl.ANY)
    return pl.pallas_call(
        lambda *refs: None,
        out_shape=jax.ShapeDtypeStruct(value.shape, value.dtype),
        in_specs=[hbm] * (1 + len(others)),
        out_specs=hbm,
        input_output_aliases={0: 0},
        cost_estimate=SMALL,
    )(value, *others)


def prepare_kernel(own_ref, pair_ref, cos_ref, sin_ref, scale_ref, key_ref, value_ref):
    blocks = 4
    rows = pair_ref.shape[0] // blocks
    own = own_ref[0]
    key_ref[:SEG_MOST, :] = jnp.zeros((SEG_MOST, HD), jnp.bfloat16)
    value_ref[:SEG_MOST, :] = jnp.zeros((SEG_MOST, HD), jnp.bfloat16)
    for block in range(blocks):
        start = pl.multiple_of((block ^ own) * rows, rows)
        here = pl.ds(block * rows, rows)
        there = pl.ds(SEG_MOST + block * rows, rows)
        key = pair_ref[pl.ds(start, rows), :HD].astype(jnp.float32)
        value = pair_ref[pl.ds(start, rows), HD:].astype(jnp.float32)
        key = key * cos_ref[here, :] + pltpu.roll(key, HD // 2, 1) * sin_ref[here, :]
        key_ref[there, :] = key.astype(jnp.bfloat16)
        value_ref[there, :] = (value * scale_ref[here, :]).astype(jnp.bfloat16)


def prepare(own, pair, cosine, sine, scale):
    tokens = pair.shape[0]
    padded = jax.ShapeDtypeStruct((SEG_MOST + tokens, HD), jnp.bfloat16)
    vmem = pl.BlockSpec(memory_space=pltpu.VMEM)
    return pl.pallas_call(
        prepare_kernel,
        out_shape=[padded, padded],
        in_specs=[pl.BlockSpec(memory_space=pltpu.SMEM)] + [vmem] * 4,
        out_specs=[vmem, vmem],
        compiler_params=pltpu.CompilerParams(vmem_limit_bytes=SCOPE),
        cost_estimate=SMALL,
    )(own, pair, cosine, sine, scale)


def attend_kernel(first, half, own_ref, len_ref, query_ref, key_ref, value_ref, cos_ref, sin_ref, out_ref):
    rows = query_ref.shape[0] // 2
    block_rows = cos_ref.shape[0] // 4
    window = SEG_MOST + rows
    own = own_ref[0]
    for piece in range(2):
        start = pl.multiple_of((own ^ (first + piece)) * block_rows + half * rows, rows)
        here = pl.ds(start, rows)
        key = key_ref[pl.ds(start, window), :]
        value = value_ref[pl.ds(start, window), :]
        query_at = start + lax.broadcasted_iota(jnp.int32, (rows, 1), 0)
        key_at = start - SEG_MOST + lax.broadcasted_iota(jnp.int32, (rows, window), 1)
        begin = jnp.zeros((rows, 1), jnp.int32)
        total = len_ref[0]
        for i in range(1, len_ref.shape[0]):
            begin = jnp.where(query_at >= total, total, begin)
            total = total + len_ref[i]
        allowed = (key_at >= begin) & (key_at <= query_at)
        for head in range(2):
            at = pl.ds(head * HD, HD)
            query = query_ref[pl.ds(piece * rows, rows), at].astype(jnp.float32)
            query = query * cos_ref[here, :] + pltpu.roll(query, HD // 2, 1) * sin_ref[here, :]
            scores = lax.dot_general(
                query.astype(jnp.bfloat16),
                key,
                (((1,), (1,)), ((), ())),
                preferred_element_type=jnp.float32,
            )
            scores = jnp.where(allowed, scores * (1.0 / math.sqrt(HD)), -1e30)
            weights = jnp.exp(scores - jnp.max(scores, axis=1, keepdims=True))
            weights = jnp.where(allowed, weights, 0.0)
            denominator = jnp.sum(weights, axis=1, keepdims=True)
            added = jnp.dot(weights.astype(jnp.bfloat16), value, preferred_element_type=jnp.float32)
            out_ref[pl.ds(piece * rows, rows), at] = (added / denominator).astype(jnp.bfloat16)


def attend(first, half, own, seg_lengths, query, key, value, cosine, sine):
    rows = query.shape[0]
    vmem = pl.BlockSpec(memory_space=pltpu.VMEM)
    smem = pl.BlockSpec(memory_space=pltpu.SMEM)
    return pl.pallas_call(
        functools.partial(attend_kernel, first, half),
        out_shape=jax.ShapeDtypeStruct(query.shape, jnp.bfloat16),
        in_specs=[smem, smem] + [vmem] * 5,
        out_specs=vmem,
        compiler_params=pltpu.CompilerParams(vmem_limit_bytes=SCOPE),
        cost_estimate=pl.CostEstimate(
            flops=2**31, bytes_accessed=2**20, transcendentals=0
        ),
    )(own, seg_lengths, query, key, value, cosine, sine)


def copy_kernel(place_ref, weight_ref, out_ref):
    del place_ref
    out_ref[...] = weight_ref[...]


def reorder(place, weight):
    blocks = place.shape[0]
    shape = (weight.shape[0] // blocks, weight.shape[1])
    return pl.pallas_call(
        copy_kernel,
        out_shape=jax.ShapeDtypeStruct(weight.shape, jnp.bfloat16),
        grid_spec=pltpu.PrefetchScalarGridSpec(
            num_scalar_prefetch=1,
            grid=(blocks,),
            in_specs=[pl.BlockSpec(shape, lambda j, place: (place[j], 0))],
            out_specs=pl.BlockSpec(shape, lambda j, place: (j, 0)),
        ),
        compiler_params=pltpu.CompilerParams(vmem_limit_bytes=SCOPE),
        cost_estimate=pl.CostEstimate(
            flops=0, bytes_accessed=4 * weight.size, transcendentals=0
        ),
    )(place, weight)


def scale_rows(gain_ref, source_refs, scaled):
    @pl.when(pl.program_id(0) == 0)
    def _():
        at = 0
        for ref in source_refs:
            widened = ref[...].astype(jnp.float32) * gain_ref[...]
            scaled[pl.ds(at, ref.shape[0]), :] = widened.astype(jnp.bfloat16)
            at += ref.shape[0]


def pairs_kernel(place_ref, gain_ref, source_ref, key_ref, value_ref, given_ref, kept_ref, scaled):
    scale_rows(gain_ref, [source_ref], scaled)
    second = place_ref[place_ref.shape[0] - 1] == 1
    for i, ref in enumerate((key_ref, value_ref)):
        product = jnp.dot(scaled[...], ref[...], preferred_element_type=jnp.float32)
        product = product.astype(jnp.bfloat16)
        low, high = product[:, :HD], product[:, HD:]
        kept_ref[:, pl.ds(i * HD, HD)] = jnp.where(second, high, low)
        given_ref[:, pl.ds(i * HD, HD)] = jnp.where(second, low, high)


def pairs(place, gain, source, w_key, w_value):
    rows, depth = source.shape
    out = jax.ShapeDtypeStruct((rows, 8 * HD), jnp.bfloat16)
    picked = pl.BlockSpec((depth, 2 * HD), lambda j, place: (0, place[j]))
    made = pl.BlockSpec((rows, 2 * HD), lambda j, place: (0, j))
    return pl.pallas_call(
        pairs_kernel,
        out_shape=[out, out],
        grid_spec=pltpu.PrefetchScalarGridSpec(
            num_scalar_prefetch=1,
            grid=(4,),
            in_specs=[
                pl.BlockSpec((1, depth), lambda j, place: (0, 0)),
                pl.BlockSpec((rows, depth), lambda j, place: (0, 0)),
                picked,
                picked,
            ],
            out_specs=[made, made],
            scratch_shapes=[pltpu.VMEM((rows, depth), jnp.bfloat16)],
        ),
        compiler_params=pltpu.CompilerParams(vmem_limit_bytes=SCOPE),
        cost_estimate=pl.CostEstimate(
            flops=4 * rows * depth * 8 * HD, bytes_accessed=4 * depth * 8 * HD, transcendentals=0
        ),
    )(place, gain[None, :], source, w_key, w_value)


def project_kernel(pieces, place_ref, gain_ref, *refs):
    weight_ref, out_refs, scaled = refs[pieces], refs[pieces + 1 : -1], refs[-1]
    scale_rows(gain_ref, refs[:pieces], scaled)
    product = jnp.dot(scaled[...], weight_ref[...], preferred_element_type=jnp.float32)
    rows = product.shape[0] // len(out_refs)
    for i, ref in enumerate(out_refs):
        ref[...] = product[i * rows : (i + 1) * rows, :].astype(jnp.bfloat16)


def project(place, gain, pieces, weight, size, outs):
    piece_rows, depth = pieces[0].shape
    rows, width = len(pieces) * piece_rows, size * place.shape[0]
    out = jax.ShapeDtypeStruct((rows // outs, width), jnp.bfloat16)
    return pl.pallas_call(
        functools.partial(project_kernel, len(pieces)),
        out_shape=[out] * outs,
        grid_spec=pltpu.PrefetchScalarGridSpec(
            num_scalar_prefetch=1,
            grid=(place.shape[0],),
            in_specs=[pl.BlockSpec((1, depth), lambda j, place: (0, 0))]
            + [pl.BlockSpec((piece_rows, depth), lambda j, place: (0, 0))] * len(pieces)
            + [pl.BlockSpec((depth, size), lambda j, place: (0, place[j]))],
            out_specs=[pl.BlockSpec((rows // outs, size), lambda j, place: (0, j))] * outs,
            scratch_shapes=[pltpu.VMEM((rows, depth), jnp.bfloat16)],
        ),
        compiler_params=pltpu.CompilerParams(vmem_limit_bytes=SCOPE),
        cost_estimate=pl.CostEstimate(
            flops=2 * rows * depth * width,
            bytes_accessed=2 * (rows * depth + (depth + rows) * width),
            transcendentals=0,
        ),
    )(place, gain[None, :], *pieces, weight)


def shards_8x4(hidden_in, norm_gain, w_query, w_key, w_value, w_out, seg_lengths):
    f32, bf16 = jnp.float32, jnp.bfloat16
    rows, width = hidden_in.shape
    model_width = width * lax.axis_size("gx")
    tokens = rows * lax.axis_size("gy")
    cols = w_query.shape[1]
    half_rows, piece, pair_cols = rows // 2, cols // 8, 2 * HD
    gx, gy = lax.axis_index("gx"), lax.axis_index("gy")
    x_at, z_low, z_high = gx & 1, (gx >> 1) & 1, gx >> 2
    rank = (x_at * 4 + z_low * 2 + z_high).astype(jnp.int32)
    z_at = z_low * 2 + z_high
    own = gy.astype(jnp.int32)[None]
    order = jnp.arange(4, dtype=jnp.int32)

    widened = hidden_in.astype(f32)
    squares = jnp.sum(widened * widened, axis=1)
    squares = lax.dynamic_update_slice_in_dim(jnp.zeros((tokens,), f32), squares, gy * rows, 0)
    squares = squares.reshape(tokens // HD, HD)
    squares = squares_x = squares + swap(squares, "gx", 1)
    for axis, bit in (("gy", 1), ("gx", 2), ("gx", 4)):
        squares = squares + swap(squares, axis, bit)

    parts = {}
    for h in range(2):
        parts[0, h] = hidden_in[h * half_rows : (h + 1) * half_rows]
        parts[1, h] = swap(parts[0, h], "gy", 1)

    for h in range(2):
        parts[2, h] = swap(parts[0, h], "gy", 2)
        parts[3, h] = swap(parts[2, h], "gy", 1)


    x_served = []

    def swap_x(value, *others):
        if x_served:
            value = after(value, x_served[-1], *others)
        x_served.append(swap(value, "gx", 1))
        return x_served[-1]

    def pieces(first):
        return [parts[first + i, h] for h in range(2) for i in range(2)]

    place = jnp.concatenate([gy ^ order, x_at[None]]).astype(jnp.int32)
    given, kept_pair = pairs(place, norm_gain, hidden_in, w_key, w_value)
    near_place = after(rank ^ (order + 4), given)
    crossed_in, keeps = {}, {}
    outs = project(near_place, norm_gain, pieces(0), w_query, piece, 2)
    (keeps[0],) = project(after(rank ^ order, outs[0]), norm_gain, pieces(0), w_query, piece, 1)
    given = swap_x(after(given, squares_x))
    crossed_in[0, 0], crossed_in[0, 1] = swap_x(outs[0]), swap_x(outs[1])
    pair = given.astype(f32) + after(kept_pair, keeps[0]).astype(f32)
    pair = pair.astype(bf16)
    given = columns(pair, (1 - z_low) * 2 * pair_cols, 2 * pair_cols)
    pair = columns(pair, z_low * 2 * pair_cols, 2 * pair_cols).astype(f32)
    pair = (pair + swap(given, "gx", 2).astype(f32)).astype(bf16)
    outs = project(after(rank ^ (order + 4), pair), norm_gain, pieces(2), w_query, piece, 2)
    (keeps[2],) = project(after(rank ^ order, outs[0]), norm_gain, pieces(2), w_query, piece, 1)
    crossed_in[2, 0], crossed_in[2, 1] = swap_x(outs[0]), swap_x(outs[1])
    given = columns(pair, (1 - z_high) * pair_cols, pair_cols)
    pair = columns(pair, z_high * pair_cols, pair_cols).astype(f32)
    pair = (pair + swap(given, "gx", 4).astype(f32)).astype(bf16)
    across = []
    for i in range(8):
        for j in range(4):
            across.append((i * 4 + j, i * 4 + (j ^ ((i >> 1) & 1) * 2 ^ (i >> 2))))
    squares = after(squares, pair)
    pair = lax.ppermute(pair, ("gx", "gy"), across)
    squares = squares + swap(squares, "gy", 2)
    pair = jnp.concatenate([pair, swap(pair, "gx", 4)], axis=0)
    pair = jnp.concatenate([pair, swap(pair, "gx", 2)], axis=0)

    scale = lax.rsqrt(squares.reshape(tokens) / model_width + EPS)[:, None]
    _, position = segment_table(seg_lengths, tokens)
    lane = jnp.arange(HD, dtype=jnp.int32)
    exponent = (lane % (HD // 2)).astype(f32) * (2.0 / HD)
    angle = position.astype(f32)[:, None] * (ROPE_BASE ** (-exponent))[None, :]
    cosine = jnp.cos(angle) * scale
    sine = jnp.where(lane < HD // 2, -1.0, 1.0)[None, :] * jnp.sin(angle) * scale

    served, sums, halved, attended, gathered = [], {}, {}, {}, {}

    def halve_near(first, h, *others):
        cross = crossed_in[first, h]
        keep = keeps[first][h * rows : (h + 1) * rows]
        low = (keep[:, 2 * piece :].astype(f32) + cross[:, 2 * piece :].astype(f32)).astype(bf16)
        if served:
            low = after(low, served[-1], *others)
        served.append(swap(low, "gx", 2))
        near = keep[:, : 2 * piece].astype(f32) + cross[:, : 2 * piece].astype(f32)
        sums[first, h] = near, served[-1]

    def halve_far(first, h, *others):
        near, got = sums[first, h]
        if others:
            got = after(got, *others)
        high = near[:, piece:] + got[:, piece:].astype(f32)
        near = near[:, :piece] + got[:, :piece].astype(f32)
        halved[first, h] = near, swap(high.astype(bf16), "gx", 4)

    def attend_chunk(first, h):
        near, got = halved[first, h]
        query = (near + got.astype(f32)).astype(bf16)
        attended[first, h] = attend(first, h, own, seg_lengths, query, key, value, cosine, sine)

    halve_near(0, 0)
    halve_far(0, 0)
    halve_near(0, 1)
    pair = after(pair, served[-1])
    key, value = prepare(own ^ z_at, pair, cosine, sine, jnp.broadcast_to(scale, (tokens, HD)))
    attend_chunk(0, 0)
    gathered[0, 0] = swap(attended[0, 0], "gx", 4)
    halve_near(2, 0, gathered[0, 0])
    wide = jnp.concatenate([attended[0, 0], gathered[0, 0]], axis=1)
    halve_far(2, 0, wide)
    attend_chunk(2, 0)
    halve_far(0, 1)
    attend_chunk(0, 1)
    halve_near(2, 1)
    halve_far(2, 1)
    attend_chunk(2, 1)
    got = halved[2, 1][1]
    attended[0, 1] = after(attended[0, 1], got)

    w_rows = reorder(after(rank ^ jnp.arange(8, dtype=jnp.int32), crossed_in[2, 0]), w_out)
    kept, crossed = {}, {}
    mine_given = {}
    for first, h in ((0, 0), (2, 0), (2, 1), (0, 1)):
        a = attended[first, h]
        a = wide if (first, h) in gathered else jnp.concatenate([a, swap(a, "gx", 4)], axis=1)
        a = jnp.concatenate([a, swap(a, "gx", 2)], axis=1)
        got = swap_x(a, *([mine_given[0]] if (first, h) == (0, 1) else []))
        a = jnp.concatenate([a, got], axis=1)
        given = jnp.dot(a[half_rows:], w_rows, preferred_element_type=f32).astype(bf16)
        mine = jnp.dot(a[:half_rows], w_rows, preferred_element_type=f32)
        mine = mine + swap(given, "gy", 1).astype(f32)
        if first:
            mine_given[h] = mine.astype(bf16)
            crossed[h] = swap(mine_given[h], "gy", 2)
        else:
            kept[h] = mine
    return jnp.concatenate(
        [(kept[h] + crossed[h].astype(f32)).astype(bf16) for h in range(2)], axis=0
    )


def shards(hidden_in, norm_gain, w_query, w_key, w_value, w_out, seg_lengths):
    split = (lax.axis_size("gx"), lax.axis_size("gy"))
    body = shards_8x4 if split == (8, 4) else shards_any
    return body(hidden_in, norm_gain, w_query, w_key, w_value, w_out, seg_lengths)


def solution(mesh):
    in_specs = (
        P("gy", "gx"),
        P("gx"),
        P("gx", "gy"),
        P("gx", None),
        P("gx", None),
        P("gy", "gx"),
        P(),
    )
    out_specs = P("gy", "gx")
    return jax.shard_map(shards, mesh=mesh, in_specs=in_specs, out_specs=out_specs, check_vma=False)
```

```python
import functools
import math

import jax
import jax.numpy as jnp
from jax import lax
from jax.experimental import pallas as pl
from jax.experimental.pallas import tpu as pltpu
from jax.sharding import PartitionSpec as P

H = 64
KVH = 8
HD = 128


ROPE_BASE = 500000.0
EPS = 1e-05
SEG_MOST = 512


def rotate(values, position, head_size):
    half = head_size // 2
    exponent = jnp.arange(half, dtype=jnp.float32) * (2.0 / head_size)
    frequency = ROPE_BASE ** (-exponent)
    angle = position[:, None, None] * frequency[None, None, :]
    cosine = jnp.cos(angle)
    sine = jnp.sin(angle)
    first = values[..., :half]
    second = values[..., half:]
    return jnp.concatenate(
        [first * cosine - second * sine, second * cosine + first * sine], axis=-1
    )


def segment_table(seg_lengths, tokens):
    ends = jnp.cumsum(seg_lengths)
    starts = ends - seg_lengths
    index = jnp.arange(tokens, dtype=jnp.int32)
    member = ((index[:, None] >= starts[None, :]) & (index[:, None] < ends[None, :])).astype(
        jnp.int32
    )
    seg_id = jnp.sum(member * jnp.arange(seg_lengths.shape[0], dtype=jnp.int32)[None, :], axis=1)
    first_index = jnp.sum(member * starts[None, :], axis=1)
    return (seg_id, index - first_index)


def normalize(block, gain, squares, model_width):
    widened = block.astype(jnp.float32)
    scale = lax.rsqrt(squares / model_width + EPS)
    return (widened * scale[:, None] * gain[None, :]).astype(jnp.bfloat16)


def shards_any(hidden_in, norm_gain, w_query, w_key, w_value, w_out, seg_lengths):
    rows_own, width = hidden_in.shape
    model_width = width * lax.axis_size("gx")
    tokens = rows_own * lax.axis_size("gy")
    query_rows = tokens // lax.axis_size("gx")
    widened = hidden_in.astype(jnp.float32)
    squares = lax.psum(jnp.sum(widened * widened, axis=1), "gx")
    source = normalize(hidden_in, norm_gain, squares, model_width)
    gathered = lax.all_gather(source, "gy", axis=0, tiled=True)
    query_cols = w_query.shape[1]
    heads_local = query_cols // HD
    group = H // KVH
    kv_local = max(1, heads_local // group)
    pair_cols = kv_local * HD
    first_head = lax.axis_index("gy") * heads_local // group
    key_own = lax.dynamic_slice_in_dim(w_key, first_head * HD, pair_cols, 1)
    value_own = lax.dynamic_slice_in_dim(w_value, first_head * HD, pair_cols, 1)
    seg_id, position = segment_table(seg_lengths, tokens)
    here = lax.axis_index("gx") * query_rows
    query_seg = lax.dynamic_slice_in_dim(seg_id, here, query_rows)
    query_pos = lax.dynamic_slice_in_dim(position, here, query_rows)
    query_index = here + jnp.arange(query_rows, dtype=jnp.int32)
    query_sum = lax.psum_scatter(
        jnp.dot(gathered, w_query, preferred_element_type=jnp.float32).astype(jnp.bfloat16),
        "gx",
        scatter_dimension=0,
        tiled=True,
    ).astype(jnp.float32)
    pair_part = jnp.concatenate(
        [
            jnp.dot(gathered, key_own, preferred_element_type=jnp.float32),
            jnp.dot(gathered, value_own, preferred_element_type=jnp.float32),
        ],
        axis=1,
    )
    pair_sum = lax.psum(pair_part.astype(jnp.bfloat16), "gx").astype(jnp.float32)
    key_raw = pair_sum[:, :pair_cols].astype(jnp.bfloat16)
    value_raw = pair_sum[:, pair_cols:].astype(jnp.bfloat16)
    group_local = heads_local // kv_local
    queries = rotate(
        query_sum.reshape(query_rows, heads_local, HD), query_pos.astype(jnp.float32), HD
    ).astype(jnp.bfloat16)
    queries = queries.reshape(query_rows, kv_local, group_local, HD)
    key_count = key_raw.shape[0]
    keys = rotate(
        key_raw.astype(jnp.float32).reshape(key_count, kv_local, HD),
        position.astype(jnp.float32),
        HD,
    )
    keys = keys.astype(jnp.bfloat16).reshape(key_count, pair_cols)
    score_scale = 1.0 / math.sqrt(HD)
    running = jnp.full((kv_local, group_local, query_rows), -1e30, jnp.float32)
    count = keys.shape[0]
    key_index = jnp.arange(count, dtype=jnp.int32)
    allowed = (query_seg[:, None] == seg_id[None, :]) & (key_index[None, :] <= query_index[:, None])
    key_heads = keys.reshape(count, kv_local, HD)
    value_heads = value_raw.reshape(count, kv_local, HD)
    scores = (
        jnp.einsum("rkgd,nkd->kgrn", queries, key_heads, preferred_element_type=jnp.float32)
        * score_scale
    )
    scores = jnp.where(allowed[None, None], scores, -1e30)
    newest = jnp.maximum(running, jnp.max(scores, axis=-1))
    weights = jnp.where(allowed[None, None], jnp.exp(scores - newest[..., None]), 0.0)
    denominator = jnp.sum(weights, axis=-1)
    added = jnp.einsum(
        "kgrn,nkd->rkgd",
        weights.astype(jnp.bfloat16),
        value_heads,
        preferred_element_type=jnp.float32,
    )
    accum = added
    running, denominator, accum = (newest, denominator, accum)
    attended = (
        (accum / denominator.transpose(2, 0, 1)[..., None])
        .reshape(query_rows, query_cols)
        .astype(jnp.bfloat16)
    )
    partial_out = jnp.dot(
        lax.all_gather(attended, "gx", axis=0, tiled=True),
        w_out,
        preferred_element_type=jnp.float32,
    )
    return lax.psum_scatter(partial_out.astype(jnp.bfloat16), "gy", scatter_dimension=0, tiled=True)


SCOPE = 32 * 2**20
SMALL = pl.CostEstimate(flops=0, bytes_accessed=0, transcendentals=0)


def swap(value, axis, bit):
    return lax.ppermute(value, axis, [(i, i ^ bit) for i in range(lax.axis_size(axis))])


def columns(array, start, size):
    return lax.dynamic_slice_in_dim(array, start, size, 1)


def after(value, *others):
    hbm = pl.BlockSpec(memory_space=pl.ANY)
    return pl.pallas_call(
        lambda *refs: None,
        out_shape=jax.ShapeDtypeStruct(value.shape, value.dtype),
        in_specs=[hbm] * (1 + len(others)),
        out_specs=hbm,
        input_output_aliases={0: 0},
        cost_estimate=SMALL,
    )(value, *others)


def prepare_kernel(own_ref, pair_ref, cos_ref, sin_ref, scale_ref, key_ref, value_ref):
    blocks = 4
    rows = pair_ref.shape[0] // blocks
    own = own_ref[0]
    key_ref[:SEG_MOST, :] = jnp.zeros((SEG_MOST, HD), jnp.bfloat16)
    value_ref[:SEG_MOST, :] = jnp.zeros((SEG_MOST, HD), jnp.bfloat16)
    for block in range(blocks):
        start = pl.multiple_of((block ^ own) * rows, rows)
        here = pl.ds(block * rows, rows)
        there = pl.ds(SEG_MOST + block * rows, rows)
        key = pair_ref[pl.ds(start, rows), :HD].astype(jnp.float32)
        value = pair_ref[pl.ds(start, rows), HD:].astype(jnp.float32)
        key = key * cos_ref[here, :] + pltpu.roll(key, HD // 2, 1) * sin_ref[here, :]
        key_ref[there, :] = key.astype(jnp.bfloat16)
        value_ref[there, :] = (value * scale_ref[here, :]).astype(jnp.bfloat16)


def prepare(own, pair, cosine, sine, scale):
    tokens = pair.shape[0]
    padded = jax.ShapeDtypeStruct((SEG_MOST + tokens, HD), jnp.bfloat16)
    vmem = pl.BlockSpec(memory_space=pltpu.VMEM)
    return pl.pallas_call(
        prepare_kernel,
        out_shape=[padded, padded],
        in_specs=[pl.BlockSpec(memory_space=pltpu.SMEM)] + [vmem] * 4,
        out_specs=[vmem, vmem],
        compiler_params=pltpu.CompilerParams(vmem_limit_bytes=SCOPE),
        cost_estimate=SMALL,
    )(own, pair, cosine, sine, scale)


def attend_kernel(first, half, own_ref, len_ref, query_ref, key_ref, value_ref, cos_ref, sin_ref, out_ref):
    rows = query_ref.shape[0] // 2
    block_rows = cos_ref.shape[0] // 4
    window = SEG_MOST + rows
    own = own_ref[0]
    for piece in range(2):
        start = pl.multiple_of((own ^ (first + piece)) * block_rows + half * rows, rows)
        here = pl.ds(start, rows)
        key = key_ref[pl.ds(start, window), :]
        value = value_ref[pl.ds(start, window), :]
        query_at = start + lax.broadcasted_iota(jnp.int32, (rows, 1), 0)
        key_at = start - SEG_MOST + lax.broadcasted_iota(jnp.int32, (rows, window), 1)
        begin = jnp.zeros((rows, 1), jnp.int32)
        total = len_ref[0]
        for i in range(1, len_ref.shape[0]):
            begin = jnp.where(query_at >= total, total, begin)
            total = total + len_ref[i]
        allowed = (key_at >= begin) & (key_at <= query_at)
        for head in range(2):
            at = pl.ds(head * HD, HD)
            query = query_ref[pl.ds(piece * rows, rows), at].astype(jnp.float32)
            query = query * cos_ref[here, :] + pltpu.roll(query, HD // 2, 1) * sin_ref[here, :]
            scores = lax.dot_general(
                query.astype(jnp.bfloat16),
                key,
                (((1,), (1,)), ((), ())),
                preferred_element_type=jnp.float32,
            )
            scores = jnp.where(allowed, scores * (1.0 / math.sqrt(HD)), -1e30)
            weights = jnp.exp(scores - jnp.max(scores, axis=1, keepdims=True))
            weights = jnp.where(allowed, weights, 0.0)
            denominator = jnp.sum(weights, axis=1, keepdims=True)
            added = jnp.dot(weights.astype(jnp.bfloat16), value, preferred_element_type=jnp.float32)
            out_ref[pl.ds(piece * rows, rows), at] = (added / denominator).astype(jnp.bfloat16)


def attend(first, half, own, seg_lengths, query, key, value, cosine, sine):
    rows = query.shape[0]
    vmem = pl.BlockSpec(memory_space=pltpu.VMEM)
    smem = pl.BlockSpec(memory_space=pltpu.SMEM)
    return pl.pallas_call(
        functools.partial(attend_kernel, first, half),
        out_shape=jax.ShapeDtypeStruct(query.shape, jnp.bfloat16),
        in_specs=[smem, smem] + [vmem] * 5,
        out_specs=vmem,
        compiler_params=pltpu.CompilerParams(vmem_limit_bytes=SCOPE),
        cost_estimate=pl.CostEstimate(
            flops=2**31, bytes_accessed=2**20, transcendentals=0
        ),
    )(own, seg_lengths, query, key, value, cosine, sine)


def copy_kernel(place_ref, weight_ref, out_ref):
    del place_ref
    out_ref[...] = weight_ref[...]


def reorder(place, weight):
    blocks = place.shape[0]
    shape = (weight.shape[0] // blocks, weight.shape[1])
    return pl.pallas_call(
        copy_kernel,
        out_shape=jax.ShapeDtypeStruct(weight.shape, jnp.bfloat16),
        grid_spec=pltpu.PrefetchScalarGridSpec(
            num_scalar_prefetch=1,
            grid=(blocks,),
            in_specs=[pl.BlockSpec(shape, lambda j, place: (place[j], 0))],
            out_specs=pl.BlockSpec(shape, lambda j, place: (j, 0)),
        ),
        compiler_params=pltpu.CompilerParams(vmem_limit_bytes=SCOPE),
        cost_estimate=pl.CostEstimate(
            flops=0, bytes_accessed=4 * weight.size, transcendentals=0
        ),
    )(place, weight)


def scale_rows(gain_ref, source_refs, scaled):
    @pl.when(pl.program_id(0) == 0)
    def _():
        at = 0
        for ref in source_refs:
            widened = ref[...].astype(jnp.float32) * gain_ref[...]
            scaled[pl.ds(at, ref.shape[0]), :] = widened.astype(jnp.bfloat16)
            at += ref.shape[0]


def pairs_kernel(place_ref, gain_ref, source_ref, key_ref, value_ref, given_ref, kept_ref, scaled):
    scale_rows(gain_ref, [source_ref], scaled)
    second = place_ref[place_ref.shape[0] - 1] == 1
    for i, ref in enumerate((key_ref, value_ref)):
        product = jnp.dot(scaled[...], ref[...], preferred_element_type=jnp.float32)
        product = product.astype(jnp.bfloat16)
        low, high = product[:, :HD], product[:, HD:]
        kept_ref[:, pl.ds(i * HD, HD)] = jnp.where(second, high, low)
        given_ref[:, pl.ds(i * HD, HD)] = jnp.where(second, low, high)


def pairs(place, gain, source, w_key, w_value):
    rows, depth = source.shape
    out = jax.ShapeDtypeStruct((rows, 8 * HD), jnp.bfloat16)
    picked = pl.BlockSpec((depth, 2 * HD), lambda j, place: (0, place[j]))
    made = pl.BlockSpec((rows, 2 * HD), lambda j, place: (0, j))
    return pl.pallas_call(
        pairs_kernel,
        out_shape=[out, out],
        grid_spec=pltpu.PrefetchScalarGridSpec(
            num_scalar_prefetch=1,
            grid=(4,),
            in_specs=[
                pl.BlockSpec((1, depth), lambda j, place: (0, 0)),
                pl.BlockSpec((rows, depth), lambda j, place: (0, 0)),
                picked,
                picked,
            ],
            out_specs=[made, made],
            scratch_shapes=[pltpu.VMEM((rows, depth), jnp.bfloat16)],
        ),
        compiler_params=pltpu.CompilerParams(vmem_limit_bytes=SCOPE),
        cost_estimate=pl.CostEstimate(
            flops=4 * rows * depth * 8 * HD, bytes_accessed=4 * depth * 8 * HD, transcendentals=0
        ),
    )(place, gain[None, :], source, w_key, w_value)


def project_kernel(pieces, place_ref, gain_ref, *refs):
    weight_ref, out_refs, scaled = refs[pieces], refs[pieces + 1 : -1], refs[-1]
    scale_rows(gain_ref, refs[:pieces], scaled)
    product = jnp.dot(scaled[...], weight_ref[...], preferred_element_type=jnp.float32)
    rows = product.shape[0] // len(out_refs)
    for i, ref in enumerate(out_refs):
        ref[...] = product[i * rows : (i + 1) * rows, :].astype(jnp.bfloat16)


def project(place, gain, pieces, weight, size, outs):
    piece_rows, depth = pieces[0].shape
    rows, width = len(pieces) * piece_rows, size * place.shape[0]
    out = jax.ShapeDtypeStruct((rows // outs, width), jnp.bfloat16)
    return pl.pallas_call(
        functools.partial(project_kernel, len(pieces)),
        out_shape=[out] * outs,
        grid_spec=pltpu.PrefetchScalarGridSpec(
            num_scalar_prefetch=1,
            grid=(place.shape[0],),
            in_specs=[pl.BlockSpec((1, depth), lambda j, place: (0, 0))]
            + [pl.BlockSpec((piece_rows, depth), lambda j, place: (0, 0))] * len(pieces)
            + [pl.BlockSpec((depth, size), lambda j, place: (0, place[j]))],
            out_specs=[pl.BlockSpec((rows // outs, size), lambda j, place: (0, j))] * outs,
            scratch_shapes=[pltpu.VMEM((rows, depth), jnp.bfloat16)],
        ),
        compiler_params=pltpu.CompilerParams(vmem_limit_bytes=SCOPE),
        cost_estimate=pl.CostEstimate(
            flops=2 * rows * depth * width,
            bytes_accessed=2 * (rows * depth + (depth + rows) * width),
            transcendentals=0,
        ),
    )(place, gain[None, :], *pieces, weight)


def shards_8x4(hidden_in, norm_gain, w_query, w_key, w_value, w_out, seg_lengths):
    f32, bf16 = jnp.float32, jnp.bfloat16
    rows, width = hidden_in.shape
    model_width = width * lax.axis_size("gx")
    tokens = rows * lax.axis_size("gy")
    cols = w_query.shape[1]
    half_rows, piece, pair_cols = rows // 2, cols // 8, 2 * HD
    gx, gy = lax.axis_index("gx"), lax.axis_index("gy")
    x_at, z_low, z_high = gx & 1, (gx >> 1) & 1, gx >> 2
    rank = (x_at * 4 + z_low * 2 + z_high).astype(jnp.int32)
    z_at = z_low * 2 + z_high
    own = gy.astype(jnp.int32)[None]
    order = jnp.arange(4, dtype=jnp.int32)

    widened = hidden_in.astype(f32)
    squares = jnp.sum(widened * widened, axis=1)
    squares = lax.dynamic_update_slice_in_dim(jnp.zeros((tokens,), f32), squares, gy * rows, 0)
    squares = squares.reshape(tokens // HD, HD)
    squares = squares_x = squares + swap(squares, "gx", 1)
    for axis, bit in (("gy", 1), ("gx", 2), ("gx", 4)):
        squares = squares + swap(squares, axis, bit)

    parts = {}
    for h in range(2):
        parts[0, h] = hidden_in[h * half_rows : (h + 1) * half_rows]
        parts[1, h] = swap(parts[0, h], "gy", 1)

    for h in range(2):
        parts[2, h] = swap(parts[0, h], "gy", 2)
        parts[3, h] = swap(parts[2, h], "gy", 1)


    x_served = []

    def swap_x(value):
        if x_served:
            value = after(value, x_served[-1])
        x_served.append(swap(value, "gx", 1))
        return x_served[-1]

    def pieces(first):
        return [parts[first + i, h] for h in range(2) for i in range(2)]

    place = jnp.concatenate([gy ^ order, x_at[None]]).astype(jnp.int32)
    given, kept_pair = pairs(place, norm_gain, hidden_in, w_key, w_value)
    near_place = after(rank ^ (order + 4), given)
    crossed_in, keeps = {}, {}
    outs = project(near_place, norm_gain, pieces(0), w_query, piece, 2)
    (keeps[0],) = project(after(rank ^ order, outs[0]), norm_gain, pieces(0), w_query, piece, 1)
    given = swap_x(after(given, squares_x))
    crossed_in[0, 0], crossed_in[0, 1] = swap_x(outs[0]), swap_x(outs[1])
    pair = given.astype(f32) + after(kept_pair, keeps[0]).astype(f32)
    pair = pair.astype(bf16)
    given = columns(pair, (1 - z_low) * 2 * pair_cols, 2 * pair_cols)
    pair = columns(pair, z_low * 2 * pair_cols, 2 * pair_cols).astype(f32)
    pair = (pair + swap(given, "gx", 2).astype(f32)).astype(bf16)
    outs = project(after(rank ^ (order + 4), pair), norm_gain, pieces(2), w_query, piece, 2)
    (keeps[2],) = project(after(rank ^ order, outs[0]), norm_gain, pieces(2), w_query, piece, 1)
    crossed_in[2, 0], crossed_in[2, 1] = swap_x(outs[0]), swap_x(outs[1])
    given = columns(pair, (1 - z_high) * pair_cols, pair_cols)
    pair = columns(pair, z_high * pair_cols, pair_cols).astype(f32)
    pair = (pair + swap(given, "gx", 4).astype(f32)).astype(bf16)
    across = []
    for i in range(8):
        for j in range(4):
            across.append((i * 4 + j, i * 4 + (j ^ ((i >> 1) & 1) * 2 ^ (i >> 2))))
    squares = after(squares, pair)
    pair = lax.ppermute(pair, ("gx", "gy"), across)
    squares = squares + swap(squares, "gy", 2)
    pair = jnp.concatenate([pair, swap(pair, "gx", 4)], axis=0)
    pair = jnp.concatenate([pair, swap(pair, "gx", 2)], axis=0)

    scale = lax.rsqrt(squares.reshape(tokens) / model_width + EPS)[:, None]
    _, position = segment_table(seg_lengths, tokens)
    lane = jnp.arange(HD, dtype=jnp.int32)
    exponent = (lane % (HD // 2)).astype(f32) * (2.0 / HD)
    angle = position.astype(f32)[:, None] * (ROPE_BASE ** (-exponent))[None, :]
    cosine = jnp.cos(angle) * scale
    sine = jnp.where(lane < HD // 2, -1.0, 1.0)[None, :] * jnp.sin(angle) * scale
    key, value = prepare(own ^ z_at, pair, cosine, sine, jnp.broadcast_to(scale, (tokens, HD)))

    attended, last = {}, None
    for first, h in ((0, 0), (0, 1), (2, 0), (2, 1)):
        cross = crossed_in[first, h]
        keep = keeps[first][h * rows : (h + 1) * rows]
        low = (keep[:, 2 * piece :].astype(f32) + cross[:, 2 * piece :].astype(f32)).astype(bf16)
        if last is not None:
            marks = [attended[0, 0]] if (first, h) == (2, 0) else [keeps[2]]
            low = after(low, last, *marks)
        last = got = swap(low, "gx", 2)
        near = keep[:, : 2 * piece].astype(f32) + cross[:, : 2 * piece].astype(f32)
        high = near[:, piece:] + got[:, piece:].astype(f32)
        near = near[:, :piece] + got[:, :piece].astype(f32)
        got = swap(high.astype(bf16), "gx", 4)
        query = (near + got.astype(f32)).astype(bf16)
        attended[first, h] = attend(first, h, own, seg_lengths, query, key, value, cosine, sine)
    attended[0, 1] = after(attended[0, 1], got)

    w_rows = reorder(after(rank ^ jnp.arange(8, dtype=jnp.int32), crossed_in[2, 0]), w_out)
    kept, crossed = {}, {}
    done = None
    for first, h in ((0, 0), (2, 0), (2, 1), (0, 1)):
        a = attended[first, h]
        got = swap(a, "gx", 4)
        if (first, h) == (0, 0):
            got = after(got, w_rows)
        a = jnp.concatenate([a, got], axis=1)
        a = jnp.concatenate([a, swap(a, "gx", 2)], axis=1)
        got = swap_x(a)
        if done is not None:
            got = after(got, done)
        a = jnp.concatenate([a, got], axis=1)
        given = jnp.dot(a[half_rows:], w_rows, preferred_element_type=f32).astype(bf16)
        a = a[:half_rows]
        if (first, h) == (2, 1):
            a = after(a, crossed[0])
        mine = jnp.dot(a, w_rows, preferred_element_type=f32)
        mine = mine + swap(given, "gy", 1).astype(f32)
        if first:
            done = mine.astype(bf16)
            crossed[h] = swap(done, "gy", 2)
        else:
            kept[h] = mine
    return jnp.concatenate(
        [(kept[h] + crossed[h].astype(f32)).astype(bf16) for h in range(2)], axis=0
    )


def shards(hidden_in, norm_gain, w_query, w_key, w_value, w_out, seg_lengths):
    split = (lax.axis_size("gx"), lax.axis_size("gy"))
    body = shards_8x4 if split == (8, 4) else shards_any
    return body(hidden_in, norm_gain, w_query, w_key, w_value, w_out, seg_lengths)


def solution(mesh):
    in_specs = (
        P("gy", "gx"),
        P("gx"),
        P("gx", "gy"),
        P("gx", None),
        P("gx", None),
        P("gy", "gx"),
        P(),
    )
    out_specs = P("gy", "gx")
    return jax.shard_map(shards, mesh=mesh, in_specs=in_specs, out_specs=out_specs, check_vma=False)
```

```python
import functools
import math

import jax
import jax.numpy as jnp
from jax import lax
from jax.experimental import pallas as pl
from jax.experimental.pallas import tpu as pltpu
from jax.sharding import PartitionSpec as P

H = 64
KVH = 8
HD = 128


ROPE_BASE = 500000.0
EPS = 1e-05
SEG_MOST = 512


def rotate(values, position, head_size):
    half = head_size // 2
    exponent = jnp.arange(half, dtype=jnp.float32) * (2.0 / head_size)
    frequency = ROPE_BASE ** (-exponent)
    angle = position[:, None, None] * frequency[None, None, :]
    cosine = jnp.cos(angle)
    sine = jnp.sin(angle)
    first = values[..., :half]
    second = values[..., half:]
    return jnp.concatenate(
        [first * cosine - second * sine, second * cosine + first * sine], axis=-1
    )


def segment_table(seg_lengths, tokens):
    ends = jnp.cumsum(seg_lengths)
    starts = ends - seg_lengths
    index = jnp.arange(tokens, dtype=jnp.int32)
    member = ((index[:, None] >= starts[None, :]) & (index[:, None] < ends[None, :])).astype(
        jnp.int32
    )
    seg_id = jnp.sum(member * jnp.arange(seg_lengths.shape[0], dtype=jnp.int32)[None, :], axis=1)
    first_index = jnp.sum(member * starts[None, :], axis=1)
    return (seg_id, index - first_index)


def normalize(block, gain, squares, model_width):
    widened = block.astype(jnp.float32)
    scale = lax.rsqrt(squares / model_width + EPS)
    return (widened * scale[:, None] * gain[None, :]).astype(jnp.bfloat16)


def shards_any(hidden_in, norm_gain, w_query, w_key, w_value, w_out, seg_lengths):
    rows_own, width = hidden_in.shape
    model_width = width * lax.axis_size("gx")
    tokens = rows_own * lax.axis_size("gy")
    query_rows = tokens // lax.axis_size("gx")
    widened = hidden_in.astype(jnp.float32)
    squares = lax.psum(jnp.sum(widened * widened, axis=1), "gx")
    source = normalize(hidden_in, norm_gain, squares, model_width)
    gathered = lax.all_gather(source, "gy", axis=0, tiled=True)
    query_cols = w_query.shape[1]
    heads_local = query_cols // HD
    group = H // KVH
    kv_local = max(1, heads_local // group)
    pair_cols = kv_local * HD
    first_head = lax.axis_index("gy") * heads_local // group
    key_own = lax.dynamic_slice_in_dim(w_key, first_head * HD, pair_cols, 1)
    value_own = lax.dynamic_slice_in_dim(w_value, first_head * HD, pair_cols, 1)
    seg_id, position = segment_table(seg_lengths, tokens)
    here = lax.axis_index("gx") * query_rows
    query_seg = lax.dynamic_slice_in_dim(seg_id, here, query_rows)
    query_pos = lax.dynamic_slice_in_dim(position, here, query_rows)
    query_index = here + jnp.arange(query_rows, dtype=jnp.int32)
    query_sum = lax.psum_scatter(
        jnp.dot(gathered, w_query, preferred_element_type=jnp.float32).astype(jnp.bfloat16),
        "gx",
        scatter_dimension=0,
        tiled=True,
    ).astype(jnp.float32)
    pair_part = jnp.concatenate(
        [
            jnp.dot(gathered, key_own, preferred_element_type=jnp.float32),
            jnp.dot(gathered, value_own, preferred_element_type=jnp.float32),
        ],
        axis=1,
    )
    pair_sum = lax.psum(pair_part.astype(jnp.bfloat16), "gx").astype(jnp.float32)
    key_raw = pair_sum[:, :pair_cols].astype(jnp.bfloat16)
    value_raw = pair_sum[:, pair_cols:].astype(jnp.bfloat16)
    group_local = heads_local // kv_local
    queries = rotate(
        query_sum.reshape(query_rows, heads_local, HD), query_pos.astype(jnp.float32), HD
    ).astype(jnp.bfloat16)
    queries = queries.reshape(query_rows, kv_local, group_local, HD)
    key_count = key_raw.shape[0]
    keys = rotate(
        key_raw.astype(jnp.float32).reshape(key_count, kv_local, HD),
        position.astype(jnp.float32),
        HD,
    )
    keys = keys.astype(jnp.bfloat16).reshape(key_count, pair_cols)
    score_scale = 1.0 / math.sqrt(HD)
    running = jnp.full((kv_local, group_local, query_rows), -1e30, jnp.float32)
    count = keys.shape[0]
    key_index = jnp.arange(count, dtype=jnp.int32)
    allowed = (query_seg[:, None] == seg_id[None, :]) & (key_index[None, :] <= query_index[:, None])
    key_heads = keys.reshape(count, kv_local, HD)
    value_heads = value_raw.reshape(count, kv_local, HD)
    scores = (
        jnp.einsum("rkgd,nkd->kgrn", queries, key_heads, preferred_element_type=jnp.float32)
        * score_scale
    )
    scores = jnp.where(allowed[None, None], scores, -1e30)
    newest = jnp.maximum(running, jnp.max(scores, axis=-1))
    weights = jnp.where(allowed[None, None], jnp.exp(scores - newest[..., None]), 0.0)
    denominator = jnp.sum(weights, axis=-1)
    added = jnp.einsum(
        "kgrn,nkd->rkgd",
        weights.astype(jnp.bfloat16),
        value_heads,
        preferred_element_type=jnp.float32,
    )
    accum = added
    running, denominator, accum = (newest, denominator, accum)
    attended = (
        (accum / denominator.transpose(2, 0, 1)[..., None])
        .reshape(query_rows, query_cols)
        .astype(jnp.bfloat16)
    )
    partial_out = jnp.dot(
        lax.all_gather(attended, "gx", axis=0, tiled=True),
        w_out,
        preferred_element_type=jnp.float32,
    )
    return lax.psum_scatter(partial_out.astype(jnp.bfloat16), "gy", scatter_dimension=0, tiled=True)


SCOPE = 32 * 2**20
SMALL = pl.CostEstimate(flops=0, bytes_accessed=0, transcendentals=0)


def swap(value, axis, bit):
    return lax.ppermute(value, axis, [(i, i ^ bit) for i in range(lax.axis_size(axis))])


def columns(array, start, size):
    return lax.dynamic_slice_in_dim(array, start, size, 1)


def after(value, *others):
    hbm = pl.BlockSpec(memory_space=pl.ANY)
    return pl.pallas_call(
        lambda *refs: None,
        out_shape=jax.ShapeDtypeStruct(value.shape, value.dtype),
        in_specs=[hbm] * (1 + len(others)),
        out_specs=hbm,
        input_output_aliases={0: 0},
        cost_estimate=SMALL,
    )(value, *others)


def prepare_kernel(own_ref, pair_ref, cos_ref, sin_ref, scale_ref, key_ref, value_ref):
    blocks = 4
    rows = pair_ref.shape[0] // blocks
    own = own_ref[0]
    key_ref[:SEG_MOST, :] = jnp.zeros((SEG_MOST, HD), jnp.bfloat16)
    value_ref[:SEG_MOST, :] = jnp.zeros((SEG_MOST, HD), jnp.bfloat16)
    for block in range(blocks):
        start = pl.multiple_of((block ^ own) * rows, rows)
        here = pl.ds(block * rows, rows)
        there = pl.ds(SEG_MOST + block * rows, rows)
        key = pair_ref[pl.ds(start, rows), :HD].astype(jnp.float32)
        value = pair_ref[pl.ds(start, rows), HD:].astype(jnp.float32)
        key = key * cos_ref[here, :] + pltpu.roll(key, HD // 2, 1) * sin_ref[here, :]
        key_ref[there, :] = key.astype(jnp.bfloat16)
        value_ref[there, :] = (value * scale_ref[here, :]).astype(jnp.bfloat16)


def prepare(own, pair, cosine, sine, scale):
    tokens = pair.shape[0]
    padded = jax.ShapeDtypeStruct((SEG_MOST + tokens, HD), jnp.bfloat16)
    vmem = pl.BlockSpec(memory_space=pltpu.VMEM)
    return pl.pallas_call(
        prepare_kernel,
        out_shape=[padded, padded],
        in_specs=[pl.BlockSpec(memory_space=pltpu.SMEM)] + [vmem] * 4,
        out_specs=[vmem, vmem],
        compiler_params=pltpu.CompilerParams(vmem_limit_bytes=SCOPE),
        cost_estimate=SMALL,
    )(own, pair, cosine, sine, scale)


def attend_kernel(first, half, own_ref, len_ref, query_ref, key_ref, value_ref, cos_ref, sin_ref, out_ref):
    rows = query_ref.shape[0] // 2
    block_rows = cos_ref.shape[0] // 4
    window = SEG_MOST + rows
    own = own_ref[0]
    for piece in range(2):
        start = pl.multiple_of((own ^ (first + piece)) * block_rows + half * rows, rows)
        here = pl.ds(start, rows)
        key = key_ref[pl.ds(start, window), :]
        value = value_ref[pl.ds(start, window), :]
        query_at = start + lax.broadcasted_iota(jnp.int32, (rows, 1), 0)
        key_at = start - SEG_MOST + lax.broadcasted_iota(jnp.int32, (rows, window), 1)
        begin = jnp.zeros((rows, 1), jnp.int32)
        total = len_ref[0]
        for i in range(1, len_ref.shape[0]):
            begin = jnp.where(query_at >= total, total, begin)
            total = total + len_ref[i]
        allowed = (key_at >= begin) & (key_at <= query_at)
        for head in range(2):
            at = pl.ds(head * HD, HD)
            query = query_ref[pl.ds(piece * rows, rows), at].astype(jnp.float32)
            query = query * cos_ref[here, :] + pltpu.roll(query, HD // 2, 1) * sin_ref[here, :]
            scores = lax.dot_general(
                query.astype(jnp.bfloat16),
                key,
                (((1,), (1,)), ((), ())),
                preferred_element_type=jnp.float32,
            )
            scores = jnp.where(allowed, scores * (1.0 / math.sqrt(HD)), -1e30)
            weights = jnp.exp(scores - jnp.max(scores, axis=1, keepdims=True))
            weights = jnp.where(allowed, weights, 0.0)
            denominator = jnp.sum(weights, axis=1, keepdims=True)
            added = jnp.dot(weights.astype(jnp.bfloat16), value, preferred_element_type=jnp.float32)
            out_ref[pl.ds(piece * rows, rows), at] = (added / denominator).astype(jnp.bfloat16)


def attend(first, half, own, seg_lengths, query, key, value, cosine, sine):
    rows = query.shape[0]
    vmem = pl.BlockSpec(memory_space=pltpu.VMEM)
    smem = pl.BlockSpec(memory_space=pltpu.SMEM)
    return pl.pallas_call(
        functools.partial(attend_kernel, first, half),
        out_shape=jax.ShapeDtypeStruct(query.shape, jnp.bfloat16),
        in_specs=[smem, smem] + [vmem] * 5,
        out_specs=vmem,
        compiler_params=pltpu.CompilerParams(vmem_limit_bytes=SCOPE),
        cost_estimate=pl.CostEstimate(
            flops=2**31, bytes_accessed=2**20, transcendentals=0
        ),
    )(own, seg_lengths, query, key, value, cosine, sine)


def copy_kernel(place_ref, weight_ref, out_ref):
    del place_ref
    out_ref[...] = weight_ref[...]


def reorder(place, weight):
    blocks = place.shape[0]
    shape = (weight.shape[0] // blocks, weight.shape[1])
    return pl.pallas_call(
        copy_kernel,
        out_shape=jax.ShapeDtypeStruct(weight.shape, jnp.bfloat16),
        grid_spec=pltpu.PrefetchScalarGridSpec(
            num_scalar_prefetch=1,
            grid=(blocks,),
            in_specs=[pl.BlockSpec(shape, lambda j, place: (place[j], 0))],
            out_specs=pl.BlockSpec(shape, lambda j, place: (j, 0)),
        ),
        compiler_params=pltpu.CompilerParams(vmem_limit_bytes=SCOPE),
        cost_estimate=pl.CostEstimate(
            flops=0, bytes_accessed=4 * weight.size, transcendentals=0
        ),
    )(place, weight)


def scale_rows(gain_ref, source_refs, scaled):
    @pl.when(pl.program_id(0) == 0)
    def _():
        at = 0
        for ref in source_refs:
            widened = ref[...].astype(jnp.float32) * gain_ref[...]
            scaled[pl.ds(at, ref.shape[0]), :] = widened.astype(jnp.bfloat16)
            at += ref.shape[0]


def pairs_kernel(place_ref, gain_ref, source_ref, key_ref, value_ref, given_ref, kept_ref, scaled):
    scale_rows(gain_ref, [source_ref], scaled)
    second = place_ref[place_ref.shape[0] - 1] == 1
    for i, ref in enumerate((key_ref, value_ref)):
        product = jnp.dot(scaled[...], ref[...], preferred_element_type=jnp.float32)
        product = product.astype(jnp.bfloat16)
        low, high = product[:, :HD], product[:, HD:]
        kept_ref[:, pl.ds(i * HD, HD)] = jnp.where(second, high, low)
        given_ref[:, pl.ds(i * HD, HD)] = jnp.where(second, low, high)


def pairs(place, gain, source, w_key, w_value):
    rows, depth = source.shape
    out = jax.ShapeDtypeStruct((rows, 8 * HD), jnp.bfloat16)
    picked = pl.BlockSpec((depth, 2 * HD), lambda j, place: (0, place[j]))
    made = pl.BlockSpec((rows, 2 * HD), lambda j, place: (0, j))
    return pl.pallas_call(
        pairs_kernel,
        out_shape=[out, out],
        grid_spec=pltpu.PrefetchScalarGridSpec(
            num_scalar_prefetch=1,
            grid=(4,),
            in_specs=[
                pl.BlockSpec((1, depth), lambda j, place: (0, 0)),
                pl.BlockSpec((rows, depth), lambda j, place: (0, 0)),
                picked,
                picked,
            ],
            out_specs=[made, made],
            scratch_shapes=[pltpu.VMEM((rows, depth), jnp.bfloat16)],
        ),
        compiler_params=pltpu.CompilerParams(vmem_limit_bytes=SCOPE),
        cost_estimate=pl.CostEstimate(
            flops=4 * rows * depth * 8 * HD, bytes_accessed=4 * depth * 8 * HD, transcendentals=0
        ),
    )(place, gain[None, :], source, w_key, w_value)


def project_kernel(pieces, place_ref, gain_ref, *refs):
    weight_ref, out_refs, scaled = refs[pieces], refs[pieces + 1 : -1], refs[-1]
    scale_rows(gain_ref, refs[:pieces], scaled)
    product = jnp.dot(scaled[...], weight_ref[...], preferred_element_type=jnp.float32)
    rows = product.shape[0] // len(out_refs)
    for i, ref in enumerate(out_refs):
        ref[...] = product[i * rows : (i + 1) * rows, :].astype(jnp.bfloat16)


def project(place, gain, pieces, weight, size, outs):
    piece_rows, depth = pieces[0].shape
    rows, width = len(pieces) * piece_rows, size * place.shape[0]
    out = jax.ShapeDtypeStruct((rows // outs, width), jnp.bfloat16)
    return pl.pallas_call(
        functools.partial(project_kernel, len(pieces)),
        out_shape=[out] * outs,
        grid_spec=pltpu.PrefetchScalarGridSpec(
            num_scalar_prefetch=1,
            grid=(place.shape[0],),
            in_specs=[pl.BlockSpec((1, depth), lambda j, place: (0, 0))]
            + [pl.BlockSpec((piece_rows, depth), lambda j, place: (0, 0))] * len(pieces)
            + [pl.BlockSpec((depth, size), lambda j, place: (0, place[j]))],
            out_specs=[pl.BlockSpec((rows // outs, size), lambda j, place: (0, j))] * outs,
            scratch_shapes=[pltpu.VMEM((rows, depth), jnp.bfloat16)],
        ),
        compiler_params=pltpu.CompilerParams(vmem_limit_bytes=SCOPE),
        cost_estimate=pl.CostEstimate(
            flops=2 * rows * depth * width,
            bytes_accessed=2 * (rows * depth + (depth + rows) * width),
            transcendentals=0,
        ),
    )(place, gain[None, :], *pieces, weight)


def shards_8x4(hidden_in, norm_gain, w_query, w_key, w_value, w_out, seg_lengths):
    f32, bf16 = jnp.float32, jnp.bfloat16
    rows, width = hidden_in.shape
    model_width = width * lax.axis_size("gx")
    tokens = rows * lax.axis_size("gy")
    cols = w_query.shape[1]
    half_rows, piece, pair_cols = rows // 2, cols // 8, 2 * HD
    gx, gy = lax.axis_index("gx"), lax.axis_index("gy")
    x_at, z_low, z_high = gx & 1, (gx >> 1) & 1, gx >> 2
    rank = (x_at * 4 + z_low * 2 + z_high).astype(jnp.int32)
    z_at = z_low * 2 + z_high
    own = gy.astype(jnp.int32)[None]
    order = jnp.arange(4, dtype=jnp.int32)

    widened = hidden_in.astype(f32)
    squares = jnp.sum(widened * widened, axis=1)
    squares = lax.dynamic_update_slice_in_dim(jnp.zeros((tokens,), f32), squares, gy * rows, 0)
    squares = squares.reshape(tokens // HD, HD)
    squares = squares_x = squares + swap(squares, "gx", 1)
    for axis, bit in (("gy", 1), ("gx", 2), ("gx", 4)):
        squares = squares + swap(squares, axis, bit)

    parts = {}
    for h in range(2):
        parts[0, h] = hidden_in[h * half_rows : (h + 1) * half_rows]
        parts[1, h] = swap(parts[0, h], "gy", 1)

    for h in range(2):
        parts[2, h] = swap(parts[0, h], "gy", 2)
        parts[3, h] = swap(parts[2, h], "gy", 1)


    x_served = []

    def swap_x(value):
        if x_served:
            value = after(value, x_served[-1])
        x_served.append(swap(value, "gx", 1))
        return x_served[-1]

    def pieces(first):
        return [parts[first + i, h] for h in range(2) for i in range(2)]

    place = jnp.concatenate([gy ^ order, x_at[None]]).astype(jnp.int32)
    given, kept_pair = pairs(place, norm_gain, hidden_in, w_key, w_value)
    near_place = after(rank ^ (order + 4), given)
    crossed_in, keeps = {}, {}
    outs = project(near_place, norm_gain, pieces(0), w_query, piece, 2)
    (keeps[0],) = project(after(rank ^ order, outs[0]), norm_gain, pieces(0), w_query, piece, 1)
    given = swap_x(after(given, squares_x))
    crossed_in[0, 0], crossed_in[0, 1] = swap_x(outs[0]), swap_x(outs[1])
    pair = given.astype(f32) + after(kept_pair, keeps[0]).astype(f32)
    pair = pair.astype(bf16)
    given = columns(pair, (1 - z_low) * 2 * pair_cols, 2 * pair_cols)
    pair = columns(pair, z_low * 2 * pair_cols, 2 * pair_cols).astype(f32)
    pair = (pair + swap(given, "gx", 2).astype(f32)).astype(bf16)
    outs = project(after(rank ^ (order + 4), pair), norm_gain, pieces(2), w_query, piece, 2)
    (keeps[2],) = project(after(rank ^ order, outs[0]), norm_gain, pieces(2), w_query, piece, 1)
    crossed_in[2, 0], crossed_in[2, 1] = swap_x(outs[0]), swap_x(outs[1])
    given = columns(pair, (1 - z_high) * pair_cols, pair_cols)
    pair = columns(pair, z_high * pair_cols, pair_cols).astype(f32)
    pair = (pair + swap(given, "gx", 4).astype(f32)).astype(bf16)
    across = []
    for i in range(8):
        for j in range(4):
            across.append((i * 4 + j, i * 4 + (j ^ ((i >> 1) & 1) * 2 ^ (i >> 2))))
    squares = after(squares, pair)
    pair = lax.ppermute(pair, ("gx", "gy"), across)
    squares = squares + swap(squares, "gy", 2)
    pair = jnp.concatenate([pair, swap(pair, "gx", 4)], axis=0)
    pair = jnp.concatenate([pair, swap(pair, "gx", 2)], axis=0)

    scale = lax.rsqrt(squares.reshape(tokens) / model_width + EPS)[:, None]
    _, position = segment_table(seg_lengths, tokens)
    lane = jnp.arange(HD, dtype=jnp.int32)
    exponent = (lane % (HD // 2)).astype(f32) * (2.0 / HD)
    angle = position.astype(f32)[:, None] * (ROPE_BASE ** (-exponent))[None, :]
    cosine = jnp.cos(angle) * scale
    sine = jnp.where(lane < HD // 2, -1.0, 1.0)[None, :] * jnp.sin(angle) * scale
    key, value = prepare(own ^ z_at, pair, cosine, sine, jnp.broadcast_to(scale, (tokens, HD)))

    def halve_far(near, got):
        high = near[:, piece:] + got[:, piece:].astype(f32)
        near = near[:, :piece] + got[:, :piece].astype(f32)
        got = swap(high.astype(bf16), "gx", 4)
        return (near + got.astype(f32)).astype(bf16), got

    attended, last = {}, None
    for first, h in ((0, 0), (0, 1), (2, 0), (2, 1)):
        cross = crossed_in[first, h]
        keep = keeps[first][h * rows : (h + 1) * rows]
        low = (keep[:, 2 * piece :].astype(f32) + cross[:, 2 * piece :].astype(f32)).astype(bf16)
        if last is not None:
            marks = [attended[0, 0]] if (first, h) == (2, 0) else [keeps[2]]
            low = after(low, last, *marks)
        last = got = swap(low, "gx", 2)
        if (first, h) == (2, 1):
            query = after(query, got)
            attended[2, 0] = attend(2, 0, own, seg_lengths, query, key, value, cosine, sine)
        near = keep[:, : 2 * piece].astype(f32) + cross[:, : 2 * piece].astype(f32)
        if (first, h) == (0, 1):
            waiting = near, got
            continue
        query, got = halve_far(near, got)
        if (first, h) != (2, 0):
            attended[first, h] = attend(first, h, own, seg_lengths, query, key, value, cosine, sine)
    near, halved = waiting
    query, _ = halve_far(near, after(halved, got))
    attended[0, 1] = attend(0, 1, own, seg_lengths, query, key, value, cosine, sine)

    w_rows = reorder(after(rank ^ jnp.arange(8, dtype=jnp.int32), crossed_in[2, 0]), w_out)
    kept, crossed = {}, {}
    done = None
    for first, h in ((0, 0), (2, 0), (2, 1), (0, 1)):
        a = attended[first, h]
        got = swap(a, "gx", 4)
        if (first, h) == (0, 0):
            got = after(got, w_rows)
        a = jnp.concatenate([a, got], axis=1)
        a = jnp.concatenate([a, swap(a, "gx", 2)], axis=1)
        got = swap_x(a)
        if done is not None:
            got = after(got, done)
        a = jnp.concatenate([a, got], axis=1)
        given = jnp.dot(a[half_rows:], w_rows, preferred_element_type=f32).astype(bf16)
        a = a[:half_rows]
        if (first, h) == (2, 1):
            a = after(a, crossed[0])
        mine = jnp.dot(a, w_rows, preferred_element_type=f32)
        mine = mine + swap(given, "gy", 1).astype(f32)
        if first:
            done = mine.astype(bf16)
            crossed[h] = swap(done, "gy", 2)
        else:
            kept[h] = mine
    return jnp.concatenate(
        [(kept[h] + crossed[h].astype(f32)).astype(bf16) for h in range(2)], axis=0
    )


def shards(hidden_in, norm_gain, w_query, w_key, w_value, w_out, seg_lengths):
    split = (lax.axis_size("gx"), lax.axis_size("gy"))
    body = shards_8x4 if split == (8, 4) else shards_any
    return body(hidden_in, norm_gain, w_query, w_key, w_value, w_out, seg_lengths)


def solution(mesh):
    in_specs = (
        P("gy", "gx"),
        P("gx"),
        P("gx", "gy"),
        P("gx", None),
        P("gx", None),
        P("gy", "gx"),
        P(),
    )
    out_specs = P("gy", "gx")
    return jax.shard_map(shards, mesh=mesh, in_specs=in_specs, out_specs=out_specs, check_vma=False)
```

```python
import functools
import math

import jax
import jax.numpy as jnp
from jax import lax
from jax.experimental import pallas as pl
from jax.experimental.pallas import tpu as pltpu
from jax.sharding import PartitionSpec as P

H = 64
KVH = 8
HD = 128


ROPE_BASE = 500000.0
EPS = 1e-05
SEG_MOST = 512


def rotate(values, position, head_size):
    half = head_size // 2
    exponent = jnp.arange(half, dtype=jnp.float32) * (2.0 / head_size)
    frequency = ROPE_BASE ** (-exponent)
    angle = position[:, None, None] * frequency[None, None, :]
    cosine = jnp.cos(angle)
    sine = jnp.sin(angle)
    first = values[..., :half]
    second = values[..., half:]
    return jnp.concatenate(
        [first * cosine - second * sine, second * cosine + first * sine], axis=-1
    )


def segment_table(seg_lengths, tokens):
    ends = jnp.cumsum(seg_lengths)
    starts = ends - seg_lengths
    index = jnp.arange(tokens, dtype=jnp.int32)
    member = ((index[:, None] >= starts[None, :]) & (index[:, None] < ends[None, :])).astype(
        jnp.int32
    )
    seg_id = jnp.sum(member * jnp.arange(seg_lengths.shape[0], dtype=jnp.int32)[None, :], axis=1)
    first_index = jnp.sum(member * starts[None, :], axis=1)
    return (seg_id, index - first_index)


def normalize(block, gain, squares, model_width):
    widened = block.astype(jnp.float32)
    scale = lax.rsqrt(squares / model_width + EPS)
    return (widened * scale[:, None] * gain[None, :]).astype(jnp.bfloat16)


def shards_any(hidden_in, norm_gain, w_query, w_key, w_value, w_out, seg_lengths):
    rows_own, width = hidden_in.shape
    model_width = width * lax.axis_size("gx")
    tokens = rows_own * lax.axis_size("gy")
    query_rows = tokens // lax.axis_size("gx")
    widened = hidden_in.astype(jnp.float32)
    squares = lax.psum(jnp.sum(widened * widened, axis=1), "gx")
    source = normalize(hidden_in, norm_gain, squares, model_width)
    gathered = lax.all_gather(source, "gy", axis=0, tiled=True)
    query_cols = w_query.shape[1]
    heads_local = query_cols // HD
    group = H // KVH
    kv_local = max(1, heads_local // group)
    pair_cols = kv_local * HD
    first_head = lax.axis_index("gy") * heads_local // group
    key_own = lax.dynamic_slice_in_dim(w_key, first_head * HD, pair_cols, 1)
    value_own = lax.dynamic_slice_in_dim(w_value, first_head * HD, pair_cols, 1)
    seg_id, position = segment_table(seg_lengths, tokens)
    here = lax.axis_index("gx") * query_rows
    query_seg = lax.dynamic_slice_in_dim(seg_id, here, query_rows)
    query_pos = lax.dynamic_slice_in_dim(position, here, query_rows)
    query_index = here + jnp.arange(query_rows, dtype=jnp.int32)
    query_sum = lax.psum_scatter(
        jnp.dot(gathered, w_query, preferred_element_type=jnp.float32).astype(jnp.bfloat16),
        "gx",
        scatter_dimension=0,
        tiled=True,
    ).astype(jnp.float32)
    pair_part = jnp.concatenate(
        [
            jnp.dot(gathered, key_own, preferred_element_type=jnp.float32),
            jnp.dot(gathered, value_own, preferred_element_type=jnp.float32),
        ],
        axis=1,
    )
    pair_sum = lax.psum(pair_part.astype(jnp.bfloat16), "gx").astype(jnp.float32)
    key_raw = pair_sum[:, :pair_cols].astype(jnp.bfloat16)
    value_raw = pair_sum[:, pair_cols:].astype(jnp.bfloat16)
    group_local = heads_local // kv_local
    queries = rotate(
        query_sum.reshape(query_rows, heads_local, HD), query_pos.astype(jnp.float32), HD
    ).astype(jnp.bfloat16)
    queries = queries.reshape(query_rows, kv_local, group_local, HD)
    key_count = key_raw.shape[0]
    keys = rotate(
        key_raw.astype(jnp.float32).reshape(key_count, kv_local, HD),
        position.astype(jnp.float32),
        HD,
    )
    keys = keys.astype(jnp.bfloat16).reshape(key_count, pair_cols)
    score_scale = 1.0 / math.sqrt(HD)
    running = jnp.full((kv_local, group_local, query_rows), -1e30, jnp.float32)
    count = keys.shape[0]
    key_index = jnp.arange(count, dtype=jnp.int32)
    allowed = (query_seg[:, None] == seg_id[None, :]) & (key_index[None, :] <= query_index[:, None])
    key_heads = keys.reshape(count, kv_local, HD)
    value_heads = value_raw.reshape(count, kv_local, HD)
    scores = (
        jnp.einsum("rkgd,nkd->kgrn", queries, key_heads, preferred_element_type=jnp.float32)
        * score_scale
    )
    scores = jnp.where(allowed[None, None], scores, -1e30)
    newest = jnp.maximum(running, jnp.max(scores, axis=-1))
    weights = jnp.where(allowed[None, None], jnp.exp(scores - newest[..., None]), 0.0)
    denominator = jnp.sum(weights, axis=-1)
    added = jnp.einsum(
        "kgrn,nkd->rkgd",
        weights.astype(jnp.bfloat16),
        value_heads,
        preferred_element_type=jnp.float32,
    )
    accum = added
    running, denominator, accum = (newest, denominator, accum)
    attended = (
        (accum / denominator.transpose(2, 0, 1)[..., None])
        .reshape(query_rows, query_cols)
        .astype(jnp.bfloat16)
    )
    partial_out = jnp.dot(
        lax.all_gather(attended, "gx", axis=0, tiled=True),
        w_out,
        preferred_element_type=jnp.float32,
    )
    return lax.psum_scatter(partial_out.astype(jnp.bfloat16), "gy", scatter_dimension=0, tiled=True)


SCOPE = 32 * 2**20
SMALL = pl.CostEstimate(flops=0, bytes_accessed=0, transcendentals=0)


def swap(value, axis, bit):
    return lax.ppermute(value, axis, [(i, i ^ bit) for i in range(lax.axis_size(axis))])


def columns(array, start, size):
    return lax.dynamic_slice_in_dim(array, start, size, 1)


def after(value, *others):
    hbm = pl.BlockSpec(memory_space=pl.ANY)
    return pl.pallas_call(
        lambda *refs: None,
        out_shape=jax.ShapeDtypeStruct(value.shape, value.dtype),
        in_specs=[hbm] * (1 + len(others)),
        out_specs=hbm,
        input_output_aliases={0: 0},
        cost_estimate=SMALL,
    )(value, *others)


def prepare_kernel(own_ref, pair_ref, cos_ref, sin_ref, scale_ref, key_ref, value_ref):
    blocks = 4
    rows = pair_ref.shape[0] // blocks
    own = own_ref[0]
    key_ref[:SEG_MOST, :] = jnp.zeros((SEG_MOST, HD), jnp.bfloat16)
    value_ref[:SEG_MOST, :] = jnp.zeros((SEG_MOST, HD), jnp.bfloat16)
    for block in range(blocks):
        start = pl.multiple_of((block ^ own) * rows, rows)
        here = pl.ds(block * rows, rows)
        there = pl.ds(SEG_MOST + block * rows, rows)
        key = pair_ref[pl.ds(start, rows), :HD].astype(jnp.float32)
        value = pair_ref[pl.ds(start, rows), HD:].astype(jnp.float32)
        key = key * cos_ref[here, :] + pltpu.roll(key, HD // 2, 1) * sin_ref[here, :]
        key_ref[there, :] = key.astype(jnp.bfloat16)
        value_ref[there, :] = (value * scale_ref[here, :]).astype(jnp.bfloat16)


def prepare(own, pair, cosine, sine, scale):
    tokens = pair.shape[0]
    padded = jax.ShapeDtypeStruct((SEG_MOST + tokens, HD), jnp.bfloat16)
    vmem = pl.BlockSpec(memory_space=pltpu.VMEM)
    return pl.pallas_call(
        prepare_kernel,
        out_shape=[padded, padded],
        in_specs=[pl.BlockSpec(memory_space=pltpu.SMEM)] + [vmem] * 4,
        out_specs=[vmem, vmem],
        compiler_params=pltpu.CompilerParams(vmem_limit_bytes=SCOPE),
        cost_estimate=SMALL,
    )(own, pair, cosine, sine, scale)


def attend_kernel(first, half, own_ref, len_ref, query_ref, key_ref, value_ref, cos_ref, sin_ref, out_ref):
    rows = query_ref.shape[0] // 2
    block_rows = cos_ref.shape[0] // 4
    window = SEG_MOST + rows
    own = own_ref[0]
    for piece in range(2):
        start = pl.multiple_of((own ^ (first + piece)) * block_rows + half * rows, rows)
        here = pl.ds(start, rows)
        key = key_ref[pl.ds(start, window), :]
        value = value_ref[pl.ds(start, window), :]
        query_at = start + lax.broadcasted_iota(jnp.int32, (rows, 1), 0)
        key_at = start - SEG_MOST + lax.broadcasted_iota(jnp.int32, (rows, window), 1)
        begin = jnp.zeros((rows, 1), jnp.int32)
        total = len_ref[0]
        for i in range(1, len_ref.shape[0]):
            begin = jnp.where(query_at >= total, total, begin)
            total = total + len_ref[i]
        allowed = (key_at >= begin) & (key_at <= query_at)
        for head in range(2):
            at = pl.ds(head * HD, HD)
            query = query_ref[pl.ds(piece * rows, rows), at].astype(jnp.float32)
            query = query * cos_ref[here, :] + pltpu.roll(query, HD // 2, 1) * sin_ref[here, :]
            scores = lax.dot_general(
                query.astype(jnp.bfloat16),
                key,
                (((1,), (1,)), ((), ())),
                preferred_element_type=jnp.float32,
            )
            scores = jnp.where(allowed, scores * (1.0 / math.sqrt(HD)), -1e30)
            weights = jnp.exp(scores - jnp.max(scores, axis=1, keepdims=True))
            weights = jnp.where(allowed, weights, 0.0)
            denominator = jnp.sum(weights, axis=1, keepdims=True)
            added = jnp.dot(weights.astype(jnp.bfloat16), value, preferred_element_type=jnp.float32)
            out_ref[pl.ds(piece * rows, rows), at] = (added / denominator).astype(jnp.bfloat16)


def attend(first, half, own, seg_lengths, query, key, value, cosine, sine):
    rows = query.shape[0]
    vmem = pl.BlockSpec(memory_space=pltpu.VMEM)
    smem = pl.BlockSpec(memory_space=pltpu.SMEM)
    return pl.pallas_call(
        functools.partial(attend_kernel, first, half),
        out_shape=jax.ShapeDtypeStruct(query.shape, jnp.bfloat16),
        in_specs=[smem, smem] + [vmem] * 5,
        out_specs=vmem,
        compiler_params=pltpu.CompilerParams(vmem_limit_bytes=SCOPE),
        cost_estimate=pl.CostEstimate(
            flops=2**31, bytes_accessed=2**20, transcendentals=0
        ),
    )(own, seg_lengths, query, key, value, cosine, sine)


def copy_kernel(place_ref, weight_ref, out_ref):
    del place_ref
    out_ref[...] = weight_ref[...]


def reorder(place, weight):
    blocks = place.shape[0]
    shape = (weight.shape[0] // blocks, weight.shape[1])
    return pl.pallas_call(
        copy_kernel,
        out_shape=jax.ShapeDtypeStruct(weight.shape, jnp.bfloat16),
        grid_spec=pltpu.PrefetchScalarGridSpec(
            num_scalar_prefetch=1,
            grid=(blocks,),
            in_specs=[pl.BlockSpec(shape, lambda j, place: (place[j], 0))],
            out_specs=pl.BlockSpec(shape, lambda j, place: (j, 0)),
        ),
        compiler_params=pltpu.CompilerParams(vmem_limit_bytes=SCOPE),
        cost_estimate=pl.CostEstimate(
            flops=0, bytes_accessed=4 * weight.size, transcendentals=0
        ),
    )(place, weight)


def scale_rows(gain_ref, source_refs, scaled):
    @pl.when(pl.program_id(0) == 0)
    def _():
        at = 0
        for ref in source_refs:
            widened = ref[...].astype(jnp.float32) * gain_ref[...]
            scaled[pl.ds(at, ref.shape[0]), :] = widened.astype(jnp.bfloat16)
            at += ref.shape[0]


def pairs_kernel(place_ref, gain_ref, source_ref, key_ref, value_ref, given_ref, kept_ref, scaled):
    scale_rows(gain_ref, [source_ref], scaled)
    second = place_ref[place_ref.shape[0] - 1] == 1
    for i, ref in enumerate((key_ref, value_ref)):
        product = jnp.dot(scaled[...], ref[...], preferred_element_type=jnp.float32)
        product = product.astype(jnp.bfloat16)
        low, high = product[:, :HD], product[:, HD:]
        kept_ref[:, pl.ds(i * HD, HD)] = jnp.where(second, high, low)
        given_ref[:, pl.ds(i * HD, HD)] = jnp.where(second, low, high)


def pairs(place, gain, source, w_key, w_value):
    rows, depth = source.shape
    out = jax.ShapeDtypeStruct((rows, 8 * HD), jnp.bfloat16)
    picked = pl.BlockSpec((depth, 2 * HD), lambda j, place: (0, place[j]))
    made = pl.BlockSpec((rows, 2 * HD), lambda j, place: (0, j))
    return pl.pallas_call(
        pairs_kernel,
        out_shape=[out, out],
        grid_spec=pltpu.PrefetchScalarGridSpec(
            num_scalar_prefetch=1,
            grid=(4,),
            in_specs=[
                pl.BlockSpec((1, depth), lambda j, place: (0, 0)),
                pl.BlockSpec((rows, depth), lambda j, place: (0, 0)),
                picked,
                picked,
            ],
            out_specs=[made, made],
            scratch_shapes=[pltpu.VMEM((rows, depth), jnp.bfloat16)],
        ),
        compiler_params=pltpu.CompilerParams(vmem_limit_bytes=SCOPE),
        cost_estimate=pl.CostEstimate(
            flops=4 * rows * depth * 8 * HD, bytes_accessed=4 * depth * 8 * HD, transcendentals=0
        ),
    )(place, gain[None, :], source, w_key, w_value)


def project_kernel(pieces, place_ref, gain_ref, *refs):
    weight_ref, out_refs, scaled = refs[pieces], refs[pieces + 1 : -1], refs[-1]
    scale_rows(gain_ref, refs[:pieces], scaled)
    product = jnp.dot(scaled[...], weight_ref[...], preferred_element_type=jnp.float32)
    rows = product.shape[0] // len(out_refs)
    for i, ref in enumerate(out_refs):
        ref[...] = product[i * rows : (i + 1) * rows, :].astype(jnp.bfloat16)


def project(place, gain, pieces, weight, size, outs):
    piece_rows, depth = pieces[0].shape
    rows, width = len(pieces) * piece_rows, size * place.shape[0]
    out = jax.ShapeDtypeStruct((rows // outs, width), jnp.bfloat16)
    return pl.pallas_call(
        functools.partial(project_kernel, len(pieces)),
        out_shape=[out] * outs,
        grid_spec=pltpu.PrefetchScalarGridSpec(
            num_scalar_prefetch=1,
            grid=(place.shape[0],),
            in_specs=[pl.BlockSpec((1, depth), lambda j, place: (0, 0))]
            + [pl.BlockSpec((piece_rows, depth), lambda j, place: (0, 0))] * len(pieces)
            + [pl.BlockSpec((depth, size), lambda j, place: (0, place[j]))],
            out_specs=[pl.BlockSpec((rows // outs, size), lambda j, place: (0, j))] * outs,
            scratch_shapes=[pltpu.VMEM((rows, depth), jnp.bfloat16)],
        ),
        compiler_params=pltpu.CompilerParams(vmem_limit_bytes=SCOPE),
        cost_estimate=pl.CostEstimate(
            flops=2 * rows * depth * width,
            bytes_accessed=2 * (rows * depth + (depth + rows) * width),
            transcendentals=0,
        ),
    )(place, gain[None, :], *pieces, weight)


def shards_8x4(hidden_in, norm_gain, w_query, w_key, w_value, w_out, seg_lengths):
    f32, bf16 = jnp.float32, jnp.bfloat16
    rows, width = hidden_in.shape
    model_width = width * lax.axis_size("gx")
    tokens = rows * lax.axis_size("gy")
    cols = w_query.shape[1]
    half_rows, piece, pair_cols = rows // 2, cols // 8, 2 * HD
    gx, gy = lax.axis_index("gx"), lax.axis_index("gy")
    x_at, z_low, z_high = gx & 1, (gx >> 1) & 1, gx >> 2
    rank = (x_at * 4 + z_low * 2 + z_high).astype(jnp.int32)
    z_at = z_low * 2 + z_high
    own = gy.astype(jnp.int32)[None]
    order = jnp.arange(4, dtype=jnp.int32)

    widened = hidden_in.astype(f32)
    squares = jnp.sum(widened * widened, axis=1)
    squares = lax.dynamic_update_slice_in_dim(jnp.zeros((tokens,), f32), squares, gy * rows, 0)
    squares = squares.reshape(tokens // HD, HD)
    squares = squares_x = squares + swap(squares, "gx", 1)
    for axis, bit in (("gy", 1), ("gx", 2), ("gx", 4)):
        squares = squares + swap(squares, axis, bit)

    parts = {}
    for h in range(2):
        parts[0, h] = hidden_in[h * half_rows : (h + 1) * half_rows]
        parts[1, h] = swap(parts[0, h], "gy", 1)

    for h in range(2):
        parts[2, h] = swap(parts[0, h], "gy", 2)
        parts[3, h] = swap(parts[2, h], "gy", 1)


    x_served = []

    def swap_x(value, *others):
        if x_served:
            value = after(value, x_served[-1], *others)
        x_served.append(swap(value, "gx", 1))
        return x_served[-1]

    def pieces(first):
        return [parts[first + i, h] for h in range(2) for i in range(2)]

    place = jnp.concatenate([gy ^ order, x_at[None]]).astype(jnp.int32)
    given, kept_pair = pairs(place, norm_gain, hidden_in, w_key, w_value)
    near_place = after(rank ^ (order + 4), given)
    crossed_in, keeps = {}, {}
    outs = project(near_place, norm_gain, pieces(0), w_query, piece, 2)
    (keeps[0],) = project(after(rank ^ order, outs[0]), norm_gain, pieces(0), w_query, piece, 1)
    given = swap_x(after(given, squares_x))
    crossed_in[0, 0], crossed_in[0, 1] = swap_x(outs[0]), swap_x(outs[1])
    pair = given.astype(f32) + after(kept_pair, keeps[0]).astype(f32)
    pair = pair.astype(bf16)
    given = columns(pair, (1 - z_low) * 2 * pair_cols, 2 * pair_cols)
    pair = columns(pair, z_low * 2 * pair_cols, 2 * pair_cols).astype(f32)
    pair = (pair + swap(given, "gx", 2).astype(f32)).astype(bf16)
    outs = project(after(rank ^ (order + 4), pair), norm_gain, pieces(2), w_query, piece, 2)
    (keeps[2],) = project(after(rank ^ order, outs[0]), norm_gain, pieces(2), w_query, piece, 1)
    crossed_in[2, 0], crossed_in[2, 1] = swap_x(outs[0]), swap_x(outs[1])
    given = columns(pair, (1 - z_high) * pair_cols, pair_cols)
    pair = columns(pair, z_high * pair_cols, pair_cols).astype(f32)
    pair = (pair + swap(given, "gx", 4).astype(f32)).astype(bf16)
    across = []
    for i in range(8):
        for j in range(4):
            across.append((i * 4 + j, i * 4 + (j ^ ((i >> 1) & 1) * 2 ^ (i >> 2))))
    squares = after(squares, pair)
    pair = lax.ppermute(pair, ("gx", "gy"), across)
    squares = squares + swap(squares, "gy", 2)
    pair = jnp.concatenate([pair, swap(pair, "gx", 4)], axis=0)
    pair = jnp.concatenate([pair, swap(pair, "gx", 2)], axis=0)

    scale = lax.rsqrt(squares.reshape(tokens) / model_width + EPS)[:, None]
    _, position = segment_table(seg_lengths, tokens)
    lane = jnp.arange(HD, dtype=jnp.int32)
    exponent = (lane % (HD // 2)).astype(f32) * (2.0 / HD)
    angle = position.astype(f32)[:, None] * (ROPE_BASE ** (-exponent))[None, :]
    cosine = jnp.cos(angle) * scale
    sine = jnp.where(lane < HD // 2, -1.0, 1.0)[None, :] * jnp.sin(angle) * scale
    key, value = prepare(own ^ z_at, pair, cosine, sine, jnp.broadcast_to(scale, (tokens, HD)))

    def halve_far(near, got):
        high = near[:, piece:] + got[:, piece:].astype(f32)
        near = near[:, :piece] + got[:, :piece].astype(f32)
        got = swap(high.astype(bf16), "gx", 4)
        return (near + got.astype(f32)).astype(bf16), got

    attended, last = {}, None
    for first, h in ((0, 0), (0, 1), (2, 0), (2, 1)):
        cross = crossed_in[first, h]
        keep = keeps[first][h * rows : (h + 1) * rows]
        low = (keep[:, 2 * piece :].astype(f32) + cross[:, 2 * piece :].astype(f32)).astype(bf16)
        if last is not None:
            marks = [attended[0, 0]] if (first, h) == (2, 0) else [keeps[2]]
            low = after(low, last, *marks)
        last = got = swap(low, "gx", 2)
        if (first, h) == (2, 1):
            query = after(query, got)
            attended[2, 0] = attend(2, 0, own, seg_lengths, query, key, value, cosine, sine)
        near = keep[:, : 2 * piece].astype(f32) + cross[:, : 2 * piece].astype(f32)
        if (first, h) == (0, 1):
            waiting = near, got
            continue
        query, got = halve_far(near, got)
        if (first, h) != (2, 0):
            attended[first, h] = attend(first, h, own, seg_lengths, query, key, value, cosine, sine)
    gathered = swap(attended[2, 1], "gx", 4)
    wide = jnp.concatenate([attended[2, 1], gathered], axis=1)
    nearest = swap(wide, "gx", 2)
    ahead = {(0, 0): [got], (2, 0): [attended[2, 1]]}
    near, halved = waiting
    query, _ = halve_far(near, after(halved, gathered))
    query = after(query, nearest)
    attended[0, 1] = attend(0, 1, own, seg_lengths, query, key, value, cosine, sine)

    w_rows = reorder(after(rank ^ jnp.arange(8, dtype=jnp.int32), crossed_in[2, 0]), w_out)
    kept, crossed = {}, {}
    done = None
    for first, h in ((0, 0), (2, 0), (2, 1), (0, 1)):
        a = attended[first, h]
        if (first, h) == (2, 1):
            a = jnp.concatenate([wide, nearest], axis=1)
        else:
            got = swap(a, "gx", 4)
            if (first, h) == (0, 0):
                got = after(got, w_rows)
            a = jnp.concatenate([a, got], axis=1)
            a = jnp.concatenate([a, swap(a, "gx", 2)], axis=1)
        got = swap_x(a, *ahead.get((first, h), []))
        if done is not None:
            got = after(got, done)
        a = jnp.concatenate([a, got], axis=1)
        given = jnp.dot(a[half_rows:], w_rows, preferred_element_type=f32).astype(bf16)
        a = a[:half_rows]
        if (first, h) == (2, 1):
            a = after(a, crossed[0])
        mine = jnp.dot(a, w_rows, preferred_element_type=f32)
        mine = mine + swap(given, "gy", 1).astype(f32)
        if first:
            done = mine.astype(bf16)
            crossed[h] = swap(done, "gy", 2)
        else:
            kept[h] = mine
    return jnp.concatenate(
        [(kept[h] + crossed[h].astype(f32)).astype(bf16) for h in range(2)], axis=0
    )


def shards(hidden_in, norm_gain, w_query, w_key, w_value, w_out, seg_lengths):
    split = (lax.axis_size("gx"), lax.axis_size("gy"))
    body = shards_8x4 if split == (8, 4) else shards_any
    return body(hidden_in, norm_gain, w_query, w_key, w_value, w_out, seg_lengths)


def solution(mesh):
    in_specs = (
        P("gy", "gx"),
        P("gx"),
        P("gx", "gy"),
        P("gx", None),
        P("gx", None),
        P("gy", "gx"),
        P(),
    )
    out_specs = P("gy", "gx")
    return jax.shard_map(shards, mesh=mesh, in_specs=in_specs, out_specs=out_specs, check_vma=False)
```
